32 devices in a mesh: dp: 16 (over z, y, core), stream: 2 (over x).
Axes of the slice: x: 2, y: 2, z: 4, core: 2. Of those that a mesh axis runs over, the one named last changes fastest.
Arguments:
- main_rows: bfloat16 [10240, 1024], P(('dp', 'stream')), may hold values from -6 to 6
- pred_rows: bfloat16 [20480, 1024], P(('dp', 'stream')), may hold values from -6 to 6
- enc_rows: bfloat16 [10240, 1024], P(('dp', 'stream')), may hold values from -6 to 6
- doc_lengths: int32 [16, 8], P('dp'), may hold values from 1 to 512, as said below
- main_cotangent: bfloat16 [10240, 1024], P(('dp', 'stream')), may hold values from -6 to 6
- pred_cotangent: bfloat16 [20480, 1024], P(('dp', 'stream')), may hold values from -6 to 6
- proj_master: float32 [1024, 12800], P(None, ('dp', 'stream'))
- proj_first: float32 [1024, 12800], P(None, ('dp', 'stream')), may hold values from -56 to 56
- proj_second: float32 [1024, 12800], P(None, ('dp', 'stream')), may hold values from 7.68 to 30.72
- bias_master: float32 [10752], P(('dp', 'stream')), may hold values from -0.6 to 0.6
- bias_first: float32 [10752], P(('dp', 'stream')), may hold values from -56 to 56
- bias_second: float32 [10752], P(('dp', 'stream')), may hold values from 7.68 to 30.72
- down_master: float32 [4096, 1024], P(('dp', 'stream')), may hold values from -0.09375 to 0.09375
- down_first: float32 [4096, 1024], P(('dp', 'stream')), may hold values from -56 to 56
- down_second: float32 [4096, 1024], P(('dp', 'stream')), may hold values from 7.68 to 30.72
- small_master: float32 [7, 1024], replicated
- small_first: float32 [7, 1024], replicated, may hold values from -56 to 56
- small_second: float32 [7, 1024], replicated, may hold values from 7.68 to 30.72
Outputs:
- main_out: bfloat16 [10240, 1024], P(('dp', 'stream'))
- pred_out: bfloat16 [20480, 1024], P(('dp', 'stream'))
- main_grad: bfloat16 [10240, 1024], P(('dp', 'stream'))
- pred_grad: bfloat16 [20480, 1024], P(('dp', 'stream'))
- enc_grad: bfloat16 [10240, 1024], P(('dp', 'stream'))
- proj_new: float32 [1024, 12800], P(None, ('dp', 'stream'))
- proj_first_new: float32 [1024, 12800], P(None, ('dp', 'stream'))
- proj_second_new: float32 [1024, 12800], P(None, ('dp', 'stream'))
- bias_new: float32 [10752], P(('dp', 'stream'))
- bias_first_new: float32 [10752], P(('dp', 'stream'))
- bias_second_new: float32 [10752], P(('dp', 'stream'))
- down_new: float32 [4096, 1024], P(('dp', 'stream'))
- down_first_new: float32 [4096, 1024], P(('dp', 'stream'))
- down_second_new: float32 [4096, 1024], P(('dp', 'stream'))
- small_new: float32 [7, 1024], replicated
- small_first_new: float32 [7, 1024], replicated
- small_second_new: float32 [7, 1024], replicated
The draws below stay inside these ranges and needn't reach their ends.
Inputs may be any that keep to these rules, and one draw needn't show every extreme that they name: `doc_lengths`: each row's 8 lengths sum to 640; the second length of every row is 512.
All inputs are finite; a program needn't handle non-finite values.
Results may differ from the reference program's by a relative error of at most 0.023.
Values may be sent and summed in bfloat16 or wider, within the bound.
A program may use at most 384 MiB of HBM per device.

```python
import math
from functools import partial
import jax
import jax.numpy as jnp
from jax import lax

D = 1024
HEADS = 16
FF = 4096
BUCKETS = 32
LONGEST = 512
DOCS = 8
STEP = 10
HEAD_DIM = 64
GROUP = 640
PROJ_COLS = 12800
BIAS_LEN = 10752
N_DP = 16


def draw_doc_lengths(key, part):
    key = jax.random.fold_in(key, 7)
    first_key, share_key = jax.random.split(key)
    leading = jax.random.randint(first_key, (N_DP, 1), 1, LONGEST // 4 - DOCS + 3).astype(jnp.int32)
    remaining = LONGEST // 4 - leading
    piece_count = DOCS - 2
    shares = jax.random.randint(share_key, (N_DP, piece_count), 1, 9).astype(jnp.int32)
    share_total = jnp.sum(shares, axis=1, keepdims=True)
    pieces = 1 + (remaining - piece_count) * shares // share_total
    closing = remaining - jnp.sum(pieces[:, :-1], axis=1, keepdims=True)
    pieces = jnp.concatenate([pieces[:, :-1], closing], axis=1)
    longest_doc = jnp.full((N_DP, 1), LONGEST, jnp.int32)
    return jnp.concatenate([leading, longest_doc, pieces], axis=1).astype(jnp.int32)


def draw_proj_master(key, part):
    key = jax.random.fold_in(key, 11)
    normal_draw = jax.random.normal(key, (D, PROJ_COLS), jnp.float32) / math.sqrt(D)
    columns = jnp.arange(PROJ_COLS)
    rel_width = BUCKETS * HEADS
    boosted = (columns >= 2 * D) & (columns < 3 * D) | (columns >= 6 * D + rel_width) & (columns < 7 * D + rel_width)
    return normal_draw * jnp.where(boosted, 4.0, 1.0)


def draw_small_master(key, part):
    key = jax.random.fold_in(key, 5)
    normal_draw = jax.random.normal(key, (7, D), jnp.float32)
    row_index = jnp.arange(7)[:, None]
    is_gain = (row_index >= 1) & (row_index <= 3)
    return jnp.where(is_gain, 1.0 + 0.1 * normal_draw, 0.1 * normal_draw)


def block_levels(rng, dims, cuts, least, largest):
    gain = 1.0
    for axis_at, blocks in cuts:
        steps = jax.random.uniform(jax.random.fold_in(jax.random.fold_in(rng, 6), axis_at), (blocks,), jnp.float32, least / len(cuts), largest / len(cuts))
        gain = gain * jnp.repeat(jnp.exp(steps), dims[axis_at] // blocks).reshape((-1,) + (1,) * (len(dims) - 1 - axis_at))
    return gain


def gaussian(own_key, extent, deviation, most, cuts=(), kind=jnp.bfloat16):
    entries = deviation * jax.random.normal(own_key, extent, jnp.float32)
    if cuts:
        entries = entries * block_levels(own_key, extent, cuts, -0.22, 0.18)
    return jnp.clip(entries, -most, most).astype(kind)


def setup_inputs(seed: int = 0) -> dict:
    arg_keys = jax.random.split(jax.random.key(seed), 19)
    main_rows = gaussian(arg_keys[0], (N_DP * GROUP, D), 1.0, 6.0, ((0, 32),))
    pred_rows = gaussian(arg_keys[1], (2 * N_DP * GROUP, D), 1.0, 6.0, ((0, 32),))
    enc_rows = gaussian(arg_keys[2], (N_DP * GROUP, D), 1.0, 6.0, ((0, 32),))
    doc_lengths = draw_doc_lengths(jax.random.fold_in(arg_keys[18], 71), 0)
    main_cotangent = gaussian(arg_keys[4], (N_DP * GROUP, D), 1.0, 6.0, ((0, 32),))
    pred_cotangent = gaussian(arg_keys[5], (2 * N_DP * GROUP, D), 1.0, 6.0, ((0, 32),))
    proj_master = draw_proj_master(jax.random.fold_in(arg_keys[18], 71), 0)
    proj_first = gaussian(arg_keys[7], (D, PROJ_COLS), (0.055 * (3 * GROUP * N_DP) ** 0.5), 56.0, ((1, 32),), jnp.float32)
    proj_second = jnp.clip(jnp.exp(math.log(30.72) - 1.3862944 * jax.random.uniform(arg_keys[8], (D, PROJ_COLS), jnp.float32) ** block_levels(arg_keys[8], (D, PROJ_COLS), ((1, 32),), -0.2, 0.2)), 7.68, 30.72)
    bias_master = gaussian(arg_keys[9], (BIAS_LEN,), 0.1, 0.6, ((0, 32),), jnp.float32)
    bias_first = gaussian(arg_keys[10], (BIAS_LEN,), (0.055 * (3 * GROUP * N_DP) ** 0.5), 56.0, ((0, 32),), jnp.float32)
    bias_second = jnp.clip(jnp.exp(math.log(30.72) - 1.3862944 * jax.random.uniform(arg_keys[11], (BIAS_LEN,), jnp.float32) ** block_levels(arg_keys[11], (BIAS_LEN,), ((0, 32),), -0.2, 0.2)), 7.68, 30.72)
    down_master = gaussian(arg_keys[12], (FF, D), FF ** -0.5, 0.09375, ((0, 32),), jnp.float32)
    down_first = gaussian(arg_keys[13], (FF, D), (0.055 * (3 * GROUP * N_DP) ** 0.5), 56.0, ((0, 32),), jnp.float32)
    down_second = jnp.clip(jnp.exp(math.log(30.72) - 1.3862944 * jax.random.uniform(arg_keys[14], (FF, D), jnp.float32) ** block_levels(arg_keys[14], (FF, D), ((0, 32),), -0.2, 0.2)), 7.68, 30.72)
    small_master = draw_small_master(jax.random.fold_in(arg_keys[18], 71), 0)
    small_first = gaussian(arg_keys[16], (7, D), (0.055 * (3 * GROUP * N_DP) ** 0.5), 56.0, (), jnp.float32)
    small_second = jnp.clip(jnp.exp(jax.random.uniform(arg_keys[17], (7, D), jnp.float32, math.log(7.68), math.log(30.72))), 7.68, 30.72)
    return {"main_rows": main_rows, "pred_rows": pred_rows, "enc_rows": enc_rows, "doc_lengths": doc_lengths, "main_cotangent": main_cotangent, "pred_cotangent": pred_cotangent, "proj_master": proj_master, "proj_first": proj_first, "proj_second": proj_second, "bias_master": bias_master, "bias_first": bias_first, "bias_second": bias_second, "down_master": down_master, "down_first": down_first, "down_second": down_second, "small_master": small_master, "small_first": small_first, "small_second": small_second}


NORM_EPS = 1e-05
BETA_FIRST = 0.9
BETA_SECOND = 0.999
ADAM_EPS = 1e-08
RATE_MATRIX = 0.04
RATE_VECTOR = 0.15
RATE_SMALL = 0.5
WEIGHT_DECAY = 0.01
MASKED = -1e+30
HIGHEST = lax.Precision.HIGHEST

@jax.custom_vjp
def low(v):
    return lax.optimization_barrier(v.astype(jnp.bfloat16)).astype(jnp.float32)

@jax.custom_vjp
def low_back(v):
    return v

def low_keep(v):
    return (low(v), None)

def low_pass(kept, grad):
    return (grad,)

def back_keep(v):
    return (v, None)

def back_low(kept, grad):
    return (low(grad),)
low.defvjp(low_keep, low_pass)
low_back.defvjp(back_keep, back_low)

def bucket_edges():
    return [int(math.ceil(16.0 * 8.0 ** (step_index / 16.0))) for step_index in range(1, 16)]

def bucket_of(distance):
    counted = jnp.zeros_like(distance)
    for threshold in bucket_edges():
        counted = counted + (distance >= threshold).astype(jnp.int32)
    return jnp.where(distance < 16, distance, 16 + counted).astype(jnp.int32)

def doc_ids(lengths, length_total):
    doc_ends = jnp.cumsum(lengths).astype(jnp.int32)
    places = jnp.arange(length_total, dtype=jnp.int32)
    return lax.optimization_barrier(jnp.sum((places[:, None] >= doc_ends[None, :]).astype(jnp.int32), axis=1)).astype(jnp.int32)

def layer_norm(hidden, gain_row, shift_row):
    centre = hidden - lax.optimization_barrier(jnp.mean(hidden, axis=-1, keepdims=True))
    spread = lax.optimization_barrier(jnp.mean(centre * centre, axis=-1, keepdims=True))
    return centre * lax.rsqrt(spread + NORM_EPS) * gain_row + shift_row

def product(left_side, right_side):
    return jnp.dot(left_side, right_side, precision=HIGHEST)

def copy_of(master):
    return lax.optimization_barrier(master.astype(jnp.bfloat16)).astype(jnp.float32)

def proj_blocks(matrix):
    rel_width = BUCKETS * HEADS
    edges = [0, D, 2 * D, 3 * D, 4 * D, 4 * D + rel_width, 5 * D + rel_width, 6 * D + rel_width, 7 * D + rel_width, 8 * D + rel_width, 8 * D + rel_width + FF]
    return tuple((matrix[:, edges[block]:edges[block + 1]] for block in range(10)))

def bias_blocks(vector):
    rel_width = BUCKETS * HEADS
    edges = [0, D, 2 * D, 3 * D, 3 * D + rel_width, 4 * D + rel_width, 5 * D + rel_width, 6 * D + rel_width, 6 * D + rel_width + FF]
    return tuple((vector[edges[block]:edges[block + 1]] for block in range(8)))

def self_attention(queries, key_rows, value_rows, table, query_places, query_docs, key_docs, main_flag):
    query_count = queries.shape[0]
    score_scale = HEAD_DIM ** (-0.5)
    query_heads = queries.reshape(query_count, HEADS, HEAD_DIM)
    key_heads = key_rows[:GROUP].reshape(GROUP, HEADS, HEAD_DIM)
    value_heads = value_rows[:GROUP].reshape(GROUP, HEADS, HEAD_DIM)
    own_keys = key_rows.reshape(query_count, HEADS, HEAD_DIM)
    own_values = value_rows.reshape(query_count, HEADS, HEAD_DIM)
    raw_scores = jnp.einsum('qhd,khd->hqk', query_heads, key_heads, precision=HIGHEST) * score_scale
    key_places = jnp.arange(GROUP, dtype=jnp.int32)
    distance = query_places[:, None] - key_places[None, :]
    buckets = bucket_of(jnp.maximum(distance, 0))
    table_heads = jnp.transpose(table.reshape(query_count, BUCKETS, HEADS), (2, 0, 1))
    bias_terms = jnp.take_along_axis(table_heads, jnp.broadcast_to(buckets[None], raw_scores.shape), axis=2)
    scores = low_back(raw_scores + bias_terms)
    own_score = low_back(lax.optimization_barrier(jnp.sum(query_heads * own_keys, axis=2)).T * score_scale + table_heads[:, :, 0])
    allowed = (query_docs[:, None] == key_docs[None, :]) & ((distance > 0) | (distance == 0) & main_flag[:, None])
    scores = jnp.where(allowed[None], scores, MASKED)
    own_score = jnp.where(main_flag[None], MASKED, own_score)
    row_top = jnp.maximum(lax.optimization_barrier(jnp.max(scores, axis=2)), own_score)
    weights = jnp.exp(scores - row_top[:, :, None])
    own_weight = jnp.exp(own_score - row_top)
    row_total = lax.optimization_barrier(jnp.sum(weights, axis=2)) + own_weight
    probabilities = low(weights / row_total[:, :, None])
    own_prob = low(own_weight / row_total)
    context = jnp.einsum('hqk,khd->qhd', probabilities, value_heads, precision=HIGHEST)
    context = context + own_prob.T[:, :, None] * own_values
    return context.reshape(query_count, HEADS * HEAD_DIM)

def cross_attention(queries, key_rows, value_rows, query_docs, key_docs):
    query_count = queries.shape[0]
    key_count = key_rows.shape[0]
    score_scale = HEAD_DIM ** (-0.5)
    query_heads = queries.reshape(query_count, HEADS, HEAD_DIM)
    key_heads = key_rows.reshape(key_count, HEADS, HEAD_DIM)
    value_heads = value_rows.reshape(key_count, HEADS, HEAD_DIM)
    scores = low_back(jnp.einsum('qhd,khd->hqk', query_heads, key_heads, precision=HIGHEST) * score_scale)
    same_doc = query_docs[:, None] == key_docs[None, :]
    scores = jnp.where(same_doc[None], scores, MASKED)
    row_top = lax.optimization_barrier(jnp.max(scores, axis=2))
    weights = jnp.exp(scores - row_top[:, :, None])
    row_total = lax.optimization_barrier(jnp.sum(weights, axis=2))
    probabilities = low(weights / row_total[:, :, None])
    context = jnp.einsum('hqk,khd->qhd', probabilities, value_heads, precision=HIGHEST)
    return context.reshape(query_count, HEADS * HEAD_DIM)

def group_forward(params, main_group, pred_group, enc_group, lengths):
    proj_weight, bias_weight, down_weight, small_weight = params
    query_weight, key_weight, value_weight, out_weight, table_weight, cross_weight, ckey_weight, cvalue_weight, back_weight, up_weight = proj_blocks(proj_weight)
    query_bias, value_bias, out_bias, table_bias, cross_bias, cvalue_bias, back_bias, up_bias = bias_blocks(bias_weight)
    places = jnp.arange(GROUP, dtype=jnp.int32)
    group_docs = doc_ids(lengths, GROUP)
    inputs = jnp.concatenate([main_group, pred_group[0], pred_group[1]], axis=0)
    query_places = jnp.concatenate([places, places, places])
    query_docs = jnp.concatenate([group_docs, group_docs, group_docs])
    main_flag = jnp.arange(3 * GROUP, dtype=jnp.int32) < GROUP
    queries = low(low_back(product(inputs, query_weight) + query_bias))
    key_rows = low(low_back(product(inputs, key_weight)))
    value_rows = low(low_back(product(inputs, value_weight) + value_bias))
    table = low_back(product(inputs, table_weight) + table_bias)
    context = low(low_back(self_attention(queries, key_rows, value_rows, table, query_places, query_docs, group_docs, main_flag)))
    attn_out = low_back(product(context, out_weight) + out_bias)
    hidden_one = layer_norm(inputs + attn_out, small_weight[1], small_weight[4])
    cross_queries = low(low_back(product(low(hidden_one), cross_weight) + cross_bias))
    cross_keys = low(low_back(product(enc_group, ckey_weight)))
    cross_values = low(low_back(product(enc_group, cvalue_weight) + cvalue_bias))
    cross_context = low(low_back(cross_attention(cross_queries, cross_keys, cross_values, query_docs, group_docs)))
    cross_out = low_back(product(cross_context, back_weight) + back_bias)
    hidden_two = layer_norm(hidden_one + cross_out, small_weight[2], small_weight[5])
    pre_act = low_back(product(low(hidden_two), up_weight) + up_bias)
    activated = low(jax.nn.gelu(pre_act, approximate=False))
    ffn_out = low_back(product(activated, down_weight) + small_weight[0])
    return layer_norm(hidden_two + ffn_out, small_weight[3], small_weight[6])

def forward(params, main_all, pred_all, enc_all, doc_lengths):
    main_groups = main_all.reshape(N_DP, GROUP, D)
    pred_groups = pred_all.reshape(N_DP, 2, GROUP, D)
    enc_groups = enc_all.reshape(N_DP, GROUP, D)
    step_fn = jax.checkpoint(partial(group_forward, params))

    def scan_step(carried, pieces):
        return (carried, step_fn(pieces[0], pieces[1], pieces[2], pieces[3]))
    unused, outputs = lax.scan(scan_step, jnp.zeros((), jnp.float32), (main_groups, pred_groups, enc_groups, doc_lengths))
    main_out = outputs[:, :GROUP].reshape(N_DP * GROUP, D)
    pred_out = outputs[:, GROUP:].reshape(N_DP * 2 * GROUP, D)
    return (main_out, pred_out)

def adam_step(master, first_moment, second_moment, gradient, step_rate, step_decay):
    first_new = BETA_FIRST * first_moment + (1.0 - BETA_FIRST) * gradient
    second_new = BETA_SECOND * second_moment + (1.0 - BETA_SECOND) * gradient * gradient
    first_hat = first_new / (1.0 - BETA_FIRST ** STEP)
    second_hat = second_new / (1.0 - BETA_SECOND ** STEP)
    master_new = master - step_rate * (first_hat / (jnp.sqrt(second_hat) + ADAM_EPS) + step_decay * master)
    return (master_new, first_new, second_new)

def reference(main_rows, pred_rows, enc_rows, doc_lengths, main_cotangent, pred_cotangent, proj_master, proj_first, proj_second, bias_master, bias_first, bias_second, down_master, down_first, down_second, small_master, small_first, small_second):
    params = (copy_of(proj_master), copy_of(bias_master), copy_of(down_master), small_master)
    outputs, pullback = jax.vjp(partial(forward, doc_lengths=doc_lengths), params, main_rows.astype(jnp.float32), pred_rows.astype(jnp.float32), enc_rows.astype(jnp.float32))
    grads = pullback((main_cotangent.astype(jnp.float32), pred_cotangent.astype(jnp.float32)))
    param_grads, main_back, pred_back, enc_back = grads
    proj_grad, bias_grad, down_grad, small_grad = param_grads
    proj_new, proj_first_new, proj_second_new = adam_step(proj_master, proj_first, proj_second, proj_grad, RATE_MATRIX, WEIGHT_DECAY)
    bias_new, bias_first_new, bias_second_new = adam_step(bias_master, bias_first, bias_second, bias_grad, RATE_VECTOR, 0.0)
    down_new, down_first_new, down_second_new = adam_step(down_master, down_first, down_second, down_grad, RATE_MATRIX, WEIGHT_DECAY)
    small_new, small_first_new, small_second_new = adam_step(small_master, small_first, small_second, small_grad, RATE_SMALL, 0.0)
    return (outputs[0].astype(jnp.bfloat16), outputs[1].astype(jnp.bfloat16), main_back.astype(jnp.bfloat16), pred_back.astype(jnp.bfloat16), enc_back.astype(jnp.bfloat16), proj_new, proj_first_new, proj_second_new, bias_new, bias_first_new, bias_second_new, down_new, down_first_new, down_second_new, small_new, small_first_new, small_second_new)
```

```python
from functools import partial
import math

import jax
import jax.numpy as jnp
from jax import lax
from jax.sharding import PartitionSpec as P

D = 1024
HEADS = 16
BUCKETS = 32
STEP = 10
HEAD_DIM = 64


NORM_EPS = 1e-05
BETA_FIRST = 0.9
BETA_SECOND = 0.999
ADAM_EPS = 1e-08
RATE_MATRIX = 0.04
RATE_VECTOR = 0.15
RATE_SMALL = 0.5
WEIGHT_DECAY = 0.01
MASKED = -1e30
HEAD_GROUP = 4


def bucket_edges():
    return [int(math.ceil(16.0 * 8.0 ** (step_index / 16.0))) for step_index in range(1, 16)]


def bucket_of(distance):
    counted = jnp.zeros_like(distance)
    for threshold in bucket_edges():
        counted = counted + (distance >= threshold).astype(jnp.int32)
    return jnp.where(distance < 16, distance, 16 + counted)


def doc_ids(lengths, length_total):
    doc_ends = jnp.cumsum(lengths)
    places = jnp.arange(length_total, dtype=jnp.int32)
    return jnp.sum((places[:, None] >= doc_ends[None, :]).astype(jnp.int32), axis=1)


def layer_norm(hidden, gain_row, shift_row):
    centre = hidden - jnp.mean(hidden, axis=-1, keepdims=True)
    spread = jnp.mean(centre * centre, axis=-1, keepdims=True)
    return centre * lax.rsqrt(spread + NORM_EPS) * gain_row + shift_row


def matmul(left_side, right_side):
    return jnp.dot(left_side, right_side, preferred_element_type=jnp.float32)


def outer_sum(left_side, right_side):
    return lax.dot_general(
        left_side, right_side, (((0,), (0,)), ((), ())), preferred_element_type=jnp.float32
    )


def times_transpose(left_side, right_side):
    return lax.dot_general(
        left_side, right_side, (((1,), (1,)), ((), ())), preferred_element_type=jnp.float32
    )


def split_heads(matrix):
    row_count = matrix.shape[0]
    return matrix.reshape(row_count, HEADS // HEAD_GROUP, HEAD_GROUP, HEAD_DIM).transpose(
        1, 2, 0, 3
    )


def join_heads(stacked):
    row_count = stacked.shape[2]
    return stacked.transpose(2, 0, 1, 3).reshape(row_count, HEADS * HEAD_DIM)


def split_table(table):
    row_count = table.shape[0]
    return table.reshape(row_count, BUCKETS, HEADS // HEAD_GROUP, HEAD_GROUP).transpose(2, 3, 0, 1)


def join_table(stacked):
    row_count = stacked.shape[2]
    return stacked.transpose(2, 3, 0, 1).reshape(row_count, BUCKETS * HEADS)


def bucket_bias(table_heads, buckets):
    total = jnp.zeros(table_heads.shape[:2] + buckets.shape[1:], jnp.float32)
    for column in range(BUCKETS):
        total = total + jnp.where(
            buckets[None] == column, table_heads[:, :, column][:, :, None], 0.0
        )
    return total


def self_scores(query_heads, key_heads, table_heads, own_keys, buckets, allowed, main_flag):
    score_scale = HEAD_DIM ** (-0.5)
    raw_scores = (
        jnp.einsum("hqd,hkd->hqk", query_heads, key_heads, preferred_element_type=jnp.float32)
        * score_scale
    )
    scores = raw_scores + bucket_bias(table_heads, buckets)
    own_score = (
        jnp.sum(query_heads.astype(jnp.float32) * own_keys.astype(jnp.float32), axis=2)
        * score_scale
    )
    own_score = own_score + table_heads[:, :, 0]
    scores = jnp.where(allowed[None], scores, MASKED)
    own_score = jnp.where(main_flag[None], MASKED, own_score)
    return (scores, own_score)


def self_forward(pieces, buckets, allowed, main_flag):
    query_heads, key_heads, value_heads, table_heads, own_keys, own_values = pieces
    scores, own_score = self_scores(
        query_heads, key_heads, table_heads, own_keys, buckets, allowed, main_flag
    )
    row_top = jnp.maximum(jnp.max(scores, axis=2), own_score)
    weights = jnp.exp(scores - row_top[:, :, None])
    own_weight = jnp.exp(own_score - row_top)
    row_total = jnp.sum(weights, axis=2) + own_weight
    probabilities = (weights / row_total[:, :, None]).astype(jnp.bfloat16)
    own_prob = (own_weight / row_total).astype(jnp.bfloat16)
    context = jnp.einsum(
        "hqk,hkd->hqd", probabilities, value_heads, preferred_element_type=jnp.float32
    )
    context = context + own_prob.astype(jnp.float32)[:, :, None] * own_values.astype(jnp.float32)
    return (context, row_top + jnp.log(row_total))


def self_backward(pieces, buckets, allowed, main_flag, one_hot):
    (
        query_heads,
        key_heads,
        value_heads,
        table_heads,
        own_keys,
        own_values,
        log_total,
        context_grad,
    ) = pieces
    score_scale = HEAD_DIM ** (-0.5)
    scores, own_score = self_scores(
        query_heads, key_heads, table_heads, own_keys, buckets, allowed, main_flag
    )
    probs_full = jnp.exp(scores - log_total[:, :, None])
    own_full = jnp.exp(own_score - log_total)
    prob_grad = jnp.einsum(
        "hqd,hkd->hqk", context_grad, value_heads, preferred_element_type=jnp.float32
    )
    context_wide = context_grad.astype(jnp.float32)
    own_prob_grad = jnp.sum(context_wide * own_values.astype(jnp.float32), axis=2)
    row_dot = jnp.sum(probs_full * prob_grad, axis=2) + own_full * own_prob_grad
    score_grad = (probs_full * (prob_grad - row_dot[:, :, None])).astype(jnp.bfloat16)
    own_grad = (own_full * (own_prob_grad - row_dot)).astype(jnp.bfloat16)
    own_wide = own_grad.astype(jnp.float32)[:, :, None]
    query_grad = jnp.einsum(
        "hqk,hkd->hqd", score_grad, key_heads, preferred_element_type=jnp.float32
    )
    query_grad = (query_grad + own_wide * own_keys.astype(jnp.float32)) * score_scale
    key_grad = (
        jnp.einsum("hqk,hqd->hkd", score_grad, query_heads, preferred_element_type=jnp.float32)
        * score_scale
    )
    own_key_grad = own_wide * query_heads.astype(jnp.float32) * score_scale
    value_grad = jnp.einsum(
        "hqk,hqd->hkd",
        probs_full.astype(jnp.bfloat16),
        context_grad,
        preferred_element_type=jnp.float32,
    )
    own_value_grad = own_full.astype(jnp.bfloat16).astype(jnp.float32)[:, :, None] * context_wide
    table_grad = jnp.einsum("hqk,qkb->hqb", score_grad, one_hot, preferred_element_type=jnp.float32)
    table_grad = table_grad.at[:, :, 0].add(own_grad.astype(jnp.float32))
    return (query_grad, key_grad, value_grad, own_key_grad, own_value_grad, table_grad)


def cross_scores(query_heads, key_heads, same_doc):
    score_scale = HEAD_DIM ** (-0.5)
    raw_scores = (
        jnp.einsum("hqd,hkd->hqk", query_heads, key_heads, preferred_element_type=jnp.float32)
        * score_scale
    )
    return jnp.where(same_doc[None], raw_scores, MASKED)


def cross_forward(pieces, same_doc):
    query_heads, key_heads, value_heads = pieces
    scores = cross_scores(query_heads, key_heads, same_doc)
    row_top = jnp.max(scores, axis=2)
    weights = jnp.exp(scores - row_top[:, :, None])
    row_total = jnp.sum(weights, axis=2)
    probabilities = (weights / row_total[:, :, None]).astype(jnp.bfloat16)
    context = jnp.einsum(
        "hqk,hkd->hqd", probabilities, value_heads, preferred_element_type=jnp.float32
    )
    return (context, row_top + jnp.log(row_total))


def cross_backward(pieces, same_doc):
    query_heads, key_heads, value_heads, log_total, context_grad = pieces
    score_scale = HEAD_DIM ** (-0.5)
    scores = cross_scores(query_heads, key_heads, same_doc)
    probs_full = jnp.exp(scores - log_total[:, :, None])
    prob_grad = jnp.einsum(
        "hqd,hkd->hqk", context_grad, value_heads, preferred_element_type=jnp.float32
    )
    row_dot = jnp.sum(probs_full * prob_grad, axis=2)
    score_grad = (probs_full * (prob_grad - row_dot[:, :, None])).astype(jnp.bfloat16)
    query_grad = (
        jnp.einsum("hqk,hkd->hqd", score_grad, key_heads, preferred_element_type=jnp.float32)
        * score_scale
    )
    key_grad = (
        jnp.einsum("hqk,hqd->hkd", score_grad, query_heads, preferred_element_type=jnp.float32)
        * score_scale
    )
    value_grad = jnp.einsum(
        "hqk,hqd->hkd",
        probs_full.astype(jnp.bfloat16),
        context_grad,
        preferred_element_type=jnp.float32,
    )
    return (query_grad, key_grad, value_grad)


def adam_step(master, first_moment, second_moment, gradient, step_rate, step_decay):
    first_new = BETA_FIRST * first_moment + (1.0 - BETA_FIRST) * gradient
    second_new = BETA_SECOND * second_moment + (1.0 - BETA_SECOND) * gradient * gradient
    first_hat = first_new / (1.0 - BETA_FIRST**STEP)
    second_hat = second_new / (1.0 - BETA_SECOND**STEP)
    master_new = master - step_rate * (
        first_hat / (jnp.sqrt(second_hat) + ADAM_EPS) + step_decay * master
    )
    return (master_new, first_new, second_new)


def column_sums(left_side, right_side):
    return outer_sum(left_side, right_side).astype(jnp.bfloat16)


def inner_levels(dp_count):
    levels = [("dp", 1, 2), ("stream", 1, 2)]
    if dp_count == 64:
        return levels + [("dp", 2, 2), ("dp", 4, 4)]
    return levels + [("dp", 2, 2)]


def rotation(level, shift, dp_count):
    axis, stride, size = level
    total = 2 if axis == "stream" else dp_count
    pairs = []
    for source in range(total):
        place = (source // stride) % size
        target = source + ((place + shift) % size - place) * stride
        pairs.append((source, target))
    return pairs


def place_on(level):
    axis, stride, size = level
    return (lax.axis_index(axis) // stride) % size


def pick(stacked, index, dim):
    return lax.dynamic_index_in_dim(stacked, index, dim, keepdims=False)


def scatter_level(stacked, dim, level, dp_count, final_type):
    axis, stride, size = level
    mine = place_on(level)
    total = pick(stacked, mine, dim).astype(jnp.float32)
    for shift in range(1, size):
        sent = pick(stacked, (mine + shift) % size, dim)
        came = lax.ppermute(sent, axis, rotation(level, shift, dp_count))
        total = total + came.astype(jnp.float32)
    return total.astype(final_type)


def scatter_rows(rows, outer_range, dp_count):
    levels = inner_levels(dp_count)
    inner = levels[2:]
    sizes = [size for axis, stride, size in reversed(inner)]
    outer_count = len(outer_range)
    width = rows.shape[1]
    block = rows.shape[0] // (outer_count * math.prod(sizes) * 4)
    stacked = rows.reshape([outer_count] + sizes + [2, 2, block, width])
    core_dim = 1 + len(sizes)
    stacked = scatter_level(stacked, core_dim, levels[0], dp_count, jnp.bfloat16)
    outer_level = ("dp", dp_count // 4, 4)
    zi = place_on(outer_level)
    results = []
    for part in range(2):
        cut = (block // 2 + 15) // 16 * 16
        piece = stacked[..., :cut, :] if part == 0 else stacked[..., cut:, :]
        names = list(reversed(inner)) + [levels[1]]
        order = [levels[1]] + inner if part == 0 else [inner[0], levels[1]] + inner[1:]
        for level in order:
            dim = 1 + names.index(level)
            names.remove(level)
            piece = scatter_level(piece, dim, level, dp_count, jnp.bfloat16)
        first = outer_range[0]
        total = pick(piece, jnp.clip(zi - first, 0, outer_count - 1), 0).astype(jnp.float32)
        for shift in range(1, 4):
            pairs = [
                pair
                for pair in rotation(outer_level, shift, dp_count)
                if pair[1] // outer_level[1] in outer_range
            ]
            target = jnp.clip((zi + shift) % 4 - first, 0, outer_count - 1)
            total = total + lax.ppermute(pick(piece, target, 0), "dp", pairs).astype(jnp.float32)
        results.append(total)
    return jnp.concatenate(results)


def local(
    dp_count,
    main_rows,
    pred_rows,
    enc_rows,
    doc_lengths,
    main_cotangent,
    pred_cotangent,
    proj_master,
    proj_first,
    proj_second,
    bias_master,
    bias_first,
    bias_second,
    down_master,
    down_first,
    down_second,
    small_master,
    small_first,
    small_second,
):
    proj_low = proj_master.astype(jnp.bfloat16).T
    bias_low = bias_master.astype(jnp.bfloat16)
    down_low = down_master.astype(jnp.bfloat16)
    proj_rows, bias_weight, down_weight = (
        lax.all_gather(proj_low, ("dp", "stream"), axis=0, tiled=True),
        lax.all_gather(bias_low, ("dp", "stream"), axis=0, tiled=True),
        lax.all_gather(down_low, ("dp", "stream"), axis=0, tiled=True),
    )
    proj_weight = proj_rows.T
    rel_width = BUCKETS * HEADS
    cross_start = 4 * D + rel_width
    self_weight = proj_weight[:, 0 : 3 * D]
    out_weight = proj_weight[:, 3 * D : 4 * D]
    table_weight = proj_weight[:, 4 * D : cross_start]
    cross_weight = proj_weight[:, cross_start : cross_start + D]
    pair_weight = proj_weight[:, cross_start + D : cross_start + 3 * D]
    back_weight = proj_weight[:, cross_start + 3 * D : cross_start + 4 * D]
    up_weight = proj_weight[:, cross_start + 4 * D :]
    bias_wide = bias_weight.astype(jnp.float32)
    query_bias = bias_wide[0:D]
    value_bias = bias_wide[D : 2 * D]
    out_bias = bias_wide[2 * D : 3 * D]
    table_bias = bias_wide[3 * D : 3 * D + rel_width]
    cross_bias = bias_wide[3 * D + rel_width : 4 * D + rel_width]
    pair_bias = bias_wide[4 * D + rel_width : 5 * D + rel_width]
    back_bias = bias_wide[5 * D + rel_width : 6 * D + rel_width]
    up_bias = bias_wide[6 * D + rel_width :]
    zero_bias = jnp.zeros((D,), jnp.float32)
    half_rows = main_rows.shape[0]
    group_rows = pred_rows.shape[0]
    main_start = lax.axis_index("stream") * half_rows
    zi = place_on(("dp", dp_count // 4, 4))
    places = jnp.arange(group_rows, dtype=jnp.int32)
    group_docs = doc_ids(doc_lengths[0], group_rows)
    query_docs = jnp.concatenate(
        [lax.dynamic_slice_in_dim(group_docs, main_start, half_rows), group_docs]
    )
    query_places = jnp.concatenate([main_start + jnp.arange(half_rows, dtype=jnp.int32), places])
    main_flag = jnp.arange(half_rows + group_rows, dtype=jnp.int32) < half_rows
    same_doc = query_docs[:, None] == group_docs[None, :]
    distance = query_places[:, None] - places[None, :]
    allowed = same_doc & ((distance > 0) | (distance == 0) & main_flag[:, None])
    buckets = bucket_of(jnp.maximum(distance, 0))
    inputs = jnp.concatenate([main_rows, pred_rows], axis=0)
    input_values = inputs.astype(jnp.float32)
    self_low = (
        matmul(inputs, self_weight) + jnp.concatenate([query_bias, zero_bias, value_bias])
    ).astype(jnp.bfloat16)
    query_rows = self_low[:, 0:D]
    key_rows = self_low[:, D : 2 * D]
    value_rows = self_low[:, 2 * D :]
    table = matmul(inputs, table_weight) + table_bias
    key_main, value_main = (
        lax.all_gather(key_rows[:half_rows], "stream", axis=0, tiled=True),
        lax.all_gather(value_rows[:half_rows], "stream", axis=0, tiled=True),
    )
    pair_low = (matmul(enc_rows, pair_weight) + jnp.concatenate([zero_bias, pair_bias])).astype(
        jnp.bfloat16
    )
    cross_keys, cross_values = (
        lax.all_gather(pair_low[:, 0:D], "stream", axis=0, tiled=True),
        lax.all_gather(pair_low[:, D:], "stream", axis=0, tiled=True),
    )
    self_pieces = (
        split_heads(query_rows),
        split_heads(key_main),
        split_heads(value_main),
        split_table(table),
        split_heads(key_rows),
        split_heads(value_rows),
    )
    context_stack, self_log = lax.map(
        partial(self_forward, buckets=buckets, allowed=allowed, main_flag=main_flag), self_pieces
    )
    context_low = join_heads(context_stack).astype(jnp.bfloat16)
    attn_out = matmul(context_low, out_weight) + out_bias
    norm_one_in = input_values + attn_out
    hidden_one = layer_norm(norm_one_in, small_master[1], small_master[4])
    one_low = hidden_one.astype(jnp.bfloat16)
    cross_query = (matmul(one_low, cross_weight) + cross_bias).astype(jnp.bfloat16)
    cross_pieces = (split_heads(cross_query), split_heads(cross_keys), split_heads(cross_values))
    cross_stack, cross_log = lax.map(partial(cross_forward, same_doc=same_doc), cross_pieces)
    cross_context_low = join_heads(cross_stack).astype(jnp.bfloat16)
    cross_out = matmul(cross_context_low, back_weight) + back_bias
    norm_two_in = hidden_one + cross_out
    hidden_two = layer_norm(norm_two_in, small_master[2], small_master[5])
    two_low = hidden_two.astype(jnp.bfloat16)
    pre_act = matmul(two_low, up_weight) + up_bias
    activated = jax.nn.gelu(pre_act, approximate=False).astype(jnp.bfloat16)
    ffn_out = matmul(activated, down_weight) + small_master[0]
    norm_three_in = hidden_two + ffn_out
    final_rows = layer_norm(norm_three_in, small_master[3], small_master[6])
    cotangent = jnp.concatenate([main_cotangent, pred_cotangent], axis=0).astype(jnp.float32)
    unused, norm_three = jax.vjp(layer_norm, norm_three_in, small_master[3], small_master[6])
    sum_three, gain_three, shift_three = norm_three(cotangent)
    ffn_grad = sum_three.astype(jnp.bfloat16)
    down_shard_grad = scatter_rows(column_sums(activated, ffn_grad), range(4), dp_count)
    act_grad = times_transpose(ffn_grad, down_weight)
    unused, gelu_back = jax.vjp(partial(jax.nn.gelu, approximate=False), pre_act)
    pre_grad = gelu_back(act_grad)[0].astype(jnp.bfloat16)
    up_rows = column_sums(pre_grad, two_low)
    two_grad = sum_three + times_transpose(pre_grad, up_weight)
    unused, norm_two = jax.vjp(layer_norm, norm_two_in, small_master[2], small_master[5])
    sum_two, gain_two, shift_two = norm_two(two_grad)
    branch_grad = sum_two.astype(jnp.bfloat16)
    cross_context_grad = times_transpose(branch_grad, back_weight).astype(jnp.bfloat16)
    cquery_stack, ckey_stack, cvalue_stack = lax.map(
        partial(cross_backward, same_doc=same_doc),
        (
            split_heads(cross_query),
            split_heads(cross_keys),
            split_heads(cross_values),
            cross_log,
            split_heads(cross_context_grad),
        ),
    )
    ckey_grad, cvalue_grad = (
        lax.psum_scatter(
            join_heads(ckey_stack).astype(jnp.bfloat16), "stream", scatter_dimension=0, tiled=True
        ).astype(jnp.float32),
        lax.psum_scatter(
            join_heads(cvalue_stack).astype(jnp.bfloat16), "stream", scatter_dimension=0, tiled=True
        ).astype(jnp.float32),
    )
    pair_grad = jnp.concatenate([ckey_grad, cvalue_grad], axis=1).astype(jnp.bfloat16)
    pair_rows = column_sums(pair_grad, enc_rows)
    half_cols = proj_rows.shape[0] // 2
    early_rows = jnp.concatenate(
        [pair_rows[half_cols - cross_start - D :], column_sums(branch_grad, cross_context_low), up_rows]
    )
    proj_early = scatter_rows(early_rows, range(2, 4), dp_count)
    enc_grad = times_transpose(pair_grad, pair_weight).astype(jnp.bfloat16)
    cquery_grad = join_heads(cquery_stack).astype(jnp.bfloat16)
    one_grad = sum_two + times_transpose(cquery_grad, cross_weight)
    unused, norm_one = jax.vjp(layer_norm, norm_one_in, small_master[1], small_master[4])
    sum_one, gain_one, shift_one = norm_one(one_grad)
    attn_grad = sum_one.astype(jnp.bfloat16)
    context_grad = times_transpose(attn_grad, out_weight).astype(jnp.bfloat16)
    one_hot = (buckets[:, :, None] == jnp.arange(BUCKETS, dtype=jnp.int32)[None, None, :]).astype(
        jnp.bfloat16
    )
    back_pieces = (
        split_heads(query_rows),
        split_heads(key_main),
        split_heads(value_main),
        split_table(table),
        split_heads(key_rows),
        split_heads(value_rows),
        self_log,
        split_heads(context_grad),
    )
    query_stack, key_stack, value_stack, own_key_stack, own_value_stack, table_stack = lax.map(
        partial(
            self_backward, buckets=buckets, allowed=allowed, main_flag=main_flag, one_hot=one_hot
        ),
        back_pieces,
    )
    key_main_grad, value_main_grad = (
        lax.psum_scatter(
            join_heads(key_stack).astype(jnp.bfloat16), "stream", scatter_dimension=0, tiled=True
        ).astype(jnp.float32),
        lax.psum_scatter(
            join_heads(value_stack).astype(jnp.bfloat16), "stream", scatter_dimension=0, tiled=True
        ).astype(jnp.float32),
    )
    key_grad = jnp.concatenate([key_main_grad, join_heads(own_key_stack)[half_rows:]], axis=0)
    value_grad = jnp.concatenate([value_main_grad, join_heads(own_value_stack)[half_rows:]], axis=0)
    self_grad = jnp.concatenate([join_heads(query_stack), key_grad, value_grad], axis=1).astype(
        jnp.bfloat16
    )
    table_grad = join_table(table_stack).astype(jnp.bfloat16)
    input_grad = (
        sum_one
        + times_transpose(self_grad, self_weight)
        + times_transpose(table_grad, table_weight)
    )
    self_sums = jnp.sum(self_grad, axis=0, dtype=jnp.float32)
    late_rows = jnp.concatenate(
        [
            column_sums(self_grad, inputs),
            column_sums(attn_grad, context_low),
            column_sums(table_grad, inputs),
            column_sums(cquery_grad, one_low),
            pair_rows[: half_cols - cross_start - D],
        ]
    )
    proj_late = scatter_rows(late_rows, range(0, 2), dp_count)
    proj_grad = jnp.where(zi < 2, proj_late, proj_early).T
    bias_grad_full = jnp.concatenate(
        [
            self_sums[0:D],
            self_sums[2 * D :],
            jnp.sum(attn_grad, axis=0, dtype=jnp.float32),
            jnp.sum(table_grad, axis=0, dtype=jnp.float32),
            jnp.sum(cquery_grad, axis=0, dtype=jnp.float32),
            jnp.sum(pair_grad[:, D:], axis=0, dtype=jnp.float32),
            jnp.sum(branch_grad, axis=0, dtype=jnp.float32),
            jnp.sum(pre_grad, axis=0, dtype=jnp.float32),
        ]
    )
    small_stack = jnp.stack(
        [
            jnp.sum(ffn_grad, axis=0, dtype=jnp.float32),
            gain_one,
            gain_two,
            gain_three,
            shift_one,
            shift_two,
            shift_three,
        ]
    )
    count = 2 * dp_count
    vector_parts = jnp.concatenate(
        [bias_grad_full.reshape(count, -1), small_stack.reshape(count, -1)], axis=1
    )
    vector_sum = jnp.sum(
        lax.all_to_all(vector_parts, ("dp", "stream"), 0, 0, tiled=True), axis=0
    )
    bias_len = bias_master.shape[0]
    bias_grad = vector_sum[:bias_len]
    small_part = vector_sum[bias_len:]
    small_grad = lax.all_to_all(
        jnp.broadcast_to(small_part[None], (count, small_part.shape[0])),
        ("dp", "stream"),
        0,
        0,
        tiled=True,
    ).reshape(small_master.shape)
    proj_new, proj_first_new, proj_second_new = adam_step(
        proj_master, proj_first, proj_second, proj_grad, RATE_MATRIX, WEIGHT_DECAY
    )
    bias_new, bias_first_new, bias_second_new = adam_step(
        bias_master, bias_first, bias_second, bias_grad, RATE_VECTOR, 0.0
    )
    down_new, down_first_new, down_second_new = adam_step(
        down_master, down_first, down_second, down_shard_grad, RATE_MATRIX, WEIGHT_DECAY
    )
    small_new, small_first_new, small_second_new = adam_step(
        small_master, small_first, small_second, small_grad, RATE_SMALL, 0.0
    )
    return (
        final_rows[:half_rows].astype(jnp.bfloat16),
        final_rows[half_rows:].astype(jnp.bfloat16),
        input_grad[:half_rows].astype(jnp.bfloat16),
        input_grad[half_rows:].astype(jnp.bfloat16),
        enc_grad,
        proj_new,
        proj_first_new,
        proj_second_new,
        bias_new,
        bias_first_new,
        bias_second_new,
        down_new,
        down_first_new,
        down_second_new,
        small_new,
        small_first_new,
        small_second_new,
    )


def solution(mesh):
    placed = (
        P(("dp", "stream"), None),
        P(("dp", "stream"), None),
        P(("dp", "stream"), None),
        P("dp", None),
        P(("dp", "stream"), None),
        P(("dp", "stream"), None),
        P(None, ("dp", "stream")),
        P(None, ("dp", "stream")),
        P(None, ("dp", "stream")),
        P(("dp", "stream")),
        P(("dp", "stream")),
        P(("dp", "stream")),
        P(("dp", "stream"), None),
        P(("dp", "stream"), None),
        P(("dp", "stream"), None),
        P(),
        P(),
        P(),
    )
    return jax.shard_map(
        partial(local, mesh.shape["dp"]),
        mesh=mesh,
        in_specs=placed,
        out_specs=(
            P(("dp", "stream"), None),
            P(("dp", "stream"), None),
            P(("dp", "stream"), None),
            P(("dp", "stream"), None),
            P(("dp", "stream"), None),
            P(None, ("dp", "stream")),
            P(None, ("dp", "stream")),
            P(None, ("dp", "stream")),
            P(("dp", "stream")),
            P(("dp", "stream")),
            P(("dp", "stream")),
            P(("dp", "stream"), None),
            P(("dp", "stream"), None),
            P(("dp", "stream"), None),
            P(),
            P(),
            P(),
        ),
        check_vma=False,
    )
```

```python
from functools import partial
import math

import jax
import jax.numpy as jnp
from jax import lax
from jax.experimental import pallas as pl
from jax.experimental.pallas import tpu as pltpu
from jax.sharding import PartitionSpec as P

D = 1024
HEADS = 16
BUCKETS = 32
STEP = 10
HEAD_DIM = 64
LANES = 128
CHUNK = 128
SCORE_SCALE = HEAD_DIM**-0.5

NORM_EPS = 1e-05
BETA_FIRST = 0.9
BETA_SECOND = 0.999
ADAM_EPS = 1e-08
RATE_MATRIX = 0.04
RATE_VECTOR = 0.15
RATE_SMALL = 0.5
WEIGHT_DECAY = 0.01
MASKED = -1e30


def bucket_edges():
    return [int(math.ceil(16.0 * 8.0 ** (step_index / 16.0))) for step_index in range(1, 16)]


def bucket_of(distance):
    counted = jnp.zeros_like(distance)
    for threshold in bucket_edges():
        counted = counted + (distance >= threshold).astype(jnp.int32)
    return jnp.where(distance < 16, distance, 16 + counted)


def doc_ids(lengths, length_total):
    doc_ends = jnp.cumsum(lengths)
    places = jnp.arange(length_total, dtype=jnp.int32)
    return jnp.sum((places[:, None] >= doc_ends[None, :]).astype(jnp.int32), axis=1)


def matmul(left_side, right_side):
    return jnp.dot(left_side, right_side, preferred_element_type=jnp.float32)


def outer_sum(left_side, right_side):
    return lax.dot_general(
        left_side, right_side, (((0,), (0,)), ((), ())), preferred_element_type=jnp.float32
    )


def times_transpose(left_side, right_side):
    return lax.dot_general(
        left_side, right_side, (((1,), (1,)), ((), ())), preferred_element_type=jnp.float32
    )


def norm_stats(hidden):
    mean = jnp.mean(hidden, axis=-1, keepdims=True)
    centre = hidden - mean
    spread = jnp.mean(centre * centre, axis=-1, keepdims=True)
    return mean, lax.rsqrt(spread + NORM_EPS)


def norm_back(hidden, stats, gain_row, grad):
    mean, inverse = stats
    normed = (hidden - mean) * inverse
    scaled = grad * gain_row
    first = jnp.mean(scaled, axis=-1, keepdims=True)
    second = jnp.mean(scaled * normed, axis=-1, keepdims=True)
    hidden_grad = (scaled - first - normed * second) * inverse
    return hidden_grad, jnp.sum(grad * normed, axis=0), jnp.sum(grad, axis=0)


def gelu_and_slope(values):
    size = jnp.abs(values) * (0.5**0.5)
    place = 1.0 / (1.0 + 0.5 * size)
    fit = 0.17087277
    for coefficient in (
        -0.82215223,
        1.48851587,
        -1.13520398,
        0.27886807,
        -0.18628806,
        0.09678418,
        0.37409196,
        1.00002368,
        -1.26551223,
    ):
        fit = fit * place + coefficient
    bell = jnp.exp(-size * size)
    tail = 0.5 * place * bell * jnp.exp(fit)
    below = jnp.where(values >= 0.0, 1.0 - tail, tail)
    return values * below, below + values * bell * (1.0 / math.sqrt(2.0 * math.pi))


def dot_rows(left_side, right_side):
    return lax.dot_general(
        left_side, right_side, (((1,), (1,)), ((), ())), preferred_element_type=jnp.float32
    )


def lookup(table, index):
    return jnp.take_along_axis(table, index, axis=1, mode="promise_in_bounds")


def wide(column):
    return jnp.broadcast_to(column, (column.shape[0], LANES))


def tiled(block, key_count):
    return jnp.concatenate([block] * (key_count // LANES), axis=1)


def row_blocks(main_count, key_count, size):
    blocks = [(at, min(size, main_count - at), key_count) for at in range(0, main_count, size)]
    step = min(size, LANES)
    for at in range(0, key_count, step):
        seen = min(key_count, (at + step + LANES - 1) // LANES * LANES)
        blocks.append((main_count + at, min(step, key_count - at), seen))
    return blocks


def bias_of(near_bias, far_bias, edge, row_count, key_count):
    lane = lax.broadcasted_iota(jnp.int32, (row_count, LANES), 1)
    return jnp.concatenate(
        [
            jnp.where(lane + at > edge, near_bias, far_bias)
            for at in range(0, key_count, LANES)
        ],
        axis=1,
    )


def both_halves(block, head):
    lane = lax.broadcasted_iota(jnp.int32, block.shape, 1)
    turned = pltpu.roll(block, HEAD_DIM, 1)
    return jnp.where((lane < HEAD_DIM) == (head == 0), block, turned)


def self_forward_kernel(
    query_ref,
    key_ref,
    value_ref,
    own_key_ref,
    own_value_ref,
    table_ref,
    spread_ref,
    edge_ref,
    mask_ref,
    context_ref,
    log_ref,
    score_ref,
    prob_ref,
    near_ref,
    far_ref,
):
    rows, key_count = mask_ref.shape
    main_count = rows - key_count
    parity = lax.rem(pl.program_id(0), 2)
    groups = row_blocks(main_count, key_count, 512)
    chunks = row_blocks(main_count, key_count, CHUNK)
    for head in range(2):
        at = head * HEAD_DIM
        head_lanes = slice(at, at + HEAD_DIM)
        first = (parity * 2 + head) * BUCKETS
        query = query_ref[:, head_lanes] * jnp.bfloat16(SCORE_SCALE)
        keys = key_ref[:, head_lanes]
        values = value_ref[:, head_lanes]
        own_keys = own_key_ref[:, head_lanes].astype(jnp.float32)
        own_values = own_value_ref[:, head_lanes].astype(jnp.float32)
        near_ref[head] = lookup(table_ref[...], spread_ref[...] + first)
        far_ref[head] = lookup(
            table_ref[...], jnp.full((rows, LANES), first + BUCKETS - 1, jnp.int32)
        )
        own_score = wide(
            jnp.sum(query[main_count:].astype(jnp.float32) * own_keys, axis=1, keepdims=True)
        ) + lookup(table_ref[main_count:, :], jnp.full((key_count, LANES), first, jnp.int32))
        for row, count, seen in groups:
            score_ref[head, row : row + count, 0:seen] = dot_rows(
                query[row : row + count], keys[0:seen]
            )
        tops = []
        for row, count, seen in chunks:
            part = slice(row, row + count)
            scores = (
                score_ref[head, part, 0:seen]
                + bias_of(near_ref[head, part], far_ref[head, part], edge_ref[part], count, seen)
                + mask_ref[part, 0:seen]
            )
            score_ref[head, part, 0:seen] = scores
            tops.append(wide(jnp.max(scores, axis=1, keepdims=True)))
        top = jnp.concatenate(tops, axis=0)
        top = jnp.concatenate(
            [top[:main_count], jnp.maximum(top[main_count:], own_score)], axis=0
        )
        own_weight = jnp.exp(own_score - top[main_count:])
        totals = []
        for row, count, seen in chunks:
            part = slice(row, row + count)
            weights = jnp.exp(score_ref[head, part, 0:seen] - tiled(top[part], seen))
            score_ref[head, part, 0:seen] = weights
            totals.append(wide(jnp.sum(weights, axis=1, keepdims=True)))
        total = jnp.concatenate(totals, axis=0)
        total = jnp.concatenate([total[:main_count], total[main_count:] + own_weight], axis=0)
        inverse = 1.0 / total
        log_ref[:, head_lanes] = (top + jnp.log(total))[:, 0:HEAD_DIM]
        own_prob = (own_weight * inverse[main_count:]).astype(jnp.bfloat16).astype(jnp.float32)
        for row, count, seen in chunks:
            part = slice(row, row + count)
            prob_ref[head, part, 0:seen] = (
                score_ref[head, part, 0:seen] * tiled(inverse[part], seen)
            ).astype(jnp.bfloat16)
        for row, count, seen in groups:
            part = slice(row, row + count)
            context = matmul(prob_ref[head, part, 0:seen], values[0:seen])
            if row >= main_count:
                own = slice(row - main_count, row - main_count + count)
                context = context + own_prob[own, 0:HEAD_DIM] * own_values[own]
            context_ref[part, head_lanes] = context.astype(jnp.bfloat16)


def self_backward_kernel(
    query_ref,
    key_ref,
    value_ref,
    own_key_ref,
    own_value_ref,
    table_ref,
    spread_ref,
    edge_ref,
    turn_ref,
    mask_ref,
    log_ref,
    context_ref,
    query_grad_ref,
    key_grad_ref,
    value_grad_ref,
    table_grad_ref,
    score_ref,
    prob_grad_ref,
    prob_ref,
    score_grad_ref,
    near_ref,
    far_ref,
    close_ref,
    rest_ref,
):
    rows, key_count = mask_ref.shape
    main_count = rows - key_count
    parity = lax.rem(pl.program_id(0), 2)
    groups = row_blocks(main_count, key_count, 512)
    chunks = row_blocks(main_count, key_count, CHUNK)
    bucket = bucket_of(lax.broadcasted_iota(jnp.int32, (LANES, LANES), 0))
    bucket_lane = lax.broadcasted_iota(jnp.int32, (LANES, LANES), 1)
    row_lane = lax.broadcasted_iota(jnp.int32, (rows, LANES), 1)
    table_total = jnp.zeros((rows, LANES), jnp.float32)
    own_total = jnp.zeros((key_count, LANES), jnp.float32)
    for head in range(2):
        at = head * HEAD_DIM
        head_lanes = slice(at, at + HEAD_DIM)
        first = (parity * 2 + head) * BUCKETS
        query = query_ref[:, head_lanes] * jnp.bfloat16(SCORE_SCALE)
        keys = key_ref[:, head_lanes]
        values = value_ref[:, head_lanes]
        context = context_ref[:, head_lanes]
        own_keys = own_key_ref[:, head_lanes].astype(jnp.float32)
        own_values = own_value_ref[:, head_lanes].astype(jnp.float32)
        own_query = query[main_count:].astype(jnp.float32)
        own_context = context[main_count:].astype(jnp.float32)
        near_ref[head] = lookup(table_ref[...], spread_ref[...] + first)
        far_ref[head] = lookup(
            table_ref[...], jnp.full((rows, LANES), first + BUCKETS - 1, jnp.int32)
        )
        own_score = wide(jnp.sum(own_query * own_keys, axis=1, keepdims=True)) + lookup(
            table_ref[main_count:, :], jnp.full((key_count, LANES), first, jnp.int32)
        )
        log_total = both_halves(log_ref[...], head)
        own_prob = jnp.exp(own_score - log_total[main_count:])
        own_prob_grad = wide(jnp.sum(own_context * own_values, axis=1, keepdims=True))
        value_grad_ref[key_count:, head_lanes] = (
            own_prob[:, 0:HEAD_DIM].astype(jnp.bfloat16).astype(jnp.float32) * own_context
        ).astype(jnp.bfloat16)
        for row, count, seen in groups:
            part = slice(row, row + count)
            score_ref[head, part, 0:seen] = dot_rows(query[part], keys[0:seen])
            prob_grad_ref[head, part, 0:seen] = dot_rows(context[part], values[0:seen])
        row_dots = []
        for row, count, seen in chunks:
            part = slice(row, row + count)
            edge = edge_ref[part]
            bias = bias_of(near_ref[head, part], far_ref[head, part], edge, count, seen)
            probs = jnp.exp(
                score_ref[head, part, 0:seen]
                + bias
                + (mask_ref[part, 0:seen] - tiled(log_total[part], seen))
            )
            prob_grad = prob_grad_ref[head, part, 0:seen]
            row_dot = wide(jnp.sum(probs * prob_grad, axis=1, keepdims=True))
            if row >= main_count:
                own = slice(row - main_count, row - main_count + count)
                row_dot = row_dot + own_prob[own] * own_prob_grad[own]
                row_dots.append(row_dot)
            score_grad = (probs * (prob_grad - tiled(row_dot, seen))).astype(jnp.bfloat16)
            prob_ref[head, part, 0:seen] = probs.astype(jnp.bfloat16)
            score_grad_ref[head, part, 0:seen] = score_grad
            score_wide = score_grad.astype(jnp.float32)
            lane = lax.broadcasted_iota(jnp.int32, (count, LANES), 1)
            close = jnp.zeros((count, LANES), jnp.float32)
            whole = jnp.zeros((count, LANES), jnp.float32)
            for at_key in range(0, seen, LANES):
                block = score_wide[:, at_key : at_key + LANES]
                whole = whole + block
                close = close + jnp.where(lane + at_key > edge, block, 0.0)
            close_ref[head, part] = close
            rest_ref[head, part] = whole - close
        own_grad = (
            (own_prob * (own_prob_grad - jnp.concatenate(row_dots, axis=0)))
            .astype(jnp.bfloat16)
            .astype(jnp.float32)
        )
        key_grad_ref[key_count:, head_lanes] = (own_grad[:, 0:HEAD_DIM] * own_query).astype(
            jnp.bfloat16
        )
        turned = lookup(close_ref[head], turn_ref[...]).astype(jnp.bfloat16)
        table_total = table_total + matmul(
            turned, (bucket_lane == bucket + first).astype(jnp.bfloat16)
        )
        table_total = table_total + jnp.where(
            row_lane == first + BUCKETS - 1, jnp.sum(rest_ref[head], axis=1, keepdims=True), 0.0
        )
        own_total = own_total + jnp.where(row_lane[main_count:] == first, own_grad, 0.0)
        for row, count, seen in groups:
            part = slice(row, row + count)
            query_grad = matmul(score_grad_ref[head, part, 0:seen], keys[0:seen])
            if row >= main_count:
                own = slice(row - main_count, row - main_count + count)
                query_grad = query_grad + own_grad[own, 0:HEAD_DIM] * own_keys[own]
            query_grad_ref[part, head_lanes] = (query_grad * SCORE_SCALE).astype(jnp.bfloat16)
        for at_key in range(0, key_count, LANES):
            block = slice(at_key, at_key + LANES)
            later = slice(main_count + at_key, rows)
            key_grad_ref[block, head_lanes] = (
                outer_sum(score_grad_ref[head, 0:main_count, block], query[0:main_count])
                + outer_sum(score_grad_ref[head, later, block], query[later])
            ).astype(jnp.bfloat16)
            value_grad_ref[block, head_lanes] = (
                outer_sum(prob_ref[head, 0:main_count, block], context[0:main_count])
                + outer_sum(prob_ref[head, later, block], context[later])
            ).astype(jnp.bfloat16)
    table_total = jnp.concatenate(
        [table_total[:main_count], table_total[main_count:] + own_total], axis=0
    )

    @pl.when(parity == 0)
    def first_pair():
        table_grad_ref[...] = table_total

    @pl.when(parity == 1)
    def second_pair():
        table_grad_ref[...] += table_total


def cross_forward_kernel(
    query_ref, key_ref, value_ref, mask_ref, context_ref, log_ref, score_ref, prob_ref
):
    rows = mask_ref.shape[0]
    for head in range(2):
        at = head * HEAD_DIM
        head_lanes = slice(at, at + HEAD_DIM)
        query = query_ref[:, head_lanes] * jnp.bfloat16(SCORE_SCALE)
        score_ref[head] = dot_rows(query, key_ref[:, head_lanes])
        for row in range(0, rows, CHUNK):
            part = slice(row, min(row + CHUNK, rows))
            scores = score_ref[head, part] + mask_ref[part]
            top = jnp.max(scores, axis=1, keepdims=True)
            weights = jnp.exp(scores - top)
            total = jnp.sum(weights, axis=1, keepdims=True)
            prob_ref[head, part] = (weights * (1.0 / total)).astype(jnp.bfloat16)
            log_ref[part, head_lanes] = jnp.broadcast_to(
                top + jnp.log(total), (scores.shape[0], HEAD_DIM)
            )
        context_ref[:, head_lanes] = matmul(prob_ref[head], value_ref[:, head_lanes]).astype(
            jnp.bfloat16
        )


def cross_backward_kernel(
    query_ref,
    key_ref,
    value_ref,
    mask_ref,
    log_ref,
    context_ref,
    query_grad_ref,
    key_grad_ref,
    value_grad_ref,
    score_ref,
    prob_grad_ref,
    prob_ref,
    score_grad_ref,
):
    rows = mask_ref.shape[0]
    for head in range(2):
        at = head * HEAD_DIM
        head_lanes = slice(at, at + HEAD_DIM)
        query = query_ref[:, head_lanes] * jnp.bfloat16(SCORE_SCALE)
        keys = key_ref[:, head_lanes]
        context = context_ref[:, head_lanes]
        score_ref[head] = dot_rows(query, keys)
        prob_grad_ref[head] = dot_rows(context, value_ref[:, head_lanes])
        for row in range(0, rows, CHUNK):
            part = slice(row, min(row + CHUNK, rows))
            probs = jnp.exp(
                score_ref[head, part] + (mask_ref[part] - log_ref[part, at : at + 1])
            )
            prob_grad = prob_grad_ref[head, part]
            row_dot = jnp.sum(probs * prob_grad, axis=1, keepdims=True)
            prob_ref[head, part] = probs.astype(jnp.bfloat16)
            score_grad_ref[head, part] = (probs * (prob_grad - row_dot)).astype(jnp.bfloat16)
        query_grad_ref[:, head_lanes] = (matmul(score_grad_ref[head], keys) * SCORE_SCALE).astype(
            jnp.bfloat16
        )
        key_grad_ref[:, head_lanes] = outer_sum(score_grad_ref[head], query).astype(jnp.bfloat16)
        value_grad_ref[:, head_lanes] = outer_sum(prob_ref[head], context).astype(jnp.bfloat16)


def pair_block(row_count, row_block=0, first_pair=0):
    return pl.BlockSpec((row_count, LANES), lambda pair: (row_block, first_pair + pair))


def whole_block(shape):
    return pl.BlockSpec(shape, lambda pair: (0, 0))


def attention_call(kernel, name, in_specs, out_specs, out_shape, scratch, arrays, flops, passes):
    moved = sum(array.size * array.dtype.itemsize for array in arrays)
    moved += sum(math.prod(shape.shape) * shape.dtype.itemsize for shape in out_shape)
    return pl.pallas_call(
        kernel,
        grid=(HEADS // 2,),
        in_specs=in_specs,
        out_specs=out_specs,
        out_shape=out_shape,
        scratch_shapes=scratch,
        compiler_params=pltpu.CompilerParams(vmem_limit_bytes=56 * 2**20),
        cost_estimate=pl.CostEstimate(flops=flops, bytes_accessed=moved, transcendentals=passes),
        name=name,
    )(*arrays)


def low_array(row_count):
    return jax.ShapeDtypeStruct((row_count, D), jnp.bfloat16)


def self_forward(query, pairs, table, spread, edge, mask):
    rows, keys = mask.shape
    width = D // LANES
    square = pltpu.VMEM((2, rows, keys), jnp.float32)
    narrow = pltpu.VMEM((2, rows, LANES), jnp.float32)
    return attention_call(
        self_forward_kernel,
        "self_forward",
        [
            pair_block(rows),
            pair_block(keys),
            pair_block(keys, 0, width),
            pair_block(keys, 1),
            pair_block(keys, 1, width),
            pl.BlockSpec((rows, LANES), lambda pair: (0, pair // 2)),
            whole_block((rows, LANES)),
            whole_block((rows, LANES)),
            whole_block((rows, keys)),
        ],
        [pair_block(rows), pair_block(rows)],
        [low_array(rows), jax.ShapeDtypeStruct((rows, D), jnp.float32)],
        [square, pltpu.VMEM((2, rows, keys), jnp.bfloat16), narrow, narrow],
        (query, pairs, pairs, pairs, pairs, table, spread, edge, mask),
        4 * rows * keys * D,
        rows * keys * HEADS,
    )


def self_backward(query, pairs, table, spread, edge, turn, mask, log_total, context_grad):
    rows, keys = mask.shape
    width = D // LANES
    square = pltpu.VMEM((2, rows, keys), jnp.float32)
    square_low = pltpu.VMEM((2, rows, keys), jnp.bfloat16)
    narrow = pltpu.VMEM((2, rows, LANES), jnp.float32)
    table_block = pl.BlockSpec((rows, LANES), lambda pair: (0, pair // 2))
    return attention_call(
        self_backward_kernel,
        "self_backward",
        [
            pair_block(rows),
            pair_block(keys),
            pair_block(keys, 0, width),
            pair_block(keys, 1),
            pair_block(keys, 1, width),
            table_block,
            whole_block((rows, LANES)),
            whole_block((rows, LANES)),
            whole_block((rows, LANES)),
            whole_block((rows, keys)),
            pair_block(rows),
            pair_block(rows),
        ],
        [pair_block(rows), pair_block(2 * keys), pair_block(2 * keys), table_block],
        [
            low_array(rows),
            low_array(2 * keys),
            low_array(2 * keys),
            jax.ShapeDtypeStruct(table.shape, jnp.float32),
        ],
        [square, square, square_low, square_low, narrow, narrow, narrow, narrow],
        (query, pairs, pairs, pairs, pairs, table, spread, edge, turn, mask, log_total, context_grad),
        10 * rows * keys * D,
        rows * keys * HEADS,
    )


def cross_forward(query, pairs, mask):
    rows, keys = mask.shape
    return attention_call(
        cross_forward_kernel,
        "cross_forward",
        [
            pair_block(rows),
            pair_block(keys),
            pair_block(keys, 0, D // LANES),
            whole_block((rows, keys)),
        ],
        [pair_block(rows), pair_block(rows)],
        [low_array(rows), jax.ShapeDtypeStruct((rows, D), jnp.float32)],
        [pltpu.VMEM((2, rows, keys), jnp.float32), pltpu.VMEM((2, rows, keys), jnp.bfloat16)],
        (query, pairs, pairs, mask),
        4 * rows * keys * D,
        rows * keys * HEADS,
    )


def cross_backward(query, pairs, mask, log_total, context_grad):
    rows, keys = mask.shape
    square = pltpu.VMEM((2, rows, keys), jnp.float32)
    square_low = pltpu.VMEM((2, rows, keys), jnp.bfloat16)
    return attention_call(
        cross_backward_kernel,
        "cross_backward",
        [
            pair_block(rows),
            pair_block(keys),
            pair_block(keys, 0, D // LANES),
            whole_block((rows, keys)),
            pair_block(rows),
            pair_block(rows),
        ],
        [pair_block(rows), pair_block(keys), pair_block(keys)],
        [low_array(rows), low_array(keys), low_array(keys)],
        [square, square, square_low, square_low],
        (query, pairs, pairs, mask, log_total, context_grad),
        10 * rows * keys * D,
        rows * keys * HEADS,
    )


def column_sums(left_side, right_side):
    return outer_sum(left_side, right_side).astype(jnp.bfloat16)


def inner_levels(dp_count):
    levels = [("dp", 1, 2), ("stream", 1, 2)]
    if dp_count == 64:
        return levels + [("dp", 2, 2), ("dp", 4, 4)]
    return levels + [("dp", 2, 2)]


def rotation(level, shift, dp_count):
    axis, stride, size = level
    total = 2 if axis == "stream" else dp_count
    pairs = []
    for source in range(total):
        place = (source // stride) % size
        target = source + ((place + shift) % size - place) * stride
        pairs.append((source, target))
    return pairs


def place_on(level):
    axis, stride, size = level
    return (lax.axis_index(axis) // stride) % size


def pick(stacked, index, dim):
    return lax.dynamic_index_in_dim(stacked, index, dim, keepdims=False)


def scatter_level(stacked, dim, level, dp_count, final_type):
    axis, stride, size = level
    mine = place_on(level)
    total = pick(stacked, mine, dim).astype(jnp.float32)
    for shift in range(1, size):
        sent = pick(stacked, (mine + shift) % size, dim)
        came = lax.ppermute(sent, axis, rotation(level, shift, dp_count))
        total = total + came.astype(jnp.float32)
    return total.astype(final_type)


class Scatter:
    def __init__(self, rows, outer_range, dp_count, parts=2):
        self.levels = inner_levels(dp_count)
        self.inner = self.levels[2:]
        self.outer_range = outer_range
        self.dp_count = dp_count
        self.parts = parts
        sizes = [size for axis, stride, size in reversed(self.inner)]
        self.block = rows.shape[0] // (len(outer_range) * math.prod(sizes) * 4)
        self.state = [
            rows.reshape([len(outer_range)] + sizes + [2, 2, self.block, rows.shape[1]])
        ]
        self.done = 0

    def step(self):
        inner_count = len(self.inner)
        if self.done == 0:
            stacked = scatter_level(
                self.state[0], 1 + inner_count, self.levels[0], self.dp_count, jnp.bfloat16
            )
            if self.parts == 1:
                self.state = [stacked]
            else:
                cut = (self.block // 2 + 15) // 16 * 16
                self.state = [stacked[..., :cut, :], stacked[..., cut:, :]]
            order = [self.levels[1]] + self.inner
            other = [self.inner[0], self.levels[1]] + self.inner[1:]
            self.orders = [order, other]
            self.names = [list(reversed(self.inner)) + [self.levels[1]] for part in range(2)]
        elif self.done <= inner_count + 1:
            for part in range(self.parts):
                level = self.orders[part][self.done - 1]
                dim = 1 + self.names[part].index(level)
                self.names[part].remove(level)
                self.state[part] = scatter_level(
                    self.state[part], dim, level, self.dp_count, jnp.bfloat16
                )
        else:
            self.state = [self.outer_step(piece) for piece in self.state]
        self.done += 1

    def outer_step(self, piece):
        level = ("dp", self.dp_count // 4, 4)
        mine = place_on(level)
        first, count = self.outer_range[0], len(self.outer_range)
        total = pick(piece, jnp.clip(mine - first, 0, count - 1), 0).astype(jnp.float32)
        for shift in range(1, 4):
            pairs = [
                pair
                for pair in rotation(level, shift, self.dp_count)
                if pair[1] // level[1] in self.outer_range
            ]
            target = jnp.clip((mine + shift) % 4 - first, 0, count - 1)
            total = total + lax.ppermute(pick(piece, target, 0), "dp", pairs).astype(jnp.float32)
        return total

    def finish(self):
        while self.done < len(self.inner) + 3:
            self.step()
        return jnp.concatenate(self.state)


def after(value, *scatters):
    states = [array for scatter in scatters for array in scatter.state]
    return lax.optimization_barrier((value, *states))[0]


def to_all(part, count):
    shared = jnp.broadcast_to(part[None], (count, *part.shape))
    gathered = lax.all_to_all(shared, ("dp", "stream"), 0, 0, tiled=True)
    return gathered.reshape(-1, *part.shape[1:])


def swap_streams(rows):
    return lax.ppermute(rows, "stream", [(0, 1), (1, 0)])


def both_parts(rows):
    other = swap_streams(rows)
    leading = lax.axis_index("stream") == 0
    return jnp.concatenate(
        [jnp.where(leading, rows, other), jnp.where(leading, other, rows)], axis=0
    )


def pair_sum(rows):
    half = rows.shape[0] // 2
    stream = lax.axis_index("stream")
    sent = lax.dynamic_slice_in_dim(rows, (1 - stream) * half, half).astype(jnp.bfloat16)
    return lax.dynamic_slice_in_dim(rows, stream * half, half) + swap_streams(sent).astype(
        jnp.float32
    )


def adam_step(master, first_moment, second_moment, gradient, step_rate, step_decay):
    first_new = BETA_FIRST * first_moment + (1.0 - BETA_FIRST) * gradient
    second_new = BETA_SECOND * second_moment + (1.0 - BETA_SECOND) * gradient * gradient
    first_hat = first_new / (1.0 - BETA_FIRST**STEP)
    second_hat = second_new / (1.0 - BETA_SECOND**STEP)
    master_new = master - step_rate * (
        first_hat / (jnp.sqrt(second_hat) + ADAM_EPS) + step_decay * master
    )
    return (master_new, first_new, second_new)


def local(
    dp_count,
    main_rows,
    pred_rows,
    enc_rows,
    doc_lengths,
    main_cotangent,
    pred_cotangent,
    proj_master,
    proj_first,
    proj_second,
    bias_master,
    bias_first,
    bias_second,
    down_master,
    down_first,
    down_second,
    small_master,
    small_first,
    small_second,
):
    devices = 2 * dp_count
    rel_width = BUCKETS * HEADS
    cross_start = 4 * D + rel_width
    half_rows = main_rows.shape[0]
    group_rows = pred_rows.shape[0]

    bias_wide = to_all(bias_master.astype(jnp.bfloat16), devices).astype(jnp.float32)
    proj_rows = lax.all_gather(
        proj_master.astype(jnp.bfloat16).T, ("dp", "stream"), axis=0, tiled=True
    )
    down_weight = lax.all_gather(
        down_master.astype(jnp.bfloat16), ("dp", "stream"), axis=0, tiled=True
    )
    query_weight = proj_rows[0:D]
    keys_weight = proj_rows[D : 3 * D]
    out_weight = proj_rows[3 * D : 4 * D]
    table_weight = (
        proj_rows[4 * D : cross_start]
        .reshape(BUCKETS, HEADS, D)
        .transpose(1, 0, 2)
        .reshape(rel_width, D)
    )
    cross_weight = proj_rows[cross_start : cross_start + D]
    pair_weight = proj_rows[cross_start + D : cross_start + 3 * D]
    back_weight = proj_rows[cross_start + 3 * D : cross_start + 4 * D]
    up_weight = proj_rows[cross_start + 4 * D :]
    query_bias = bias_wide[0:D]
    value_bias = bias_wide[D : 2 * D]
    out_bias = bias_wide[2 * D : 3 * D]
    table_bias = bias_wide[3 * D : 3 * D + rel_width].reshape(BUCKETS, HEADS).T.reshape(rel_width)
    cross_bias = bias_wide[3 * D + rel_width : 4 * D + rel_width]
    pair_bias = bias_wide[4 * D + rel_width : 5 * D + rel_width]
    back_bias = bias_wide[5 * D + rel_width : 6 * D + rel_width]
    up_bias = bias_wide[6 * D + rel_width :]
    zero_bias = jnp.zeros((D,), jnp.float32)

    main_start = lax.axis_index("stream") * half_rows
    places = jnp.arange(group_rows, dtype=jnp.int32)
    group_docs = doc_ids(doc_lengths[0], group_rows)
    query_docs = jnp.concatenate(
        [lax.dynamic_slice_in_dim(group_docs, main_start, half_rows), group_docs]
    )
    query_places = jnp.concatenate([main_start + jnp.arange(half_rows, dtype=jnp.int32), places])
    main_flag = jnp.arange(half_rows + group_rows, dtype=jnp.int32) < half_rows
    same_doc = query_docs[:, None] == group_docs[None, :]
    distance = query_places[:, None] - places[None, :]
    allowed = same_doc & ((distance > 0) | (distance == 0) & main_flag[:, None])
    self_mask = jnp.where(allowed, 0.0, MASKED)
    cross_mask = jnp.where(same_doc, 0.0, MASKED)
    lane = jnp.arange(LANES, dtype=jnp.int32)
    turn = jnp.mod(query_places[:, None] - lane[None, :], LANES)
    spread = bucket_of(turn)
    edge = jnp.broadcast_to(query_places[:, None] - LANES, turn.shape)

    main_all = both_parts(main_rows)
    enc_all = both_parts(enc_rows)
    inputs = jnp.concatenate([main_rows, pred_rows], axis=0)
    key_inputs = jnp.concatenate([main_all, pred_rows], axis=0)
    input_values = inputs.astype(jnp.float32)
    query_low = (times_transpose(inputs, query_weight) + query_bias).astype(jnp.bfloat16)
    self_pairs = (
        times_transpose(key_inputs, keys_weight) + jnp.concatenate([zero_bias, value_bias])
    ).astype(jnp.bfloat16)
    table = times_transpose(inputs, table_weight) + table_bias
    cross_pairs = (
        times_transpose(enc_all, pair_weight) + jnp.concatenate([zero_bias, pair_bias])
    ).astype(jnp.bfloat16)
    context_low, self_log = self_forward(query_low, self_pairs, table, spread, edge, self_mask)
    norm_one_in = input_values + times_transpose(context_low, out_weight) + out_bias
    stats_one = norm_stats(norm_one_in)
    hidden_one = (norm_one_in - stats_one[0]) * stats_one[1] * small_master[1] + small_master[4]
    one_low = hidden_one.astype(jnp.bfloat16)

    cross_query = (times_transpose(one_low, cross_weight) + cross_bias).astype(jnp.bfloat16)
    cross_low, cross_log = cross_forward(cross_query, cross_pairs, cross_mask)
    norm_two_in = hidden_one + times_transpose(cross_low, back_weight) + back_bias
    stats_two = norm_stats(norm_two_in)
    hidden_two = (norm_two_in - stats_two[0]) * stats_two[1] * small_master[2] + small_master[5]
    two_low = hidden_two.astype(jnp.bfloat16)

    active, slope = gelu_and_slope(times_transpose(two_low, up_weight) + up_bias)
    active_low = active.astype(jnp.bfloat16)
    slope_low = slope.astype(jnp.bfloat16)
    norm_three_in = hidden_two + matmul(active_low, down_weight) + small_master[0]
    stats_three = norm_stats(norm_three_in)
    final_rows = (
        (norm_three_in - stats_three[0]) * stats_three[1] * small_master[3] + small_master[6]
    ).astype(jnp.bfloat16)

    cotangent = jnp.concatenate([main_cotangent, pred_cotangent], axis=0).astype(jnp.float32)
    sum_three, gain_three, shift_three = norm_back(
        norm_three_in, stats_three, small_master[3], cotangent
    )
    ffn_grad = sum_three.astype(jnp.bfloat16)
    slab = proj_rows.shape[0] // 4
    down_sum = Scatter(column_sums(active_low, ffn_grad), range(4), dp_count)
    down_sum.step()
    pre_grad = (times_transpose(ffn_grad, down_weight) * slope_low.astype(jnp.float32)).astype(
        jnp.bfloat16
    )
    pre_grad = after(pre_grad, down_sum)
    up_cut = 3 * slab - cross_start - 4 * D
    slab_three = Scatter(column_sums(pre_grad[:, up_cut:], two_low), range(3, 4), dp_count)
    up_rows = column_sums(pre_grad[:, :up_cut], two_low)
    down_sum.step()
    slab_three.step()
    two_grad = sum_three + matmul(pre_grad, up_weight)
    two_grad = after(two_grad, slab_three)

    sum_two, gain_two, shift_two = norm_back(norm_two_in, stats_two, small_master[2], two_grad)
    branch_grad = sum_two.astype(jnp.bfloat16)
    cross_low_grad = matmul(branch_grad, back_weight).astype(jnp.bfloat16)
    cross_low_grad = after(cross_low_grad, down_sum)
    down_sum.step()
    slab_three.step()
    back_rows = column_sums(branch_grad, cross_low)
    cquery_grad, ckey_grad, cvalue_grad = cross_backward(
        cross_query, cross_pairs, cross_mask, cross_log, cross_low_grad
    )
    cquery_grad = after(cquery_grad, down_sum, slab_three)
    down_sum.step()
    slab_three.step()
    ckey_rows = column_sums(ckey_grad, enc_all)
    cvalue_rows = column_sums(cvalue_grad, enc_all)
    enc_grad = pair_sum(matmul(ckey_grad, pair_weight[:D]) + matmul(cvalue_grad, pair_weight[D:]))
    one_grad = sum_two + matmul(cquery_grad, cross_weight)

    sum_one, gain_one, shift_one = norm_back(norm_one_in, stats_one, small_master[1], one_grad)
    attn_grad = sum_one.astype(jnp.bfloat16)
    out_rows = column_sums(attn_grad, context_low)
    out_cut = slab - 3 * D
    ckey_cut = 2 * slab - cross_start - D
    slab_middle = Scatter(
        jnp.concatenate(
            [
                out_rows[out_cut:],
                jnp.zeros((rel_width, D), jnp.bfloat16),
                column_sums(cquery_grad, one_low),
                ckey_rows,
                cvalue_rows,
                back_rows,
                up_rows,
            ]
        ),
        range(1, 3),
        dp_count,
    )
    slab_middle.step()
    context_grad = matmul(attn_grad, out_weight).astype(jnp.bfloat16)
    context_grad = after(context_grad, slab_middle, slab_three)
    slab_middle.step()
    slab_three.step()
    query_grad, key_grad, value_grad, table_wide = self_backward(
        query_low, self_pairs, table, spread, edge, turn, self_mask, self_log, context_grad
    )
    table_wide = after(table_wide, slab_middle, slab_three)
    slab_middle.step()
    table_grad = table_wide.astype(jnp.bfloat16)
    table_sum = Scatter(column_sums(table_grad, inputs), range(4), dp_count, 1)
    slab_zero = Scatter(
        jnp.concatenate(
            [
                column_sums(query_grad, inputs),
                column_sums(key_grad, key_inputs),
                column_sums(value_grad, key_inputs),
                out_rows[:out_cut],
            ]
        ),
        range(0, 1),
        dp_count,
    )
    device = lax.axis_index("dp") * 2 + lax.axis_index("stream")
    table_total = (
        to_all(table_sum.finish().astype(jnp.bfloat16), devices)
        .reshape(HEADS, BUCKETS, D)
        .transpose(1, 0, 2)
        .reshape(rel_width, D)
        .astype(jnp.float32)
    )
    shard = proj_rows.shape[0] // devices
    table_part = lax.dynamic_slice_in_dim(
        jnp.pad(table_total, ((shard, shard), (0, 0))),
        jnp.clip((device + 1) * shard - 4 * D, 0, rel_width + shard),
        shard,
    )
    pair_input_grad = matmul(key_grad, keys_weight[:D]) + matmul(value_grad, keys_weight[D:])
    query_input_grad = (
        sum_one + matmul(query_grad, query_weight) + matmul(table_grad, table_weight)
    )
    main_grad = query_input_grad[:half_rows] + pair_sum(pair_input_grad[:group_rows])
    pred_grad = query_input_grad[half_rows:] + pair_input_grad[group_rows:]

    def row_sum(rows):
        return jnp.sum(rows, axis=0, dtype=jnp.float32)

    bias_parts = jnp.concatenate(
        [
            row_sum(query_grad),
            row_sum(value_grad),
            row_sum(attn_grad),
            row_sum(table_grad).reshape(HEADS, BUCKETS).T.reshape(rel_width),
            row_sum(cquery_grad),
            row_sum(cvalue_grad),
            row_sum(branch_grad),
            row_sum(pre_grad),
        ]
    )
    small_parts = jnp.concatenate(
        [row_sum(ffn_grad), gain_one, gain_two, gain_three, shift_one, shift_two, shift_three]
    )
    vector_parts = jnp.concatenate(
        [bias_parts.reshape(devices, -1), small_parts.reshape(devices, -1)], axis=1
    )
    vector_sum = jnp.sum(
        lax.all_to_all(vector_parts, ("dp", "stream"), 0, 0, tiled=True), axis=0
    )
    bias_len = bias_master.shape[0]
    bias_grad = vector_sum[:bias_len]
    small_grad = to_all(vector_sum[bias_len:], devices).reshape(small_master.shape)

    outer = place_on(("dp", dp_count // 4, 4))
    proj_sum = jnp.where(
        outer == 0,
        slab_zero.finish(),
        jnp.where(outer == 3, slab_three.finish(), slab_middle.finish()),
    )
    proj_grad = (proj_sum + table_part).T
    down_grad = down_sum.finish()
    return (
        final_rows[:half_rows],
        final_rows[half_rows:],
        main_grad.astype(jnp.bfloat16),
        pred_grad.astype(jnp.bfloat16),
        enc_grad.astype(jnp.bfloat16),
        *adam_step(proj_master, proj_first, proj_second, proj_grad, RATE_MATRIX, WEIGHT_DECAY),
        *adam_step(bias_master, bias_first, bias_second, bias_grad, RATE_VECTOR, 0.0),
        *adam_step(down_master, down_first, down_second, down_grad, RATE_MATRIX, WEIGHT_DECAY),
        *adam_step(small_master, small_first, small_second, small_grad, RATE_SMALL, 0.0),
    )


def solution(mesh):
    rows = P(("dp", "stream"), None)
    columns = P(None, ("dp", "stream"))
    vector = P(("dp", "stream"))
    masters = (columns,) * 3 + (vector,) * 3 + (rows,) * 3 + (P(),) * 3
    return jax.shard_map(
        partial(local, mesh.shape["dp"]),
        mesh=mesh,
        in_specs=(rows, rows, rows, P("dp", None), rows, rows) + masters,
        out_specs=(rows,) * 5 + masters,
        check_vma=False,
    )
```

```python
from functools import partial
import math

import jax
import jax.numpy as jnp
from jax import lax
from jax.experimental import pallas as pl
from jax.experimental.pallas import tpu as pltpu
from jax.sharding import PartitionSpec as P

D = 1024
HEADS = 16
BUCKETS = 32
STEP = 10
HEAD_DIM = 64
LANES = 128
CHUNK = 128
SCORE_SCALE = HEAD_DIM**-0.5

NORM_EPS = 1e-05
BETA_FIRST = 0.9
BETA_SECOND = 0.999
ADAM_EPS = 1e-08
RATE_MATRIX = 0.04
RATE_VECTOR = 0.15
RATE_SMALL = 0.5
WEIGHT_DECAY = 0.01
MASKED = -1e30
MESH = pl.DeviceIdType.MESH


def bucket_edges():
    return [int(math.ceil(16.0 * 8.0 ** (step_index / 16.0))) for step_index in range(1, 16)]


def bucket_of(distance):
    counted = jnp.zeros_like(distance)
    for threshold in bucket_edges():
        counted = counted + (distance >= threshold).astype(jnp.int32)
    return jnp.where(distance < 16, distance, 16 + counted)


def doc_ids(lengths, length_total):
    doc_ends = jnp.cumsum(lengths)
    places = jnp.arange(length_total, dtype=jnp.int32)
    return jnp.sum((places[:, None] >= doc_ends[None, :]).astype(jnp.int32), axis=1)


def matmul(left_side, right_side):
    return jnp.dot(left_side, right_side, preferred_element_type=jnp.float32)


def outer_sum(left_side, right_side):
    return lax.dot_general(
        left_side, right_side, (((0,), (0,)), ((), ())), preferred_element_type=jnp.float32
    )


def times_transpose(left_side, right_side):
    return lax.dot_general(
        left_side, right_side, (((1,), (1,)), ((), ())), preferred_element_type=jnp.float32
    )


def norm_stats(hidden):
    mean = jnp.mean(hidden, axis=-1, keepdims=True)
    centre = hidden - mean
    spread = jnp.mean(centre * centre, axis=-1, keepdims=True)
    return mean, lax.rsqrt(spread + NORM_EPS)


def norm_back(hidden, stats, gain_row, grad):
    mean, inverse = stats
    normed = (hidden - mean) * inverse
    scaled = grad * gain_row
    first = jnp.mean(scaled, axis=-1, keepdims=True)
    second = jnp.mean(scaled * normed, axis=-1, keepdims=True)
    hidden_grad = (scaled - first - normed * second) * inverse
    return hidden_grad, jnp.sum(grad * normed, axis=0), jnp.sum(grad, axis=0)


def gelu_and_slope(values):
    size = jnp.abs(values) * (0.5**0.5)
    place = 1.0 / (1.0 + 0.5 * size)
    fit = 0.17087277
    for coefficient in (
        -0.82215223,
        1.48851587,
        -1.13520398,
        0.27886807,
        -0.18628806,
        0.09678418,
        0.37409196,
        1.00002368,
        -1.26551223,
    ):
        fit = fit * place + coefficient
    bell = jnp.exp(-size * size)
    tail = 0.5 * place * bell * jnp.exp(fit)
    below = jnp.where(values >= 0.0, 1.0 - tail, tail)
    return values * below, below + values * bell * (1.0 / math.sqrt(2.0 * math.pi))


def dot_rows(left_side, right_side):
    return lax.dot_general(
        left_side, right_side, (((1,), (1,)), ((), ())), preferred_element_type=jnp.float32
    )


def lookup(table, index):
    return jnp.take_along_axis(table, index, axis=1, mode="promise_in_bounds")


def wide(column):
    return jnp.broadcast_to(column, (column.shape[0], LANES))


def tiled(block, key_count):
    return jnp.concatenate([block] * (key_count // LANES), axis=1)


def row_blocks(main_count, key_count, size):
    blocks = [(at, min(size, main_count - at), key_count) for at in range(0, main_count, size)]
    step = min(size, LANES)
    for at in range(0, key_count, step):
        seen = min(key_count, (at + step + LANES - 1) // LANES * LANES)
        blocks.append((main_count + at, min(step, key_count - at), seen))
    return blocks


def bias_of(near_bias, far_bias, edge, row_count, key_count):
    lane = lax.broadcasted_iota(jnp.int32, (row_count, LANES), 1)
    return jnp.concatenate(
        [
            jnp.where(lane + at > edge, near_bias, far_bias)
            for at in range(0, key_count, LANES)
        ],
        axis=1,
    )


def both_halves(block, head):
    lane = lax.broadcasted_iota(jnp.int32, block.shape, 1)
    turned = pltpu.roll(block, HEAD_DIM, 1)
    return jnp.where((lane < HEAD_DIM) == (head == 0), block, turned)


def self_forward_kernel(
    query_ref,
    key_ref,
    value_ref,
    own_key_ref,
    own_value_ref,
    table_ref,
    spread_ref,
    edge_ref,
    mask_ref,
    context_ref,
    log_ref,
    score_ref,
    prob_ref,
    near_ref,
    far_ref,
):
    rows, key_count = mask_ref.shape
    main_count = rows - key_count
    parity = lax.rem(pl.program_id(0), 2)
    groups = row_blocks(main_count, key_count, 512)
    chunks = row_blocks(main_count, key_count, CHUNK)
    for head in range(2):
        at = head * HEAD_DIM
        head_lanes = slice(at, at + HEAD_DIM)
        first = (parity * 2 + head) * BUCKETS
        query = query_ref[:, head_lanes] * jnp.bfloat16(SCORE_SCALE)
        keys = key_ref[:, head_lanes]
        values = value_ref[:, head_lanes]
        own_keys = own_key_ref[:, head_lanes].astype(jnp.float32)
        own_values = own_value_ref[:, head_lanes].astype(jnp.float32)
        near_ref[head] = lookup(table_ref[...], spread_ref[...] + first)
        far_ref[head] = lookup(
            table_ref[...], jnp.full((rows, LANES), first + BUCKETS - 1, jnp.int32)
        )
        own_score = wide(
            jnp.sum(query[main_count:].astype(jnp.float32) * own_keys, axis=1, keepdims=True)
        ) + lookup(table_ref[main_count:, :], jnp.full((key_count, LANES), first, jnp.int32))
        for row, count, seen in groups:
            score_ref[head, row : row + count, 0:seen] = dot_rows(
                query[row : row + count], keys[0:seen]
            )
        tops = []
        for row, count, seen in chunks:
            part = slice(row, row + count)
            scores = (
                score_ref[head, part, 0:seen]
                + bias_of(near_ref[head, part], far_ref[head, part], edge_ref[part], count, seen)
                + mask_ref[part, 0:seen]
            )
            score_ref[head, part, 0:seen] = scores
            tops.append(wide(jnp.max(scores, axis=1, keepdims=True)))
        top = jnp.concatenate(tops, axis=0)
        top = jnp.concatenate(
            [top[:main_count], jnp.maximum(top[main_count:], own_score)], axis=0
        )
        own_weight = jnp.exp(own_score - top[main_count:])
        totals = []
        for row, count, seen in chunks:
            part = slice(row, row + count)
            weights = jnp.exp(score_ref[head, part, 0:seen] - tiled(top[part], seen))
            score_ref[head, part, 0:seen] = weights
            totals.append(wide(jnp.sum(weights, axis=1, keepdims=True)))
        total = jnp.concatenate(totals, axis=0)
        total = jnp.concatenate([total[:main_count], total[main_count:] + own_weight], axis=0)
        inverse = 1.0 / total
        log_ref[:, head_lanes] = (top + jnp.log(total))[:, 0:HEAD_DIM]
        own_prob = (own_weight * inverse[main_count:]).astype(jnp.bfloat16).astype(jnp.float32)
        for row, count, seen in chunks:
            part = slice(row, row + count)
            prob_ref[head, part, 0:seen] = (
                score_ref[head, part, 0:seen] * tiled(inverse[part], seen)
            ).astype(jnp.bfloat16)
        for row, count, seen in groups:
            part = slice(row, row + count)
            context = matmul(prob_ref[head, part, 0:seen], values[0:seen])
            if row >= main_count:
                own = slice(row - main_count, row - main_count + count)
                context = context + own_prob[own, 0:HEAD_DIM] * own_values[own]
            context_ref[part, head_lanes] = context.astype(jnp.bfloat16)


def self_backward_kernel(
    query_ref,
    key_ref,
    value_ref,
    own_key_ref,
    own_value_ref,
    table_ref,
    spread_ref,
    edge_ref,
    turn_ref,
    mask_ref,
    log_ref,
    context_ref,
    query_grad_ref,
    key_grad_ref,
    value_grad_ref,
    table_grad_ref,
    score_ref,
    prob_grad_ref,
    prob_ref,
    score_grad_ref,
    near_ref,
    far_ref,
    close_ref,
    rest_ref,
):
    rows, key_count = mask_ref.shape
    main_count = rows - key_count
    parity = lax.rem(pl.program_id(0), 2)
    groups = row_blocks(main_count, key_count, 512)
    chunks = row_blocks(main_count, key_count, CHUNK)
    bucket = bucket_of(lax.broadcasted_iota(jnp.int32, (LANES, LANES), 0))
    bucket_lane = lax.broadcasted_iota(jnp.int32, (LANES, LANES), 1)
    row_lane = lax.broadcasted_iota(jnp.int32, (rows, LANES), 1)
    table_total = jnp.zeros((rows, LANES), jnp.float32)
    own_total = jnp.zeros((key_count, LANES), jnp.float32)
    for head in range(2):
        at = head * HEAD_DIM
        head_lanes = slice(at, at + HEAD_DIM)
        first = (parity * 2 + head) * BUCKETS
        query = query_ref[:, head_lanes] * jnp.bfloat16(SCORE_SCALE)
        keys = key_ref[:, head_lanes]
        values = value_ref[:, head_lanes]
        context = context_ref[:, head_lanes]
        own_keys = own_key_ref[:, head_lanes].astype(jnp.float32)
        own_values = own_value_ref[:, head_lanes].astype(jnp.float32)
        own_query = query[main_count:].astype(jnp.float32)
        own_context = context[main_count:].astype(jnp.float32)
        near_ref[head] = lookup(table_ref[...], spread_ref[...] + first)
        far_ref[head] = lookup(
            table_ref[...], jnp.full((rows, LANES), first + BUCKETS - 1, jnp.int32)
        )
        own_score = wide(jnp.sum(own_query * own_keys, axis=1, keepdims=True)) + lookup(
            table_ref[main_count:, :], jnp.full((key_count, LANES), first, jnp.int32)
        )
        log_total = both_halves(log_ref[...], head)
        own_prob = jnp.exp(own_score - log_total[main_count:])
        own_prob_grad = wide(jnp.sum(own_context * own_values, axis=1, keepdims=True))
        value_grad_ref[key_count:, head_lanes] = (
            own_prob[:, 0:HEAD_DIM].astype(jnp.bfloat16).astype(jnp.float32) * own_context
        ).astype(jnp.bfloat16)
        for row, count, seen in groups:
            part = slice(row, row + count)
            score_ref[head, part, 0:seen] = dot_rows(query[part], keys[0:seen])
            prob_grad_ref[head, part, 0:seen] = dot_rows(context[part], values[0:seen])
        row_dots = []
        for row, count, seen in chunks:
            part = slice(row, row + count)
            edge = edge_ref[part]
            bias = bias_of(near_ref[head, part], far_ref[head, part], edge, count, seen)
            probs = jnp.exp(
                score_ref[head, part, 0:seen]
                + bias
                + (mask_ref[part, 0:seen] - tiled(log_total[part], seen))
            )
            prob_grad = prob_grad_ref[head, part, 0:seen]
            row_dot = wide(jnp.sum(probs * prob_grad, axis=1, keepdims=True))
            if row >= main_count:
                own = slice(row - main_count, row - main_count + count)
                row_dot = row_dot + own_prob[own] * own_prob_grad[own]
                row_dots.append(row_dot)
            score_grad = (probs * (prob_grad - tiled(row_dot, seen))).astype(jnp.bfloat16)
            prob_ref[head, part, 0:seen] = probs.astype(jnp.bfloat16)
            score_grad_ref[head, part, 0:seen] = score_grad
            score_wide = score_grad.astype(jnp.float32)
            lane = lax.broadcasted_iota(jnp.int32, (count, LANES), 1)
            close = jnp.zeros((count, LANES), jnp.float32)
            whole = jnp.zeros((count, LANES), jnp.float32)
            for at_key in range(0, seen, LANES):
                block = score_wide[:, at_key : at_key + LANES]
                whole = whole + block
                close = close + jnp.where(lane + at_key > edge, block, 0.0)
            close_ref[head, part] = close
            rest_ref[head, part] = whole - close
        own_grad = (
            (own_prob * (own_prob_grad - jnp.concatenate(row_dots, axis=0)))
            .astype(jnp.bfloat16)
            .astype(jnp.float32)
        )
        key_grad_ref[key_count:, head_lanes] = (own_grad[:, 0:HEAD_DIM] * own_query).astype(
            jnp.bfloat16
        )
        turned = lookup(close_ref[head], turn_ref[...]).astype(jnp.bfloat16)
        table_total = table_total + matmul(
            turned, (bucket_lane == bucket + first).astype(jnp.bfloat16)
        )
        table_total = table_total + jnp.where(
            row_lane == first + BUCKETS - 1, jnp.sum(rest_ref[head], axis=1, keepdims=True), 0.0
        )
        own_total = own_total + jnp.where(row_lane[main_count:] == first, own_grad, 0.0)
        for row, count, seen in groups:
            part = slice(row, row + count)
            query_grad = matmul(score_grad_ref[head, part, 0:seen], keys[0:seen])
            if row >= main_count:
                own = slice(row - main_count, row - main_count + count)
                query_grad = query_grad + own_grad[own, 0:HEAD_DIM] * own_keys[own]
            query_grad_ref[part, head_lanes] = (query_grad * SCORE_SCALE).astype(jnp.bfloat16)
        for at_key in range(0, key_count, LANES):
            block = slice(at_key, at_key + LANES)
            later = slice(main_count + at_key, rows)
            key_grad_ref[block, head_lanes] = (
                outer_sum(score_grad_ref[head, 0:main_count, block], query[0:main_count])
                + outer_sum(score_grad_ref[head, later, block], query[later])
            ).astype(jnp.bfloat16)
            value_grad_ref[block, head_lanes] = (
                outer_sum(prob_ref[head, 0:main_count, block], context[0:main_count])
                + outer_sum(prob_ref[head, later, block], context[later])
            ).astype(jnp.bfloat16)
    table_total = jnp.concatenate(
        [table_total[:main_count], table_total[main_count:] + own_total], axis=0
    )

    @pl.when(parity == 0)
    def first_pair():
        table_grad_ref[...] = table_total

    @pl.when(parity == 1)
    def second_pair():
        table_grad_ref[...] += table_total


def cross_forward_kernel(
    query_ref, key_ref, value_ref, mask_ref, context_ref, log_ref, score_ref, prob_ref
):
    rows = mask_ref.shape[0]
    for head in range(2):
        at = head * HEAD_DIM
        head_lanes = slice(at, at + HEAD_DIM)
        query = query_ref[:, head_lanes] * jnp.bfloat16(SCORE_SCALE)
        score_ref[head] = dot_rows(query, key_ref[:, head_lanes])
        for row in range(0, rows, CHUNK):
            part = slice(row, min(row + CHUNK, rows))
            scores = score_ref[head, part] + mask_ref[part]
            top = jnp.max(scores, axis=1, keepdims=True)
            weights = jnp.exp(scores - top)
            total = jnp.sum(weights, axis=1, keepdims=True)
            prob_ref[head, part] = (weights * (1.0 / total)).astype(jnp.bfloat16)
            log_ref[part, head_lanes] = jnp.broadcast_to(
                top + jnp.log(total), (scores.shape[0], HEAD_DIM)
            )
        context_ref[:, head_lanes] = matmul(prob_ref[head], value_ref[:, head_lanes]).astype(
            jnp.bfloat16
        )


def cross_backward_kernel(
    query_ref,
    key_ref,
    value_ref,
    mask_ref,
    log_ref,
    context_ref,
    query_grad_ref,
    key_grad_ref,
    value_grad_ref,
    score_ref,
    prob_grad_ref,
    prob_ref,
    score_grad_ref,
):
    rows = mask_ref.shape[0]
    for head in range(2):
        at = head * HEAD_DIM
        head_lanes = slice(at, at + HEAD_DIM)
        query = query_ref[:, head_lanes] * jnp.bfloat16(SCORE_SCALE)
        keys = key_ref[:, head_lanes]
        context = context_ref[:, head_lanes]
        score_ref[head] = dot_rows(query, keys)
        prob_grad_ref[head] = dot_rows(context, value_ref[:, head_lanes])
        for row in range(0, rows, CHUNK):
            part = slice(row, min(row + CHUNK, rows))
            probs = jnp.exp(
                score_ref[head, part] + (mask_ref[part] - log_ref[part, at : at + 1])
            )
            prob_grad = prob_grad_ref[head, part]
            row_dot = jnp.sum(probs * prob_grad, axis=1, keepdims=True)
            prob_ref[head, part] = probs.astype(jnp.bfloat16)
            score_grad_ref[head, part] = (probs * (prob_grad - row_dot)).astype(jnp.bfloat16)
        query_grad_ref[:, head_lanes] = (matmul(score_grad_ref[head], keys) * SCORE_SCALE).astype(
            jnp.bfloat16
        )
        key_grad_ref[:, head_lanes] = outer_sum(score_grad_ref[head], query).astype(jnp.bfloat16)
        value_grad_ref[:, head_lanes] = outer_sum(prob_ref[head], context).astype(jnp.bfloat16)


def pair_block(row_count, row_block=0, first_pair=0):
    return pl.BlockSpec((row_count, LANES), lambda pair: (row_block, first_pair + pair))


def whole_block(shape):
    return pl.BlockSpec(shape, lambda pair: (0, 0))


def attention_call(kernel, name, in_specs, out_specs, out_shape, scratch, arrays, flops, passes):
    moved = sum(array.size * array.dtype.itemsize for array in arrays)
    moved += sum(math.prod(shape.shape) * shape.dtype.itemsize for shape in out_shape)
    return pl.pallas_call(
        kernel,
        grid=(HEADS // 2,),
        in_specs=in_specs,
        out_specs=out_specs,
        out_shape=out_shape,
        scratch_shapes=scratch,
        compiler_params=pltpu.CompilerParams(vmem_limit_bytes=56 * 2**20),
        cost_estimate=pl.CostEstimate(flops=flops, bytes_accessed=moved, transcendentals=passes),
        name=name,
    )(*arrays)


def low_array(row_count):
    return jax.ShapeDtypeStruct((row_count, D), jnp.bfloat16)


def self_forward(query, pairs, table, spread, edge, mask):
    rows, keys = mask.shape
    width = D // LANES
    square = pltpu.VMEM((2, rows, keys), jnp.float32)
    narrow = pltpu.VMEM((2, rows, LANES), jnp.float32)
    return attention_call(
        self_forward_kernel,
        "self_forward",
        [
            pair_block(rows),
            pair_block(keys),
            pair_block(keys, 0, width),
            pair_block(keys, 1),
            pair_block(keys, 1, width),
            pl.BlockSpec((rows, LANES), lambda pair: (0, pair // 2)),
            whole_block((rows, LANES)),
            whole_block((rows, LANES)),
            whole_block((rows, keys)),
        ],
        [pair_block(rows), pair_block(rows)],
        [low_array(rows), jax.ShapeDtypeStruct((rows, D), jnp.float32)],
        [square, pltpu.VMEM((2, rows, keys), jnp.bfloat16), narrow, narrow],
        (query, pairs, pairs, pairs, pairs, table, spread, edge, mask),
        4 * rows * keys * D,
        rows * keys * HEADS,
    )


def self_backward(query, pairs, table, spread, edge, turn, mask, log_total, context_grad):
    rows, keys = mask.shape
    width = D // LANES
    square = pltpu.VMEM((2, rows, keys), jnp.float32)
    square_low = pltpu.VMEM((2, rows, keys), jnp.bfloat16)
    narrow = pltpu.VMEM((2, rows, LANES), jnp.float32)
    table_block = pl.BlockSpec((rows, LANES), lambda pair: (0, pair // 2))
    return attention_call(
        self_backward_kernel,
        "self_backward",
        [
            pair_block(rows),
            pair_block(keys),
            pair_block(keys, 0, width),
            pair_block(keys, 1),
            pair_block(keys, 1, width),
            table_block,
            whole_block((rows, LANES)),
            whole_block((rows, LANES)),
            whole_block((rows, LANES)),
            whole_block((rows, keys)),
            pair_block(rows),
            pair_block(rows),
        ],
        [pair_block(rows), pair_block(2 * keys), pair_block(2 * keys), table_block],
        [
            low_array(rows),
            low_array(2 * keys),
            low_array(2 * keys),
            jax.ShapeDtypeStruct(table.shape, jnp.float32),
        ],
        [square, square, square_low, square_low, narrow, narrow, narrow, narrow],
        (query, pairs, pairs, pairs, pairs, table, spread, edge, turn, mask, log_total, context_grad),
        10 * rows * keys * D,
        rows * keys * HEADS,
    )


def cross_forward(query, pairs, mask):
    rows, keys = mask.shape
    return attention_call(
        cross_forward_kernel,
        "cross_forward",
        [
            pair_block(rows),
            pair_block(keys),
            pair_block(keys, 0, D // LANES),
            whole_block((rows, keys)),
        ],
        [pair_block(rows), pair_block(rows)],
        [low_array(rows), jax.ShapeDtypeStruct((rows, D), jnp.float32)],
        [pltpu.VMEM((2, rows, keys), jnp.float32), pltpu.VMEM((2, rows, keys), jnp.bfloat16)],
        (query, pairs, pairs, mask),
        4 * rows * keys * D,
        rows * keys * HEADS,
    )


def cross_backward(query, pairs, mask, log_total, context_grad):
    rows, keys = mask.shape
    square = pltpu.VMEM((2, rows, keys), jnp.float32)
    square_low = pltpu.VMEM((2, rows, keys), jnp.bfloat16)
    return attention_call(
        cross_backward_kernel,
        "cross_backward",
        [
            pair_block(rows),
            pair_block(keys),
            pair_block(keys, 0, D // LANES),
            whole_block((rows, keys)),
            pair_block(rows),
            pair_block(rows),
        ],
        [pair_block(rows), pair_block(keys), pair_block(keys)],
        [low_array(rows), low_array(keys), low_array(keys)],
        [square, square, square_low, square_low],
        (query, pairs, pairs, mask, log_total, context_grad),
        10 * rows * keys * D,
        rows * keys * HEADS,
    )


def column_sums(left_side, right_side):
    return outer_sum(left_side, right_side).astype(jnp.bfloat16)


def inner_levels(dp_count):
    levels = [("dp", 1, 2), ("stream", 1, 2)]
    if dp_count == 64:
        return levels + [("dp", 2, 2), ("dp", 4, 4)]
    return levels + [("dp", 2, 2)]


def rotation(level, shift, dp_count):
    axis, stride, size = level
    total = 2 if axis == "stream" else dp_count
    pairs = []
    for source in range(total):
        place = (source // stride) % size
        target = source + ((place + shift) % size - place) * stride
        pairs.append((source, target))
    return pairs


def place_on(level):
    axis, stride, size = level
    return (lax.axis_index(axis) // stride) % size


def pick(stacked, index, dim):
    return lax.dynamic_index_in_dim(stacked, index, dim, keepdims=False)


def scatter_level(stacked, dim, level, dp_count, final_type):
    axis, stride, size = level
    mine = place_on(level)
    total = pick(stacked, mine, dim).astype(jnp.float32)
    for shift in range(1, size):
        sent = pick(stacked, (mine + shift) % size, dim)
        came = lax.ppermute(sent, axis, rotation(level, shift, dp_count))
        total = total + came.astype(jnp.float32)
    return total.astype(final_type)


class Scatter:
    def __init__(self, rows, outer_range, dp_count, parts=2):
        self.levels = inner_levels(dp_count)
        self.inner = self.levels[2:]
        self.outer_range = outer_range
        self.dp_count = dp_count
        self.parts = parts
        sizes = [size for axis, stride, size in reversed(self.inner)]
        self.block = rows.shape[0] // (len(outer_range) * math.prod(sizes) * 4)
        self.state = [
            rows.reshape([len(outer_range)] + sizes + [2, 2, self.block, rows.shape[1]])
        ]
        self.done = 0

    def step(self):
        inner_count = len(self.inner)
        if self.done == 0:
            stacked = scatter_level(
                self.state[0], 1 + inner_count, self.levels[0], self.dp_count, jnp.bfloat16
            )
            if self.parts == 1:
                self.state = [stacked]
            else:
                cut = (self.block // 2 + 15) // 16 * 16
                self.state = [stacked[..., :cut, :], stacked[..., cut:, :]]
            order = [self.levels[1]] + self.inner
            other = [self.inner[0], self.levels[1]] + self.inner[1:]
            self.orders = [order, other]
            self.names = [list(reversed(self.inner)) + [self.levels[1]] for part in range(2)]
        elif self.done <= inner_count + 1:
            for part in range(self.parts):
                level = self.orders[part][self.done - 1]
                dim = 1 + self.names[part].index(level)
                self.names[part].remove(level)
                self.state[part] = scatter_level(
                    self.state[part], dim, level, self.dp_count, jnp.bfloat16
                )
        else:
            self.state = [self.outer_step(piece) for piece in self.state]
        self.done += 1

    def outer_step(self, piece):
        level = ("dp", self.dp_count // 4, 4)
        mine = place_on(level)
        first, count = self.outer_range[0], len(self.outer_range)
        total = pick(piece, jnp.clip(mine - first, 0, count - 1), 0).astype(jnp.float32)
        for shift in range(1, 4):
            pairs = [
                pair
                for pair in rotation(level, shift, self.dp_count)
                if pair[1] // level[1] in self.outer_range
            ]
            target = jnp.clip((mine + shift) % 4 - first, 0, count - 1)
            total = total + lax.ppermute(pick(piece, target, 0), "dp", pairs).astype(jnp.float32)
        return total

    def finish(self):
        while self.done < len(self.inner) + 3:
            self.step()
        return jnp.concatenate(self.state)


def after(value, *scatters):
    states = [array for scatter in scatters for array in scatter.state]
    return lax.optimization_barrier((value, *states))[0]


def sum_shares(rows):
    part = lax.psum_scatter(rows, "dp", scatter_dimension=0, tiled=True)
    return lax.psum_scatter(part, "stream", scatter_dimension=0, tiled=True)


def to_last_quarter(share, devices, skipped):
    owners = devices // 4
    size = share.shape[0]
    block = (devices * size - skipped) // owners
    starts = [skipped + owner * block for owner in range(owners)]
    blocks = []
    for part in range((size - 1 + block + size - 1) // size):
        pairs = [
            (start // size + part, 3 * owners + owner)
            for owner, start in enumerate(starts)
            if start // size + part < devices
        ]
        blocks.append(lax.ppermute(share, ("dp", "stream"), pairs))
    mine = lax.axis_index("dp") * 2 + lax.axis_index("stream") - 3 * owners
    offset = jnp.mod(skipped + jnp.maximum(mine, 0) * block, size)
    return lax.dynamic_slice_in_dim(jnp.concatenate(blocks, axis=0), offset, block)


def to_all(part, count):
    shared = jnp.broadcast_to(part[None], (count, *part.shape))
    gathered = lax.all_to_all(shared, ("dp", "stream"), 0, 0, tiled=True)
    return gathered.reshape(-1, *part.shape[1:])


def swap_streams(rows):
    return lax.ppermute(rows, "stream", [(0, 1), (1, 0)])


def both_parts(rows):
    other = swap_streams(rows)
    leading = lax.axis_index("stream") == 0
    return jnp.concatenate(
        [jnp.where(leading, rows, other), jnp.where(leading, other, rows)], axis=0
    )


def pair_sum(rows):
    half = rows.shape[0] // 2
    stream = lax.axis_index("stream")
    sent = lax.dynamic_slice_in_dim(rows, (1 - stream) * half, half).astype(jnp.bfloat16)
    return lax.dynamic_slice_in_dim(rows, stream * half, half) + swap_streams(sent).astype(
        jnp.float32
    )


def adam_step(master, first_moment, second_moment, gradient, step_rate, step_decay):
    first_new = BETA_FIRST * first_moment + (1.0 - BETA_FIRST) * gradient
    second_new = BETA_SECOND * second_moment + (1.0 - BETA_SECOND) * gradient * gradient
    first_hat = first_new / (1.0 - BETA_FIRST**STEP)
    second_hat = second_new / (1.0 - BETA_SECOND**STEP)
    master_new = master - step_rate * (
        first_hat / (jnp.sqrt(second_hat) + ADAM_EPS) + step_decay * master
    )
    return (master_new, first_new, second_new)


def chunk_rows(block):
    tiles = block // 16
    counts = [(tiles + 3 - part) // 4 * 16 for part in range(4)]
    return [(sum(counts[:part]), counts[part]) for part in range(4)]


def add_rows(target_ref, source_ref, start, count):
    @pl.loop(0, count // 16)
    def tile_step(tile):
        rows = pl.ds(pl.multiple_of(start + tile * 16, 16), 16)
        target_ref[rows, :] = (
            target_ref[rows, :].astype(jnp.float32) + source_ref[rows, :].astype(jnp.float32)
        ).astype(jnp.bfloat16)


def sum_kernel(
    grad_ref,
    out_ref,
    held,
    core_in,
    first_in,
    second_in,
    along_in,
    load_sem,
    core_send,
    core_recv,
    first_send,
    first_recv,
    second_send,
    second_recv,
    along_send,
    along_recv,
):
    slabs, block = grad_ref.shape[0], grad_ref.shape[4]
    place, x = lax.axis_index("dp"), lax.axis_index("stream")
    c, y, z = place % 2, (place // 2) % 2, place // 4
    sibling, across, beside = (place + 1 - 2 * c, x), (place, 1 - x), (place + 2 - 4 * y, x)
    above, below = (place + 4, x), (place - 4, x)
    chunks = chunk_rows(block)

    barrier = pltpu.get_barrier_semaphore()
    for neighbour in (sibling, across, beside):
        pl.semaphore_signal(barrier, inc=1, device_id=neighbour, device_id_type=MESH)

    @pl.when(z < 3)
    def greet_above():
        pl.semaphore_signal(barrier, inc=1, device_id=above, device_id_type=MESH)

    @pl.when(z > 0)
    def greet_below():
        pl.semaphore_signal(barrier, inc=1, device_id=below, device_id_type=MESH)

    pl.semaphore_wait(barrier, 4 + z * (3 - z) // 2)

    def remote(source, target, send_sem, recv_sem, device):
        return pltpu.make_async_remote_copy(
            src_ref=source,
            dst_ref=target,
            send_sem=send_sem,
            recv_sem=recv_sem,
            device_id=device,
            device_id_type=MESH,
        )

    def core_copy(s, yy, xx):
        at = s * 4 + yy * 2 + xx
        return remote(
            grad_ref.at[s, yy, 1 - c, xx],
            core_in.at[s, yy, xx],
            core_send.at[at],
            core_recv.at[at],
            sibling,
        )

    def load(s, yy, xx):
        return pltpu.make_async_copy(
            grad_ref.at[s, yy, c, xx], held.at[s, yy, xx], load_sem.at[s * 4 + yy * 2 + xx]
        )

    def first_copy(s, chunk, other):
        rows = pl.ds(*chunks[chunk])
        at = (s * 4 + chunk) * 2 + other
        source = held.at[s, other, 1 - x, rows] if chunk < 2 else held.at[s, 1 - y, other, rows]
        return remote(
            source,
            first_in.at[s, other, rows],
            first_send.at[at],
            first_recv.at[at],
            across if chunk < 2 else beside,
        )

    def second_copy(s, chunk):
        rows = pl.ds(*chunks[chunk])
        source = held.at[s, 1 - y, x, rows] if chunk < 2 else held.at[s, y, 1 - x, rows]
        return remote(
            source,
            second_in.at[s, rows],
            second_send.at[s * 4 + chunk],
            second_recv.at[s * 4 + chunk],
            beside if chunk < 2 else across,
        )

    def along_copy(s, chunk, down):
        rows = pl.ds(*chunks[chunk])
        way = 0 if down else 1
        return remote(
            held.at[s, y, x, rows],
            along_in.at[way, s, rows],
            along_send.at[s * 4 + chunk],
            along_recv.at[way * slabs * 4 + s * 4 + chunk],
            below if down else above,
        )

    def core_stage(s, half):
        if half == 0:
            for yy in range(2):
                for xx in range(2):
                    load(s, yy, xx).wait()
                    core_copy(s, yy, xx).wait_recv()
        for chunk in (half, half + 2):
            for yy in range(2):
                for xx in range(2):
                    add_rows(held.at[s, yy, xx], core_in.at[s, yy, xx], *chunks[chunk])
            for other in range(2):
                first_copy(s, chunk, other).start()

    def first_stage(s, half):
        for chunk in (half, half + 2):
            for other in range(2):
                first_copy(s, chunk, other).wait_recv()
                kept = held.at[s, other, x] if chunk < 2 else held.at[s, y, other]
                add_rows(kept, first_in.at[s, other], *chunks[chunk])
            second_copy(s, chunk).start()

    def second_stage(s, half):
        for chunk in (half, half + 2):
            second_copy(s, chunk).wait_recv()
            add_rows(held.at[s, y, x], second_in.at[s], *chunks[chunk])
        along_stage(s, half, 0)

    def along_stage(s, half, hop):
        for down in (True, False):
            source = 3 - hop if down else hop
            if (source > s) if down else (source < s):

                @pl.when(z == source)
                def pass_on():
                    for chunk in (half, half + 2):
                        if hop > 0:
                            along_copy(s, chunk, down).wait_recv()
                            add_rows(
                                held.at[s, y, x], along_in.at[0 if down else 1, s], *chunks[chunk]
                            )
                        along_copy(s, chunk, down).start()

    def last_stage(s, half):
        @pl.when(z == s)
        def finish():
            for chunk in (half, half + 2):
                start, count = chunks[chunk]
                if s < 3:
                    along_copy(s, chunk, True).wait_recv()
                if s > 0:
                    along_copy(s, chunk, False).wait_recv()

                @pl.loop(0, count // 16)
                def tile_step(tile):
                    rows = pl.ds(pl.multiple_of(start + tile * 16, 16), 16)
                    total = held[s, y, x, rows, :].astype(jnp.float32)
                    if s < 3:
                        total = total + along_in[0, s, rows, :].astype(jnp.float32)
                    if s > 0:
                        total = total + along_in[1, s, rows, :].astype(jnp.float32)
                    out_ref[rows, :] = total

    for s in range(slabs):
        for yy in range(2):
            for xx in range(2):
                core_copy(s, yy, xx).start()
                load(s, yy, xx).start()
    out_ref[...] = jnp.zeros_like(out_ref)
    waves = [(s, half) for s in range(slabs) for half in range(2)]
    stages = [
        core_stage,
        first_stage,
        second_stage,
        partial(along_stage, hop=1),
        partial(along_stage, hop=2),
        last_stage,
    ]
    for step in range(len(waves) + len(stages) - 1):
        for late, stage in enumerate(stages):
            if 0 <= step - late < len(waves):
                stage(*waves[step - late])
    for s in range(slabs):
        for yy in range(2):
            for xx in range(2):
                core_copy(s, yy, xx).wait_send()
        for chunk in range(4):
            for other in range(2):
                first_copy(s, chunk, other).wait_send()
            second_copy(s, chunk).wait_send()

            @pl.when(z != s)
            def sent_along():
                along_copy(s, chunk, True).wait_send()


def sum_slabs(rows, slabs):
    block, width = rows.shape[0] // (slabs * 8), rows.shape[1]
    low = jnp.bfloat16
    dma = pltpu.SemaphoreType.DMA
    return pl.pallas_call(
        sum_kernel,
        out_shape=jax.ShapeDtypeStruct((block, width), jnp.float32),
        in_specs=[pl.BlockSpec(memory_space=pl.ANY)],
        out_specs=pl.BlockSpec(memory_space=pltpu.VMEM),
        scratch_shapes=[
            pltpu.VMEM((slabs, 2, 2, block, width), low),
            pltpu.VMEM((slabs, 2, 2, block, width), low),
            pltpu.VMEM((slabs, 2, block, width), low),
            pltpu.VMEM((slabs, block, width), low),
            pltpu.VMEM((2, slabs, block, width), low),
            dma((slabs * 4,)),
            dma((slabs * 4,)),
            dma((slabs * 4,)),
            dma((slabs * 8,)),
            dma((slabs * 8,)),
            dma((slabs * 4,)),
            dma((slabs * 4,)),
            dma((slabs * 4,)),
            dma((slabs * 8,)),
        ],
        compiler_params=pltpu.CompilerParams(
            collective_id=0, has_side_effects=True, vmem_limit_bytes=56 * 2**20
        ),
        cost_estimate=pl.CostEstimate(
            flops=rows.size, bytes_accessed=4 * rows.size, transcendentals=0
        ),
        name="sum_slabs",
    )(rows.reshape(slabs, 2, 2, 2, block, width))


def part_rows(block):
    tiles = block // 16
    one = (tiles * 2 + 4) // 5
    two = (tiles - one) * 3 // 5
    return [(0, one * 16), (one * 16, two * 16), ((one + two) * 16, (tiles - one - two) * 16)]


def digit(code, place):
    power = 1 + 9 * place + 81 * (place * (place - 1) // 2)
    power = power + 729 * (place * (place - 1) * (place - 2) // 6)
    return code // power % 10


def gather_kernel(shard_ref, out_ref, own_sem, send_sem, link_recv, core_recv):
    block = shard_ref.shape[0]
    place, x = lax.axis_index("dp"), lax.axis_index("stream")
    c, y, z = place % 2, (place // 2) % 2, place // 4
    up, down, across, beside, sibling = range(5)
    devices = [(place + 4, x), (place - 4, x), (place, 1 - x), (place + 2 - 4 * y, x)]
    devices.append((place + 1 - 2 * c, x))
    parts = part_rows(block)
    order = [z] + [digit(code, z) for code in (2101, 1322, 33)]

    barrier = pltpu.get_barrier_semaphore()
    for way in (across, beside, sibling):
        pl.semaphore_signal(barrier, inc=1, device_id=devices[way], device_id_type=MESH)

    @pl.when(z < 3)
    def greet_above():
        pl.semaphore_signal(barrier, inc=1, device_id=devices[up], device_id_type=MESH)

    @pl.when(z > 0)
    def greet_below():
        pl.semaphore_signal(barrier, inc=1, device_id=devices[down], device_id_type=MESH)

    own = pltpu.make_async_copy(shard_ref, out_ref.at[z, y, c, x], own_sem)
    own.start()
    pl.semaphore_wait(barrier, 4 + z * (3 - z) // 2)
    own.wait()

    def copy(way, zz, yy, xx, part, core=None):
        region = out_ref.at[zz, yy, c if core is None else core, xx, pl.ds(*parts[part])]
        at = ((zz * 2 + yy) * 2 + xx) * 3 + part
        return pltpu.make_async_remote_copy(
            src_ref=region,
            dst_ref=region,
            send_sem=send_sem.at[way * 48 + at],
            recv_sem=core_recv.at[at] if way == sibling else link_recv.at[at],
            device_id=devices[way],
            device_id_type=MESH,
        )

    def came(zz, yy, xx, part):
        copy(across, zz, yy, xx, part).wait_recv()

    def along(zz, yy, xx, part):
        @pl.when((z < 3) & (zz <= z))
        def send_up():
            copy(up, zz, yy, xx, part).start()

        @pl.when((z > 0) & (zz >= z))
        def send_down():
            copy(down, zz, yy, xx, part).start()

    def early(k):
        zz = order[k]
        for part in range(2):
            if k > 0:
                came(zz, y, x, part)
            along(zz, y, x, part)
            for way in (beside, across) if part == 0 else (across, beside):
                copy(way, zz, y, x, part).start()
            copy(sibling, zz, y, x, part).start()

    def middle(k):
        zz = order[k]
        came(zz, 1 - y, x, 0)
        copy(across, zz, 1 - y, x, 0).start()
        came(zz, y, 1 - x, 1)
        copy(beside, zz, y, 1 - x, 1).start()
        copy(sibling, zz, 1 - y, x, 0).start()
        copy(sibling, zz, y, 1 - x, 1).start()

    def late(k):
        zz = order[k]
        for yy, xx, part in ((y, 1 - x, 0), (1 - y, x, 1), (1 - y, 1 - x, 0), (1 - y, 1 - x, 1)):
            came(zz, yy, xx, part)
            copy(sibling, zz, yy, xx, part).start()

    def last_own(k):
        if k == 0:
            copy(across, z, y, x, 2).start()
            copy(beside, z, y, x, 2).start()
            regions = [(y, x)]
        elif k == 1:
            came(z, y, 1 - x, 2)
            copy(beside, z, y, 1 - x, 2).start()
            regions = [(y, 1 - x)]
        else:
            regions = [(1 - y, x), (1 - y, 1 - x)]
        for yy, xx in regions:
            if k == 2:
                came(z, yy, xx, 2)
            along(z, yy, xx, 2)
            copy(sibling, z, yy, xx, 2).start()

    def last(k):
        zz = order[k]
        for yy, xx in ((y, x), (y, 1 - x), (1 - y, x), (1 - y, 1 - x)):
            came(zz, yy, xx, 2)
            along(zz, yy, xx, 2)
            copy(sibling, zz, yy, xx, 2).start()

    for stage, k in (
        (early, 0),
        (last_own, 0),
        (last_own, 1),
        (early, 1),
        (middle, 0),
        (last_own, 2),
        (early, 2),
        (middle, 1),
        (early, 3),
        (last, 1),
        (late, 0),
        (middle, 2),
        (last, 2),
        (late, 1),
        (middle, 3),
        (last, 3),
        (late, 2),
        (late, 3),
    ):
        stage(k)

    for zz in range(4):
        for yy in range(2):
            for xx in range(2):
                for part in range(3):
                    copy(sibling, zz, yy, xx, part, 1 - c).wait_recv()
                    copy(sibling, zz, yy, xx, part).wait_send()

    def sent_along(zz, yy, xx, part):
        @pl.when((z < 3) & (zz <= z))
        def sent_up():
            copy(up, zz, yy, xx, part).wait_send()

        @pl.when((z > 0) & (zz >= z))
        def sent_down():
            copy(down, zz, yy, xx, part).wait_send()

    for zz in range(4):
        for part in range(2):
            sent_along(zz, y, x, part)
            copy(beside, zz, y, x, part).wait_send()
            copy(across, zz, y, x, part).wait_send()
        copy(across, zz, 1 - y, x, 0).wait_send()
        copy(beside, zz, y, 1 - x, 1).wait_send()
        for yy in range(2):
            for xx in range(2):
                sent_along(zz, yy, xx, 2)
    copy(across, z, y, x, 2).wait_send()
    copy(beside, z, y, x, 2).wait_send()
    copy(beside, z, y, 1 - x, 2).wait_send()


def gather_shards(shard):
    block, width = shard.shape
    dma = pltpu.SemaphoreType.DMA
    gathered = pl.pallas_call(
        gather_kernel,
        out_shape=jax.ShapeDtypeStruct((4, 2, 2, 2, block, width), shard.dtype),
        in_specs=[pl.BlockSpec(memory_space=pl.ANY)],
        out_specs=pl.BlockSpec(memory_space=pl.ANY),
        scratch_shapes=[dma, dma((240,)), dma((48,)), dma((48,))],
        compiler_params=pltpu.CompilerParams(
            collective_id=1, has_side_effects=True, vmem_limit_bytes=56 * 2**20
        ),
        cost_estimate=pl.CostEstimate(
            flops=0, bytes_accessed=64 * shard.size, transcendentals=0
        ),
        name="gather_shards",
    )(shard)
    return gathered.reshape(32 * block, width)


def local(
    dp_count,
    main_rows,
    pred_rows,
    enc_rows,
    doc_lengths,
    main_cotangent,
    pred_cotangent,
    proj_master,
    proj_first,
    proj_second,
    bias_master,
    bias_first,
    bias_second,
    down_master,
    down_first,
    down_second,
    small_master,
    small_first,
    small_second,
):
    devices = 2 * dp_count
    rel_width = BUCKETS * HEADS
    cross_start = 4 * D + rel_width
    half_rows = main_rows.shape[0]
    group_rows = pred_rows.shape[0]

    bias_wide = to_all(bias_master.astype(jnp.bfloat16), devices).astype(jnp.float32)
    proj_low = proj_master.astype(jnp.bfloat16).T
    if dp_count == 16:
        proj_rows = gather_shards(proj_low)
    else:
        proj_rows = lax.all_gather(proj_low, ("dp", "stream"), axis=0, tiled=True)
    down_low = lax.optimization_barrier((down_master.astype(jnp.bfloat16), proj_rows))[0]
    down_weight = lax.all_gather(down_low, ("dp", "stream"), axis=0, tiled=True)
    query_weight = proj_rows[0:D]
    keys_weight = proj_rows[D : 3 * D]
    out_weight = proj_rows[3 * D : 4 * D]
    table_weight = (
        proj_rows[4 * D : cross_start]
        .reshape(BUCKETS, HEADS, D)
        .transpose(1, 0, 2)
        .reshape(rel_width, D)
    )
    cross_weight = proj_rows[cross_start : cross_start + D]
    pair_weight = proj_rows[cross_start + D : cross_start + 3 * D]
    back_weight = proj_rows[cross_start + 3 * D : cross_start + 4 * D]
    up_weight = proj_rows[cross_start + 4 * D :]
    query_bias = bias_wide[0:D]
    value_bias = bias_wide[D : 2 * D]
    out_bias = bias_wide[2 * D : 3 * D]
    table_bias = bias_wide[3 * D : 3 * D + rel_width].reshape(BUCKETS, HEADS).T.reshape(rel_width)
    cross_bias = bias_wide[3 * D + rel_width : 4 * D + rel_width]
    pair_bias = bias_wide[4 * D + rel_width : 5 * D + rel_width]
    back_bias = bias_wide[5 * D + rel_width : 6 * D + rel_width]
    up_bias = bias_wide[6 * D + rel_width :]
    zero_bias = jnp.zeros((D,), jnp.float32)

    main_start = lax.axis_index("stream") * half_rows
    places = jnp.arange(group_rows, dtype=jnp.int32)
    group_docs = doc_ids(doc_lengths[0], group_rows)
    query_docs = jnp.concatenate(
        [lax.dynamic_slice_in_dim(group_docs, main_start, half_rows), group_docs]
    )
    query_places = jnp.concatenate([main_start + jnp.arange(half_rows, dtype=jnp.int32), places])
    main_flag = jnp.arange(half_rows + group_rows, dtype=jnp.int32) < half_rows
    same_doc = query_docs[:, None] == group_docs[None, :]
    distance = query_places[:, None] - places[None, :]
    allowed = same_doc & ((distance > 0) | (distance == 0) & main_flag[:, None])
    self_mask = jnp.where(allowed, 0.0, MASKED)
    cross_mask = jnp.where(same_doc, 0.0, MASKED)
    lane = jnp.arange(LANES, dtype=jnp.int32)
    turn = jnp.mod(query_places[:, None] - lane[None, :], LANES)
    spread = bucket_of(turn)
    edge = jnp.broadcast_to(query_places[:, None] - LANES, turn.shape)

    main_all = both_parts(main_rows)
    enc_all = both_parts(enc_rows)
    inputs = jnp.concatenate([main_rows, pred_rows], axis=0)
    key_inputs = jnp.concatenate([main_all, pred_rows], axis=0)
    input_values = inputs.astype(jnp.float32)
    query_low = (times_transpose(inputs, query_weight) + query_bias).astype(jnp.bfloat16)
    self_pairs = (
        times_transpose(key_inputs, keys_weight) + jnp.concatenate([zero_bias, value_bias])
    ).astype(jnp.bfloat16)
    table = times_transpose(inputs, table_weight) + table_bias
    cross_pairs = (
        times_transpose(enc_all, pair_weight) + jnp.concatenate([zero_bias, pair_bias])
    ).astype(jnp.bfloat16)
    context_low, self_log = self_forward(query_low, self_pairs, table, spread, edge, self_mask)
    norm_one_in = input_values + times_transpose(context_low, out_weight) + out_bias
    stats_one = norm_stats(norm_one_in)
    hidden_one = (norm_one_in - stats_one[0]) * stats_one[1] * small_master[1] + small_master[4]
    one_low = hidden_one.astype(jnp.bfloat16)

    cross_query = (times_transpose(one_low, cross_weight) + cross_bias).astype(jnp.bfloat16)
    cross_low, cross_log = cross_forward(cross_query, cross_pairs, cross_mask)
    norm_two_in = hidden_one + times_transpose(cross_low, back_weight) + back_bias
    stats_two = norm_stats(norm_two_in)
    hidden_two = (norm_two_in - stats_two[0]) * stats_two[1] * small_master[2] + small_master[5]
    two_low = hidden_two.astype(jnp.bfloat16)

    active, slope = gelu_and_slope(times_transpose(two_low, up_weight) + up_bias)
    active_low = active.astype(jnp.bfloat16)
    slope_low = slope.astype(jnp.bfloat16)
    norm_three_in = hidden_two + matmul(active_low, down_weight) + small_master[0]
    stats_three = norm_stats(norm_three_in)
    final_rows = (
        (norm_three_in - stats_three[0]) * stats_three[1] * small_master[3] + small_master[6]
    ).astype(jnp.bfloat16)

    cotangent = jnp.concatenate([main_cotangent, pred_cotangent], axis=0).astype(jnp.float32)
    sum_three, gain_three, shift_three = norm_back(
        norm_three_in, stats_three, small_master[3], cotangent
    )
    ffn_grad = sum_three.astype(jnp.bfloat16)
    slab = proj_rows.shape[0] // 4
    down_part = sum_shares(column_sums(active_low, ffn_grad))
    pre_grad = (times_transpose(ffn_grad, down_weight) * slope_low.astype(jnp.float32)).astype(
        jnp.bfloat16
    )
    up_cut = 3 * slab - cross_start - 4 * D
    up_part = sum_shares(column_sums(pre_grad, two_low))
    two_grad = sum_three + matmul(pre_grad, up_weight)

    sum_two, gain_two, shift_two = norm_back(norm_two_in, stats_two, small_master[2], two_grad)
    branch_grad = sum_two.astype(jnp.bfloat16)
    cross_low_grad = matmul(branch_grad, back_weight).astype(jnp.bfloat16)
    cquery_grad, ckey_grad, cvalue_grad = cross_backward(
        cross_query, cross_pairs, cross_mask, cross_log, cross_low_grad
    )
    enc_grad = pair_sum(matmul(ckey_grad, pair_weight[:D]) + matmul(cvalue_grad, pair_weight[D:]))
    one_grad = sum_two + matmul(cquery_grad, cross_weight)

    sum_one, gain_one, shift_one = norm_back(norm_one_in, stats_one, small_master[1], one_grad)
    attn_grad = sum_one.astype(jnp.bfloat16)
    context_grad = matmul(attn_grad, out_weight).astype(jnp.bfloat16)
    query_grad, key_grad, value_grad, table_wide = self_backward(
        query_low, self_pairs, table, spread, edge, turn, self_mask, self_log, context_grad
    )
    table_wide = lax.optimization_barrier((table_wide, down_part))[0]
    table_grad = table_wide.astype(jnp.bfloat16)
    table_rows = (
        column_sums(table_grad, inputs)
        .reshape(HEADS, BUCKETS, D)
        .transpose(1, 0, 2)
        .reshape(rel_width, D)
    )
    late_rows = jnp.concatenate(
        [
            column_sums(query_grad, inputs),
            column_sums(key_grad, key_inputs),
            column_sums(value_grad, key_inputs),
            column_sums(attn_grad, context_low),
            table_rows,
            column_sums(cquery_grad, one_low),
            column_sums(ckey_grad, enc_all),
            column_sums(cvalue_grad, enc_all),
            column_sums(branch_grad, cross_low),
            column_sums(pre_grad[:, :up_cut], two_low),
        ]
    )
    pair_input_grad = matmul(key_grad, keys_weight[:D]) + matmul(value_grad, keys_weight[D:])
    query_input_grad = (
        sum_one + matmul(query_grad, query_weight) + matmul(table_grad, table_weight)
    )
    main_grad = query_input_grad[:half_rows] + pair_sum(pair_input_grad[:group_rows])
    pred_grad = query_input_grad[half_rows:] + pair_input_grad[group_rows:]

    def row_sum(rows):
        return jnp.sum(rows, axis=0, dtype=jnp.float32)

    bias_parts = jnp.concatenate(
        [
            row_sum(query_grad),
            row_sum(value_grad),
            row_sum(attn_grad),
            row_sum(table_grad).reshape(HEADS, BUCKETS).T.reshape(rel_width),
            row_sum(cquery_grad),
            row_sum(cvalue_grad),
            row_sum(branch_grad),
            row_sum(pre_grad),
        ]
    )
    small_parts = jnp.concatenate(
        [row_sum(ffn_grad), gain_one, gain_two, gain_three, shift_one, shift_two, shift_three]
    )
    vector_parts = jnp.concatenate(
        [bias_parts.reshape(devices, -1), small_parts.reshape(devices, -1)], axis=1
    )
    vector_sum = jnp.sum(
        lax.all_to_all(vector_parts, ("dp", "stream"), 0, 0, tiled=True), axis=0
    )
    bias_len = bias_master.shape[0]
    bias_grad = vector_sum[:bias_len]
    small_grad = to_all(vector_sum[bias_len:], devices).reshape(small_master.shape)

    slab_three = to_last_quarter(up_part, devices, up_cut)
    late_rows = lax.optimization_barrier((late_rows, vector_sum, slab_three))[0]
    if dp_count == 16:
        late_sum = sum_slabs(late_rows, 3)
    else:
        late_sum = Scatter(late_rows, range(3), dp_count).finish()
    outer = place_on(("dp", dp_count // 4, 4))
    proj_grad = jnp.where(outer == 3, slab_three.astype(jnp.float32), late_sum).T
    down_grad = down_part.astype(jnp.float32)
    return (
        final_rows[:half_rows],
        final_rows[half_rows:],
        main_grad.astype(jnp.bfloat16),
        pred_grad.astype(jnp.bfloat16),
        enc_grad.astype(jnp.bfloat16),
        *adam_step(proj_master, proj_first, proj_second, proj_grad, RATE_MATRIX, WEIGHT_DECAY),
        *adam_step(bias_master, bias_first, bias_second, bias_grad, RATE_VECTOR, 0.0),
        *adam_step(down_master, down_first, down_second, down_grad, RATE_MATRIX, WEIGHT_DECAY),
        *adam_step(small_master, small_first, small_second, small_grad, RATE_SMALL, 0.0),
    )


def solution(mesh):
    rows = P(("dp", "stream"), None)
    columns = P(None, ("dp", "stream"))
    vector = P(("dp", "stream"))
    masters = (columns,) * 3 + (vector,) * 3 + (rows,) * 3 + (P(),) * 3
    return jax.shard_map(
        partial(local, mesh.shape["dp"]),
        mesh=mesh,
        in_specs=(rows, rows, rows, P("dp", None), rows, rows) + masters,
        out_specs=(rows,) * 5 + masters,
        check_vma=False,
    )
```

```python
from functools import partial
import math

import jax
import jax.numpy as jnp
from jax import lax
from jax.experimental import pallas as pl
from jax.experimental.pallas import tpu as pltpu
from jax.sharding import PartitionSpec as P

D = 1024
HEADS = 16
BUCKETS = 32
STEP = 10
HEAD_DIM = 64
LANES = 128
CHUNK = 128
SCORE_SCALE = HEAD_DIM**-0.5

NORM_EPS = 1e-05
BETA_FIRST = 0.9
BETA_SECOND = 0.999
ADAM_EPS = 1e-08
RATE_MATRIX = 0.04
RATE_VECTOR = 0.15
RATE_SMALL = 0.5
WEIGHT_DECAY = 0.01
MASKED = -1e30
FFN_TILE = 1024
FFN_PART = 256
MESH = pl.DeviceIdType.MESH


def bucket_edges():
    return [int(math.ceil(16.0 * 8.0 ** (step_index / 16.0))) for step_index in range(1, 16)]


def bucket_of(distance):
    counted = jnp.zeros_like(distance)
    for threshold in bucket_edges():
        counted = counted + (distance >= threshold).astype(jnp.int32)
    return jnp.where(distance < 16, distance, 16 + counted)


def doc_ids(lengths, length_total):
    doc_ends = jnp.cumsum(lengths)
    places = jnp.arange(length_total, dtype=jnp.int32)
    return jnp.sum((places[:, None] >= doc_ends[None, :]).astype(jnp.int32), axis=1)


def matmul(left_side, right_side):
    return jnp.dot(left_side, right_side, preferred_element_type=jnp.float32)


def outer_sum(left_side, right_side):
    return lax.dot_general(
        left_side, right_side, (((0,), (0,)), ((), ())), preferred_element_type=jnp.float32
    )


def times_transpose(left_side, right_side):
    return lax.dot_general(
        left_side, right_side, (((1,), (1,)), ((), ())), preferred_element_type=jnp.float32
    )


def norm_stats(hidden):
    mean = jnp.mean(hidden, axis=-1, keepdims=True)
    centre = hidden - mean
    spread = jnp.mean(centre * centre, axis=-1, keepdims=True)
    return mean, lax.rsqrt(spread + NORM_EPS)


def norm_back(hidden, stats, gain_row, grad):
    mean, inverse = stats
    normed = (hidden - mean) * inverse
    scaled = grad * gain_row
    first = jnp.mean(scaled, axis=-1, keepdims=True)
    second = jnp.mean(scaled * normed, axis=-1, keepdims=True)
    hidden_grad = (scaled - first - normed * second) * inverse
    return hidden_grad, jnp.sum(grad * normed, axis=0), jnp.sum(grad, axis=0)


def gelu_and_slope(values):
    size = jnp.abs(values) * (0.5**0.5)
    place = 1.0 / (1.0 + 0.3275911 * size)
    fit = 1.061405429
    for coefficient in (-1.453152027, 1.421413741, -0.284496736, 0.254829592):
        fit = fit * place + coefficient
    bell = jnp.exp(-size * size)
    tail = (0.5 * place) * (fit * bell)
    below = jnp.where(values >= 0.0, 1.0 - tail, tail)
    return values * below, below + values * bell * (1.0 / math.sqrt(2.0 * math.pi))


def dot_rows(left_side, right_side):
    return lax.dot_general(
        left_side, right_side, (((1,), (1,)), ((), ())), preferred_element_type=jnp.float32
    )


def lookup(table, index):
    return jnp.take_along_axis(table, index, axis=1, mode="promise_in_bounds")


def wide(column):
    return jnp.broadcast_to(column, (column.shape[0], LANES))


def tiled(block, key_count):
    return jnp.concatenate([block] * (key_count // LANES), axis=1)


def row_blocks(main_count, key_count, size):
    blocks = [(at, min(size, main_count - at), key_count) for at in range(0, main_count, size)]
    step = min(size, LANES)
    for at in range(0, key_count, step):
        seen = min(key_count, (at + step + LANES - 1) // LANES * LANES)
        blocks.append((main_count + at, min(step, key_count - at), seen))
    return blocks


def bias_of(near_bias, far_bias, edge, row_count, key_count):
    lane = lax.broadcasted_iota(jnp.int32, (row_count, LANES), 1)
    return jnp.concatenate(
        [
            jnp.where(lane + at > edge, near_bias, far_bias)
            for at in range(0, key_count, LANES)
        ],
        axis=1,
    )


def both_halves(block, head):
    lane = lax.broadcasted_iota(jnp.int32, block.shape, 1)
    turned = pltpu.roll(block, HEAD_DIM, 1)
    return jnp.where((lane < HEAD_DIM) == (head == 0), block, turned)


def self_forward_kernel(
    query_ref,
    key_ref,
    value_ref,
    own_key_ref,
    own_value_ref,
    table_ref,
    spread_ref,
    edge_ref,
    mask_ref,
    context_ref,
    log_ref,
    score_ref,
    prob_ref,
    near_ref,
    far_ref,
):
    rows, key_count = mask_ref.shape
    main_count = rows - key_count
    parity = lax.rem(pl.program_id(0), 2)
    groups = row_blocks(main_count, key_count, 512)
    chunks = row_blocks(main_count, key_count, CHUNK)
    for head in range(2):
        at = head * HEAD_DIM
        head_lanes = slice(at, at + HEAD_DIM)
        first = (parity * 2 + head) * BUCKETS
        query = query_ref[:, head_lanes] * jnp.bfloat16(SCORE_SCALE)
        keys = key_ref[:, head_lanes]
        values = value_ref[:, head_lanes]
        own_keys = own_key_ref[:, head_lanes].astype(jnp.float32)
        own_values = own_value_ref[:, head_lanes].astype(jnp.float32)
        near_ref[head] = lookup(table_ref[...], spread_ref[...] + first)
        far_ref[head] = lookup(
            table_ref[...], jnp.full((rows, LANES), first + BUCKETS - 1, jnp.int32)
        )
        own_score = wide(
            jnp.sum(query[main_count:].astype(jnp.float32) * own_keys, axis=1, keepdims=True)
        ) + lookup(table_ref[main_count:, :], jnp.full((key_count, LANES), first, jnp.int32))
        for row, count, seen in groups:
            score_ref[head, row : row + count, 0:seen] = dot_rows(
                query[row : row + count], keys[0:seen]
            )
        tops = []
        for row, count, seen in chunks:
            part = slice(row, row + count)
            scores = (
                score_ref[head, part, 0:seen]
                + bias_of(near_ref[head, part], far_ref[head, part], edge_ref[part], count, seen)
                + mask_ref[part, 0:seen]
            )
            score_ref[head, part, 0:seen] = scores
            tops.append(wide(jnp.max(scores, axis=1, keepdims=True)))
        top = jnp.concatenate(tops, axis=0)
        top = jnp.concatenate(
            [top[:main_count], jnp.maximum(top[main_count:], own_score)], axis=0
        )
        own_weight = jnp.exp(own_score - top[main_count:])
        totals = []
        for row, count, seen in chunks:
            part = slice(row, row + count)
            weights = jnp.exp(score_ref[head, part, 0:seen] - tiled(top[part], seen))
            score_ref[head, part, 0:seen] = weights
            totals.append(wide(jnp.sum(weights, axis=1, keepdims=True)))
        total = jnp.concatenate(totals, axis=0)
        total = jnp.concatenate([total[:main_count], total[main_count:] + own_weight], axis=0)
        inverse = 1.0 / total
        log_ref[:, head_lanes] = (top + jnp.log(total))[:, 0:HEAD_DIM]
        own_prob = (own_weight * inverse[main_count:]).astype(jnp.bfloat16).astype(jnp.float32)
        for row, count, seen in chunks:
            part = slice(row, row + count)
            prob_ref[head, part, 0:seen] = (
                score_ref[head, part, 0:seen] * tiled(inverse[part], seen)
            ).astype(jnp.bfloat16)
        for row, count, seen in groups:
            part = slice(row, row + count)
            context = matmul(prob_ref[head, part, 0:seen], values[0:seen])
            if row >= main_count:
                own = slice(row - main_count, row - main_count + count)
                context = context + own_prob[own, 0:HEAD_DIM] * own_values[own]
            context_ref[part, head_lanes] = context.astype(jnp.bfloat16)


def self_backward_kernel(
    query_ref,
    key_ref,
    value_ref,
    own_key_ref,
    own_value_ref,
    table_ref,
    spread_ref,
    edge_ref,
    turn_ref,
    mask_ref,
    log_ref,
    context_ref,
    query_grad_ref,
    key_grad_ref,
    value_grad_ref,
    table_grad_ref,
    score_ref,
    prob_grad_ref,
    prob_ref,
    score_grad_ref,
    near_ref,
    far_ref,
    close_ref,
    rest_ref,
):
    rows, key_count = mask_ref.shape
    main_count = rows - key_count
    parity = lax.rem(pl.program_id(0), 2)
    groups = row_blocks(main_count, key_count, 512)
    chunks = row_blocks(main_count, key_count, CHUNK)
    bucket = bucket_of(lax.broadcasted_iota(jnp.int32, (LANES, LANES), 0))
    bucket_lane = lax.broadcasted_iota(jnp.int32, (LANES, LANES), 1)
    row_lane = lax.broadcasted_iota(jnp.int32, (rows, LANES), 1)
    table_total = jnp.zeros((rows, LANES), jnp.float32)
    own_total = jnp.zeros((key_count, LANES), jnp.float32)
    for head in range(2):
        at = head * HEAD_DIM
        head_lanes = slice(at, at + HEAD_DIM)
        first = (parity * 2 + head) * BUCKETS
        query = query_ref[:, head_lanes] * jnp.bfloat16(SCORE_SCALE)
        keys = key_ref[:, head_lanes]
        values = value_ref[:, head_lanes]
        context = context_ref[:, head_lanes]
        own_keys = own_key_ref[:, head_lanes].astype(jnp.float32)
        own_values = own_value_ref[:, head_lanes].astype(jnp.float32)
        own_query = query[main_count:].astype(jnp.float32)
        own_context = context[main_count:].astype(jnp.float32)
        near_ref[head] = lookup(table_ref[...], spread_ref[...] + first)
        far_ref[head] = lookup(
            table_ref[...], jnp.full((rows, LANES), first + BUCKETS - 1, jnp.int32)
        )
        own_score = wide(jnp.sum(own_query * own_keys, axis=1, keepdims=True)) + lookup(
            table_ref[main_count:, :], jnp.full((key_count, LANES), first, jnp.int32)
        )
        log_total = both_halves(log_ref[...], head)
        own_prob = jnp.exp(own_score - log_total[main_count:])
        own_prob_grad = wide(jnp.sum(own_context * own_values, axis=1, keepdims=True))
        value_grad_ref[key_count:, head_lanes] = (
            own_prob[:, 0:HEAD_DIM].astype(jnp.bfloat16).astype(jnp.float32) * own_context
        ).astype(jnp.bfloat16)
        for row, count, seen in groups:
            part = slice(row, row + count)
            score_ref[head, part, 0:seen] = dot_rows(query[part], keys[0:seen])
            prob_grad_ref[head, part, 0:seen] = dot_rows(context[part], values[0:seen])
        row_dots = []
        for row, count, seen in chunks:
            part = slice(row, row + count)
            edge = edge_ref[part]
            bias = bias_of(near_ref[head, part], far_ref[head, part], edge, count, seen)
            probs = jnp.exp(
                score_ref[head, part, 0:seen]
                + bias
                + (mask_ref[part, 0:seen] - tiled(log_total[part], seen))
            )
            prob_grad = prob_grad_ref[head, part, 0:seen]
            row_dot = wide(jnp.sum(probs * prob_grad, axis=1, keepdims=True))
            if row >= main_count:
                own = slice(row - main_count, row - main_count + count)
                row_dot = row_dot + own_prob[own] * own_prob_grad[own]
                row_dots.append(row_dot)
            score_grad = (probs * (prob_grad - tiled(row_dot, seen))).astype(jnp.bfloat16)
            prob_ref[head, part, 0:seen] = probs.astype(jnp.bfloat16)
            score_grad_ref[head, part, 0:seen] = score_grad
            score_wide = score_grad.astype(jnp.float32)
            lane = lax.broadcasted_iota(jnp.int32, (count, LANES), 1)
            close = jnp.zeros((count, LANES), jnp.float32)
            whole = jnp.zeros((count, LANES), jnp.float32)
            for at_key in range(0, seen, LANES):
                block = score_wide[:, at_key : at_key + LANES]
                whole = whole + block
                close = close + jnp.where(lane + at_key > edge, block, 0.0)
            close_ref[head, part] = close
            rest_ref[head, part] = whole - close
        own_grad = (
            (own_prob * (own_prob_grad - jnp.concatenate(row_dots, axis=0)))
            .astype(jnp.bfloat16)
            .astype(jnp.float32)
        )
        key_grad_ref[key_count:, head_lanes] = (own_grad[:, 0:HEAD_DIM] * own_query).astype(
            jnp.bfloat16
        )
        turned = lookup(close_ref[head], turn_ref[...]).astype(jnp.bfloat16)
        table_total = table_total + matmul(
            turned, (bucket_lane == bucket + first).astype(jnp.bfloat16)
        )
        table_total = table_total + jnp.where(
            row_lane == first + BUCKETS - 1, jnp.sum(rest_ref[head], axis=1, keepdims=True), 0.0
        )
        own_total = own_total + jnp.where(row_lane[main_count:] == first, own_grad, 0.0)
        for row, count, seen in groups:
            part = slice(row, row + count)
            query_grad = matmul(score_grad_ref[head, part, 0:seen], keys[0:seen])
            if row >= main_count:
                own = slice(row - main_count, row - main_count + count)
                query_grad = query_grad + own_grad[own, 0:HEAD_DIM] * own_keys[own]
            query_grad_ref[part, head_lanes] = (query_grad * SCORE_SCALE).astype(jnp.bfloat16)
        for at_key in range(0, key_count, LANES):
            block = slice(at_key, at_key + LANES)
            later = slice(main_count + at_key, rows)
            key_grad_ref[block, head_lanes] = (
                outer_sum(score_grad_ref[head, 0:main_count, block], query[0:main_count])
                + outer_sum(score_grad_ref[head, later, block], query[later])
            ).astype(jnp.bfloat16)
            value_grad_ref[block, head_lanes] = (
                outer_sum(prob_ref[head, 0:main_count, block], context[0:main_count])
                + outer_sum(prob_ref[head, later, block], context[later])
            ).astype(jnp.bfloat16)
    table_total = jnp.concatenate(
        [table_total[:main_count], table_total[main_count:] + own_total], axis=0
    )

    @pl.when(parity == 0)
    def first_pair():
        table_grad_ref[...] = table_total

    @pl.when(parity == 1)
    def second_pair():
        table_grad_ref[...] += table_total


def cross_forward_kernel(
    query_ref, key_ref, value_ref, mask_ref, context_ref, log_ref, score_ref, prob_ref
):
    rows = mask_ref.shape[0]
    for head in range(2):
        at = head * HEAD_DIM
        head_lanes = slice(at, at + HEAD_DIM)
        query = query_ref[:, head_lanes] * jnp.bfloat16(SCORE_SCALE)
        score_ref[head] = dot_rows(query, key_ref[:, head_lanes])
        for row in range(0, rows, CHUNK):
            part = slice(row, min(row + CHUNK, rows))
            scores = score_ref[head, part] + mask_ref[part]
            top = jnp.max(scores, axis=1, keepdims=True)
            weights = jnp.exp(scores - top)
            total = jnp.sum(weights, axis=1, keepdims=True)
            prob_ref[head, part] = (weights * (1.0 / total)).astype(jnp.bfloat16)
            log_ref[part, head_lanes] = jnp.broadcast_to(
                top + jnp.log(total), (scores.shape[0], HEAD_DIM)
            )
        context_ref[:, head_lanes] = matmul(prob_ref[head], value_ref[:, head_lanes]).astype(
            jnp.bfloat16
        )


def cross_backward_kernel(
    query_ref,
    key_ref,
    value_ref,
    mask_ref,
    log_ref,
    context_ref,
    query_grad_ref,
    key_grad_ref,
    value_grad_ref,
    score_ref,
    prob_grad_ref,
    prob_ref,
    score_grad_ref,
):
    rows = mask_ref.shape[0]
    for head in range(2):
        at = head * HEAD_DIM
        head_lanes = slice(at, at + HEAD_DIM)
        query = query_ref[:, head_lanes] * jnp.bfloat16(SCORE_SCALE)
        keys = key_ref[:, head_lanes]
        context = context_ref[:, head_lanes]
        score_ref[head] = dot_rows(query, keys)
        prob_grad_ref[head] = dot_rows(context, value_ref[:, head_lanes])
        for row in range(0, rows, CHUNK):
            part = slice(row, min(row + CHUNK, rows))
            probs = jnp.exp(
                score_ref[head, part] + (mask_ref[part] - log_ref[part, at : at + 1])
            )
            prob_grad = prob_grad_ref[head, part]
            row_dot = jnp.sum(probs * prob_grad, axis=1, keepdims=True)
            prob_ref[head, part] = probs.astype(jnp.bfloat16)
            score_grad_ref[head, part] = (probs * (prob_grad - row_dot)).astype(jnp.bfloat16)
        query_grad_ref[:, head_lanes] = (matmul(score_grad_ref[head], keys) * SCORE_SCALE).astype(
            jnp.bfloat16
        )
        key_grad_ref[:, head_lanes] = outer_sum(score_grad_ref[head], query).astype(jnp.bfloat16)
        value_grad_ref[:, head_lanes] = outer_sum(prob_ref[head], context).astype(jnp.bfloat16)


def pair_block(row_count, row_block=0, first_pair=0):
    return pl.BlockSpec((row_count, LANES), lambda pair: (row_block, first_pair + pair))


def whole_block(shape):
    return pl.BlockSpec(shape, lambda pair: (0, 0))


def attention_call(kernel, name, in_specs, out_specs, out_shape, scratch, arrays, flops, passes):
    moved = sum(array.size * array.dtype.itemsize for array in arrays)
    moved += sum(math.prod(shape.shape) * shape.dtype.itemsize for shape in out_shape)
    return pl.pallas_call(
        kernel,
        grid=(HEADS // 2,),
        in_specs=in_specs,
        out_specs=out_specs,
        out_shape=out_shape,
        scratch_shapes=scratch,
        compiler_params=pltpu.CompilerParams(vmem_limit_bytes=56 * 2**20),
        cost_estimate=pl.CostEstimate(flops=flops, bytes_accessed=moved, transcendentals=passes),
        name=name,
    )(*arrays)


def low_array(row_count):
    return jax.ShapeDtypeStruct((row_count, D), jnp.bfloat16)


def self_forward(query, pairs, table, spread, edge, mask):
    rows, keys = mask.shape
    width = D // LANES
    square = pltpu.VMEM((2, rows, keys), jnp.float32)
    narrow = pltpu.VMEM((2, rows, LANES), jnp.float32)
    return attention_call(
        self_forward_kernel,
        "self_forward",
        [
            pair_block(rows),
            pair_block(keys),
            pair_block(keys, 0, width),
            pair_block(keys, 1),
            pair_block(keys, 1, width),
            pl.BlockSpec((rows, LANES), lambda pair: (0, pair // 2)),
            whole_block((rows, LANES)),
            whole_block((rows, LANES)),
            whole_block((rows, keys)),
        ],
        [pair_block(rows), pair_block(rows)],
        [low_array(rows), jax.ShapeDtypeStruct((rows, D), jnp.float32)],
        [square, pltpu.VMEM((2, rows, keys), jnp.bfloat16), narrow, narrow],
        (query, pairs, pairs, pairs, pairs, table, spread, edge, mask),
        4 * rows * keys * D,
        rows * keys * HEADS,
    )


def self_backward(query, pairs, table, spread, edge, turn, mask, log_total, context_grad):
    rows, keys = mask.shape
    width = D // LANES
    square = pltpu.VMEM((2, rows, keys), jnp.float32)
    square_low = pltpu.VMEM((2, rows, keys), jnp.bfloat16)
    narrow = pltpu.VMEM((2, rows, LANES), jnp.float32)
    table_block = pl.BlockSpec((rows, LANES), lambda pair: (0, pair // 2))
    return attention_call(
        self_backward_kernel,
        "self_backward",
        [
            pair_block(rows),
            pair_block(keys),
            pair_block(keys, 0, width),
            pair_block(keys, 1),
            pair_block(keys, 1, width),
            table_block,
            whole_block((rows, LANES)),
            whole_block((rows, LANES)),
            whole_block((rows, LANES)),
            whole_block((rows, keys)),
            pair_block(rows),
            pair_block(rows),
        ],
        [pair_block(rows), pair_block(2 * keys), pair_block(2 * keys), table_block],
        [
            low_array(rows),
            low_array(2 * keys),
            low_array(2 * keys),
            jax.ShapeDtypeStruct(table.shape, jnp.float32),
        ],
        [square, square, square_low, square_low, narrow, narrow, narrow, narrow],
        (query, pairs, pairs, pairs, pairs, table, spread, edge, turn, mask, log_total, context_grad),
        10 * rows * keys * D,
        rows * keys * HEADS,
    )


def cross_forward(query, pairs, mask):
    rows, keys = mask.shape
    return attention_call(
        cross_forward_kernel,
        "cross_forward",
        [
            pair_block(rows),
            pair_block(keys),
            pair_block(keys, 0, D // LANES),
            whole_block((rows, keys)),
        ],
        [pair_block(rows), pair_block(rows)],
        [low_array(rows), jax.ShapeDtypeStruct((rows, D), jnp.float32)],
        [pltpu.VMEM((2, rows, keys), jnp.float32), pltpu.VMEM((2, rows, keys), jnp.bfloat16)],
        (query, pairs, pairs, mask),
        4 * rows * keys * D,
        rows * keys * HEADS,
    )


def cross_backward(query, pairs, mask, log_total, context_grad):
    rows, keys = mask.shape
    square = pltpu.VMEM((2, rows, keys), jnp.float32)
    square_low = pltpu.VMEM((2, rows, keys), jnp.bfloat16)
    return attention_call(
        cross_backward_kernel,
        "cross_backward",
        [
            pair_block(rows),
            pair_block(keys),
            pair_block(keys, 0, D // LANES),
            whole_block((rows, keys)),
            pair_block(rows),
            pair_block(rows),
        ],
        [pair_block(rows), pair_block(keys), pair_block(keys)],
        [low_array(rows), low_array(keys), low_array(keys)],
        [square, square, square_low, square_low],
        (query, pairs, pairs, mask, log_total, context_grad),
        10 * rows * keys * D,
        rows * keys * HEADS,
    )


def column_sums(left_side, right_side):
    return outer_sum(left_side, right_side).astype(jnp.bfloat16)


def inner_levels(dp_count):
    levels = [("dp", 1, 2), ("stream", 1, 2)]
    if dp_count == 64:
        return levels + [("dp", 2, 2), ("dp", 4, 4)]
    return levels + [("dp", 2, 2)]


def rotation(level, shift, dp_count):
    axis, stride, size = level
    total = 2 if axis == "stream" else dp_count
    pairs = []
    for source in range(total):
        place = (source // stride) % size
        target = source + ((place + shift) % size - place) * stride
        pairs.append((source, target))
    return pairs


def place_on(level):
    axis, stride, size = level
    return (lax.axis_index(axis) // stride) % size


def pick(stacked, index, dim):
    return lax.dynamic_index_in_dim(stacked, index, dim, keepdims=False)


def scatter_level(stacked, dim, level, dp_count, final_type):
    axis, stride, size = level
    mine = place_on(level)
    total = pick(stacked, mine, dim).astype(jnp.float32)
    for shift in range(1, size):
        sent = pick(stacked, (mine + shift) % size, dim)
        came = lax.ppermute(sent, axis, rotation(level, shift, dp_count))
        total = total + came.astype(jnp.float32)
    return total.astype(final_type)


class Scatter:
    def __init__(self, rows, outer_range, dp_count, parts=2):
        self.levels = inner_levels(dp_count)
        self.inner = self.levels[2:]
        self.outer_range = outer_range
        self.dp_count = dp_count
        self.parts = parts
        sizes = [size for axis, stride, size in reversed(self.inner)]
        self.block = rows.shape[0] // (len(outer_range) * math.prod(sizes) * 4)
        self.state = [
            rows.reshape([len(outer_range)] + sizes + [2, 2, self.block, rows.shape[1]])
        ]
        self.done = 0

    def step(self):
        inner_count = len(self.inner)
        if self.done == 0:
            stacked = scatter_level(
                self.state[0], 1 + inner_count, self.levels[0], self.dp_count, jnp.bfloat16
            )
            if self.parts == 1:
                self.state = [stacked]
            else:
                cut = (self.block // 2 + 15) // 16 * 16
                self.state = [stacked[..., :cut, :], stacked[..., cut:, :]]
            order = [self.levels[1]] + self.inner
            other = [self.inner[0], self.levels[1]] + self.inner[1:]
            self.orders = [order, other]
            self.names = [list(reversed(self.inner)) + [self.levels[1]] for part in range(2)]
        elif self.done <= inner_count + 1:
            for part in range(self.parts):
                level = self.orders[part][self.done - 1]
                dim = 1 + self.names[part].index(level)
                self.names[part].remove(level)
                self.state[part] = scatter_level(
                    self.state[part], dim, level, self.dp_count, jnp.bfloat16
                )
        else:
            self.state = [self.outer_step(piece) for piece in self.state]
        self.done += 1

    def outer_step(self, piece):
        level = ("dp", self.dp_count // 4, 4)
        mine = place_on(level)
        first, count = self.outer_range[0], len(self.outer_range)
        total = pick(piece, jnp.clip(mine - first, 0, count - 1), 0).astype(jnp.float32)
        for shift in range(1, 4):
            pairs = [
                pair
                for pair in rotation(level, shift, self.dp_count)
                if pair[1] // level[1] in self.outer_range
            ]
            target = jnp.clip((mine + shift) % 4 - first, 0, count - 1)
            total = total + lax.ppermute(pick(piece, target, 0), "dp", pairs).astype(jnp.float32)
        return total

    def finish(self):
        while self.done < len(self.inner) + 3:
            self.step()
        return jnp.concatenate(self.state)


def after(value, *scatters):
    states = [array for scatter in scatters for array in scatter.state]
    return lax.optimization_barrier((value, *states))[0]


def sum_shares(rows):
    part = lax.psum_scatter(rows, "dp", scatter_dimension=0, tiled=True)
    return lax.psum_scatter(part, "stream", scatter_dimension=0, tiled=True)


def to_last_quarter(share, devices, skipped):
    owners = devices // 4
    size = share.shape[0]
    block = (devices * size - skipped) // owners
    starts = [skipped + owner * block for owner in range(owners)]
    blocks = []
    for part in range((size - 1 + block + size - 1) // size):
        pairs = [
            (start // size + part, 3 * owners + owner)
            for owner, start in enumerate(starts)
            if start // size + part < devices
        ]
        blocks.append(lax.ppermute(share, ("dp", "stream"), pairs))
    mine = lax.axis_index("dp") * 2 + lax.axis_index("stream") - 3 * owners
    offset = jnp.mod(skipped + jnp.maximum(mine, 0) * block, size)
    return lax.dynamic_slice_in_dim(jnp.concatenate(blocks, axis=0), offset, block)


def to_all(part, count):
    shared = jnp.broadcast_to(part[None], (count, *part.shape))
    gathered = lax.all_to_all(shared, ("dp", "stream"), 0, 0, tiled=True)
    return gathered.reshape(-1, *part.shape[1:])


def swap_streams(rows):
    return lax.ppermute(rows, "stream", [(0, 1), (1, 0)])


def both_parts(rows):
    other = swap_streams(rows)
    leading = lax.axis_index("stream") == 0
    return jnp.concatenate(
        [jnp.where(leading, rows, other), jnp.where(leading, other, rows)], axis=0
    )


def pair_sum(rows):
    half = rows.shape[0] // 2
    stream = lax.axis_index("stream")
    sent = lax.dynamic_slice_in_dim(rows, (1 - stream) * half, half).astype(jnp.bfloat16)
    return lax.dynamic_slice_in_dim(rows, stream * half, half) + swap_streams(sent).astype(
        jnp.float32
    )


def adam_step(master, first_moment, second_moment, gradient, step_rate, step_decay):
    first_new = BETA_FIRST * first_moment + (1.0 - BETA_FIRST) * gradient
    second_new = BETA_SECOND * second_moment + (1.0 - BETA_SECOND) * gradient * gradient
    first_hat = first_new / (1.0 - BETA_FIRST**STEP)
    second_hat = second_new / (1.0 - BETA_SECOND**STEP)
    master_new = master - step_rate * (
        first_hat / (jnp.sqrt(second_hat) + ADAM_EPS) + step_decay * master
    )
    return (master_new, first_new, second_new)


def chunk_rows(block):
    tiles = block // 16
    counts = [(tiles + 3 - part) // 4 * 16 for part in range(4)]
    return [(sum(counts[:part]), counts[part]) for part in range(4)]


def add_rows(target_ref, source_ref, start, count):
    @pl.loop(0, count // 16)
    def tile_step(tile):
        rows = pl.ds(pl.multiple_of(start + tile * 16, 16), 16)
        target_ref[rows, :] = (
            target_ref[rows, :].astype(jnp.float32) + source_ref[rows, :].astype(jnp.float32)
        ).astype(jnp.bfloat16)


def sum_kernel(
    grad_ref,
    out_ref,
    held,
    core_in,
    first_in,
    second_in,
    along_in,
    load_sem,
    core_send,
    core_recv,
    first_send,
    first_recv,
    second_send,
    second_recv,
    along_send,
    along_recv,
):
    slabs, block = grad_ref.shape[0], grad_ref.shape[4]
    place, x = lax.axis_index("dp"), lax.axis_index("stream")
    c, y, z = place % 2, (place // 2) % 2, place // 4
    sibling, across, beside = (place + 1 - 2 * c, x), (place, 1 - x), (place + 2 - 4 * y, x)
    above, below = (place + 4, x), (place - 4, x)
    chunks = chunk_rows(block)

    barrier = pltpu.get_barrier_semaphore()
    for neighbour in (sibling, across, beside):
        pl.semaphore_signal(barrier, inc=1, device_id=neighbour, device_id_type=MESH)

    @pl.when(z < 3)
    def greet_above():
        pl.semaphore_signal(barrier, inc=1, device_id=above, device_id_type=MESH)

    @pl.when(z > 0)
    def greet_below():
        pl.semaphore_signal(barrier, inc=1, device_id=below, device_id_type=MESH)

    pl.semaphore_wait(barrier, 4 + z * (3 - z) // 2)

    def remote(source, target, send_sem, recv_sem, device):
        return pltpu.make_async_remote_copy(
            src_ref=source,
            dst_ref=target,
            send_sem=send_sem,
            recv_sem=recv_sem,
            device_id=device,
            device_id_type=MESH,
        )

    def core_copy(s, yy, xx):
        at = s * 4 + yy * 2 + xx
        return remote(
            grad_ref.at[s, yy, 1 - c, xx],
            core_in.at[s, yy, xx],
            core_send.at[at],
            core_recv.at[at],
            sibling,
        )

    def load(s, yy, xx):
        return pltpu.make_async_copy(
            grad_ref.at[s, yy, c, xx], held.at[s, yy, xx], load_sem.at[s * 4 + yy * 2 + xx]
        )

    def first_copy(s, chunk, other):
        rows = pl.ds(*chunks[chunk])
        at = (s * 4 + chunk) * 2 + other
        source = held.at[s, other, 1 - x, rows] if chunk < 2 else held.at[s, 1 - y, other, rows]
        return remote(
            source,
            first_in.at[s, other, rows],
            first_send.at[at],
            first_recv.at[at],
            across if chunk < 2 else beside,
        )

    def second_copy(s, chunk):
        rows = pl.ds(*chunks[chunk])
        source = held.at[s, 1 - y, x, rows] if chunk < 2 else held.at[s, y, 1 - x, rows]
        return remote(
            source,
            second_in.at[s, rows],
            second_send.at[s * 4 + chunk],
            second_recv.at[s * 4 + chunk],
            beside if chunk < 2 else across,
        )

    def along_copy(s, chunk, down):
        rows = pl.ds(*chunks[chunk])
        way = 0 if down else 1
        return remote(
            held.at[s, y, x, rows],
            along_in.at[way, s, rows],
            along_send.at[s * 4 + chunk],
            along_recv.at[way * slabs * 4 + s * 4 + chunk],
            below if down else above,
        )

    def core_stage(s, half):
        if half == 0:
            for yy in range(2):
                for xx in range(2):
                    load(s, yy, xx).wait()
                    core_copy(s, yy, xx).wait_recv()
        for chunk in (half, half + 2):
            for yy in range(2):
                for xx in range(2):
                    add_rows(held.at[s, yy, xx], core_in.at[s, yy, xx], *chunks[chunk])
            for other in range(2):
                first_copy(s, chunk, other).start()

    def first_stage(s, half):
        for chunk in (half, half + 2):
            for other in range(2):
                first_copy(s, chunk, other).wait_recv()
                kept = held.at[s, other, x] if chunk < 2 else held.at[s, y, other]
                add_rows(kept, first_in.at[s, other], *chunks[chunk])
            second_copy(s, chunk).start()

    def second_stage(s, half):
        for chunk in (half, half + 2):
            second_copy(s, chunk).wait_recv()
            add_rows(held.at[s, y, x], second_in.at[s], *chunks[chunk])
        along_stage(s, half, 0)

    def along_stage(s, half, hop):
        for down in (True, False):
            source = 3 - hop if down else hop
            if (source > s) if down else (source < s):

                @pl.when(z == source)
                def pass_on():
                    for chunk in (half, half + 2):
                        if hop > 0:
                            along_copy(s, chunk, down).wait_recv()
                            add_rows(
                                held.at[s, y, x], along_in.at[0 if down else 1, s], *chunks[chunk]
                            )
                        along_copy(s, chunk, down).start()

    def last_stage(s, half):
        @pl.when(z == s)
        def finish():
            for chunk in (half, half + 2):
                start, count = chunks[chunk]
                if s < 3:
                    along_copy(s, chunk, True).wait_recv()
                if s > 0:
                    along_copy(s, chunk, False).wait_recv()

                @pl.loop(0, count // 16)
                def tile_step(tile):
                    rows = pl.ds(pl.multiple_of(start + tile * 16, 16), 16)
                    total = held[s, y, x, rows, :].astype(jnp.float32)
                    if s < 3:
                        total = total + along_in[0, s, rows, :].astype(jnp.float32)
                    if s > 0:
                        total = total + along_in[1, s, rows, :].astype(jnp.float32)
                    out_ref[rows, :] = total

    for s in range(slabs):
        for yy in range(2):
            for xx in range(2):
                core_copy(s, yy, xx).start()
                load(s, yy, xx).start()
    out_ref[...] = jnp.zeros_like(out_ref)
    waves = [(s, half) for s in range(slabs) for half in range(2)]
    stages = [
        core_stage,
        first_stage,
        second_stage,
        partial(along_stage, hop=1),
        partial(along_stage, hop=2),
        last_stage,
    ]
    for step in range(len(waves) + len(stages) - 1):
        for late, stage in enumerate(stages):
            if 0 <= step - late < len(waves):
                stage(*waves[step - late])
    for s in range(slabs):
        for yy in range(2):
            for xx in range(2):
                core_copy(s, yy, xx).wait_send()
        for chunk in range(4):
            for other in range(2):
                first_copy(s, chunk, other).wait_send()
            second_copy(s, chunk).wait_send()

            @pl.when(z != s)
            def sent_along():
                along_copy(s, chunk, True).wait_send()


def sum_slabs(rows, slabs):
    block, width = rows.shape[0] // (slabs * 8), rows.shape[1]
    low = jnp.bfloat16
    dma = pltpu.SemaphoreType.DMA
    return pl.pallas_call(
        sum_kernel,
        out_shape=jax.ShapeDtypeStruct((block, width), jnp.float32),
        in_specs=[pl.BlockSpec(memory_space=pl.ANY)],
        out_specs=pl.BlockSpec(memory_space=pltpu.VMEM),
        scratch_shapes=[
            pltpu.VMEM((slabs, 2, 2, block, width), low),
            pltpu.VMEM((slabs, 2, 2, block, width), low),
            pltpu.VMEM((slabs, 2, block, width), low),
            pltpu.VMEM((slabs, block, width), low),
            pltpu.VMEM((2, slabs, block, width), low),
            dma((slabs * 4,)),
            dma((slabs * 4,)),
            dma((slabs * 4,)),
            dma((slabs * 8,)),
            dma((slabs * 8,)),
            dma((slabs * 4,)),
            dma((slabs * 4,)),
            dma((slabs * 4,)),
            dma((slabs * 8,)),
        ],
        compiler_params=pltpu.CompilerParams(
            collective_id=0, has_side_effects=True, vmem_limit_bytes=56 * 2**20
        ),
        cost_estimate=pl.CostEstimate(
            flops=rows.size, bytes_accessed=4 * rows.size, transcendentals=0
        ),
        name="sum_slabs",
    )(rows.reshape(slabs, 2, 2, 2, block, width))


def part_rows(block):
    tiles = block // 16
    one = (tiles * 2 + 4) // 5
    two = (tiles - one) * 3 // 5
    return [(0, one * 16), (one * 16, two * 16), ((one + two) * 16, (tiles - one - two) * 16)]


def digit(code, place):
    power = 1 + 9 * place + 81 * (place * (place - 1) // 2)
    power = power + 729 * (place * (place - 1) * (place - 2) // 6)
    return code // power % 10


def gather_kernel(shard_ref, out_ref, own_sem, send_sem, link_recv, core_recv):
    block = shard_ref.shape[0]
    place, x = lax.axis_index("dp"), lax.axis_index("stream")
    c, y, z = place % 2, (place // 2) % 2, place // 4
    up, down, across, beside, sibling = range(5)
    devices = [(place + 4, x), (place - 4, x), (place, 1 - x), (place + 2 - 4 * y, x)]
    devices.append((place + 1 - 2 * c, x))
    parts = part_rows(block)
    order = [z] + [digit(code, z) for code in (2101, 1322, 33)]

    barrier = pltpu.get_barrier_semaphore()
    for way in (across, beside, sibling):
        pl.semaphore_signal(barrier, inc=1, device_id=devices[way], device_id_type=MESH)

    @pl.when(z < 3)
    def greet_above():
        pl.semaphore_signal(barrier, inc=1, device_id=devices[up], device_id_type=MESH)

    @pl.when(z > 0)
    def greet_below():
        pl.semaphore_signal(barrier, inc=1, device_id=devices[down], device_id_type=MESH)

    own = pltpu.make_async_copy(shard_ref, out_ref.at[z, y, c, x], own_sem)
    own.start()
    pl.semaphore_wait(barrier, 4 + z * (3 - z) // 2)
    own.wait()

    def copy(way, zz, yy, xx, part, core=None):
        region = out_ref.at[zz, yy, c if core is None else core, xx, pl.ds(*parts[part])]
        at = ((zz * 2 + yy) * 2 + xx) * 3 + part
        return pltpu.make_async_remote_copy(
            src_ref=region,
            dst_ref=region,
            send_sem=send_sem.at[way * 48 + at],
            recv_sem=core_recv.at[at] if way == sibling else link_recv.at[at],
            device_id=devices[way],
            device_id_type=MESH,
        )

    def came(zz, yy, xx, part):
        copy(across, zz, yy, xx, part).wait_recv()

    def along(zz, yy, xx, part):
        @pl.when((z < 3) & (zz <= z))
        def send_up():
            copy(up, zz, yy, xx, part).start()

        @pl.when((z > 0) & (zz >= z))
        def send_down():
            copy(down, zz, yy, xx, part).start()

    def early(k):
        zz = order[k]
        for part in range(2):
            if k > 0:
                came(zz, y, x, part)
            along(zz, y, x, part)
            for way in (beside, across) if part == 0 else (across, beside):
                copy(way, zz, y, x, part).start()
            copy(sibling, zz, y, x, part).start()

    def middle(k):
        zz = order[k]
        came(zz, 1 - y, x, 0)
        copy(across, zz, 1 - y, x, 0).start()
        came(zz, y, 1 - x, 1)
        copy(beside, zz, y, 1 - x, 1).start()
        copy(sibling, zz, 1 - y, x, 0).start()
        copy(sibling, zz, y, 1 - x, 1).start()

    def late(k):
        zz = order[k]
        for yy, xx, part in ((y, 1 - x, 0), (1 - y, x, 1), (1 - y, 1 - x, 0), (1 - y, 1 - x, 1)):
            came(zz, yy, xx, part)
            copy(sibling, zz, yy, xx, part).start()

    def last_own(k):
        if k == 0:
            copy(across, z, y, x, 2).start()
            copy(beside, z, y, x, 2).start()
            regions = [(y, x)]
        elif k == 1:
            came(z, y, 1 - x, 2)
            copy(beside, z, y, 1 - x, 2).start()
            regions = [(y, 1 - x)]
        else:
            regions = [(1 - y, x), (1 - y, 1 - x)]
        for yy, xx in regions:
            if k == 2:
                came(z, yy, xx, 2)
            along(z, yy, xx, 2)
            copy(sibling, z, yy, xx, 2).start()

    def last(k):
        zz = order[k]
        for yy, xx in ((y, x), (y, 1 - x), (1 - y, x), (1 - y, 1 - x)):
            came(zz, yy, xx, 2)
            along(zz, yy, xx, 2)
            copy(sibling, zz, yy, xx, 2).start()

    for stage, k in (
        (early, 0),
        (last_own, 0),
        (last_own, 1),
        (early, 1),
        (middle, 0),
        (last_own, 2),
        (early, 2),
        (middle, 1),
        (early, 3),
        (last, 1),
        (late, 0),
        (middle, 2),
        (last, 2),
        (late, 1),
        (middle, 3),
        (last, 3),
        (late, 2),
        (late, 3),
    ):
        stage(k)

    for zz in range(4):
        for yy in range(2):
            for xx in range(2):
                for part in range(3):
                    copy(sibling, zz, yy, xx, part, 1 - c).wait_recv()
                    copy(sibling, zz, yy, xx, part).wait_send()

    def sent_along(zz, yy, xx, part):
        @pl.when((z < 3) & (zz <= z))
        def sent_up():
            copy(up, zz, yy, xx, part).wait_send()

        @pl.when((z > 0) & (zz >= z))
        def sent_down():
            copy(down, zz, yy, xx, part).wait_send()

    for zz in range(4):
        for part in range(2):
            sent_along(zz, y, x, part)
            copy(beside, zz, y, x, part).wait_send()
            copy(across, zz, y, x, part).wait_send()
        copy(across, zz, 1 - y, x, 0).wait_send()
        copy(beside, zz, y, 1 - x, 1).wait_send()
        for yy in range(2):
            for xx in range(2):
                sent_along(zz, yy, xx, 2)
    copy(across, z, y, x, 2).wait_send()
    copy(beside, z, y, x, 2).wait_send()
    copy(beside, z, y, 1 - x, 2).wait_send()


def gather_shards(shard):
    block, width = shard.shape
    dma = pltpu.SemaphoreType.DMA
    gathered = pl.pallas_call(
        gather_kernel,
        out_shape=jax.ShapeDtypeStruct((4, 2, 2, 2, block, width), shard.dtype),
        in_specs=[pl.BlockSpec(memory_space=pl.ANY)],
        out_specs=pl.BlockSpec(memory_space=pl.ANY),
        scratch_shapes=[dma, dma((240,)), dma((48,)), dma((48,))],
        compiler_params=pltpu.CompilerParams(
            collective_id=1, has_side_effects=True, vmem_limit_bytes=56 * 2**20
        ),
        cost_estimate=pl.CostEstimate(
            flops=0, bytes_accessed=64 * shard.size, transcendentals=0
        ),
        name="gather_shards",
    )(shard)
    return gathered.reshape(32 * block, width)


def pre_kernel(grad_ref, weight_ref, slope_ref, pre_ref, sum_ref):
    for at in range(0, weight_ref.shape[0], FFN_PART):
        part = slice(at, at + FFN_PART)
        pre = (
            dot_rows(grad_ref[...], weight_ref[part, :]) * slope_ref[:, part].astype(jnp.float32)
        ).astype(jnp.bfloat16)
        pre_ref[:, part] = pre
        sum_ref[:, part] = jnp.sum(pre.astype(jnp.float32), axis=0, keepdims=True)


def pre_and_sum(grad, weight, slope):
    count, depth = grad.shape
    width = weight.shape[0]
    columns = pl.BlockSpec((count, FFN_TILE), lambda tile: (0, tile))
    vector = pl.BlockSpec((1, FFN_TILE), lambda tile: (0, tile))
    pre, total = pl.pallas_call(
        pre_kernel,
        grid=(width // FFN_TILE,),
        in_specs=[
            pl.BlockSpec((count, depth), lambda tile: (0, 0)),
            pl.BlockSpec((FFN_TILE, depth), lambda tile: (tile, 0)),
            columns,
        ],
        out_specs=[columns, vector],
        out_shape=[
            jax.ShapeDtypeStruct((count, width), jnp.bfloat16),
            jax.ShapeDtypeStruct((1, width), jnp.float32),
        ],
        compiler_params=pltpu.CompilerParams(vmem_limit_bytes=56 * 2**20),
        cost_estimate=pl.CostEstimate(
            flops=2 * count * depth * width,
            bytes_accessed=2 * (count * depth + depth * width + 2 * count * width),
            transcendentals=0,
        ),
        name="pre_and_sum",
    )(grad, weight, slope)
    return pre, total[0]


def local(
    dp_count,
    main_rows,
    pred_rows,
    enc_rows,
    doc_lengths,
    main_cotangent,
    pred_cotangent,
    proj_master,
    proj_first,
    proj_second,
    bias_master,
    bias_first,
    bias_second,
    down_master,
    down_first,
    down_second,
    small_master,
    small_first,
    small_second,
):
    devices = 2 * dp_count
    rel_width = BUCKETS * HEADS
    cross_start = 4 * D + rel_width
    half_rows = main_rows.shape[0]
    group_rows = pred_rows.shape[0]

    bias_wide = to_all(bias_master.astype(jnp.bfloat16), devices).astype(jnp.float32)
    proj_low = proj_master.astype(jnp.bfloat16).T
    if dp_count == 16:
        proj_rows = gather_shards(proj_low)
    else:
        proj_rows = lax.all_gather(proj_low, ("dp", "stream"), axis=0, tiled=True)
    down_low = lax.optimization_barrier((down_master.astype(jnp.bfloat16), proj_rows))[0]
    down_weight = lax.all_gather(down_low, ("dp", "stream"), axis=0, tiled=True)
    query_weight = proj_rows[0:D]
    keys_weight = proj_rows[D : 3 * D]
    out_weight = proj_rows[3 * D : 4 * D]
    table_weight = (
        proj_rows[4 * D : cross_start]
        .reshape(BUCKETS, HEADS, D)
        .transpose(1, 0, 2)
        .reshape(rel_width, D)
    )
    cross_weight = proj_rows[cross_start : cross_start + D]
    pair_weight = proj_rows[cross_start + D : cross_start + 3 * D]
    back_weight = proj_rows[cross_start + 3 * D : cross_start + 4 * D]
    up_weight = proj_rows[cross_start + 4 * D :]
    query_bias = bias_wide[0:D]
    value_bias = bias_wide[D : 2 * D]
    out_bias = bias_wide[2 * D : 3 * D]
    table_bias = bias_wide[3 * D : 3 * D + rel_width].reshape(BUCKETS, HEADS).T.reshape(rel_width)
    cross_bias = bias_wide[3 * D + rel_width : 4 * D + rel_width]
    pair_bias = bias_wide[4 * D + rel_width : 5 * D + rel_width]
    back_bias = bias_wide[5 * D + rel_width : 6 * D + rel_width]
    up_bias = bias_wide[6 * D + rel_width :]
    zero_bias = jnp.zeros((D,), jnp.float32)

    main_start = lax.axis_index("stream") * half_rows
    places = jnp.arange(group_rows, dtype=jnp.int32)
    group_docs = doc_ids(doc_lengths[0], group_rows)
    query_docs = jnp.concatenate(
        [lax.dynamic_slice_in_dim(group_docs, main_start, half_rows), group_docs]
    )
    query_places = jnp.concatenate([main_start + jnp.arange(half_rows, dtype=jnp.int32), places])
    main_flag = jnp.arange(half_rows + group_rows, dtype=jnp.int32) < half_rows
    same_doc = query_docs[:, None] == group_docs[None, :]
    distance = query_places[:, None] - places[None, :]
    allowed = same_doc & ((distance > 0) | (distance == 0) & main_flag[:, None])
    self_mask = jnp.where(allowed, 0.0, MASKED)
    cross_mask = jnp.where(same_doc, 0.0, MASKED)
    lane = jnp.arange(LANES, dtype=jnp.int32)
    turn = jnp.mod(query_places[:, None] - lane[None, :], LANES)
    spread = bucket_of(turn)
    edge = jnp.broadcast_to(query_places[:, None] - LANES, turn.shape)

    main_all = both_parts(main_rows)
    enc_all = both_parts(enc_rows)
    inputs = jnp.concatenate([main_rows, pred_rows], axis=0)
    key_inputs = jnp.concatenate([main_all, pred_rows], axis=0)
    input_values = inputs.astype(jnp.float32)
    query_low = (times_transpose(inputs, query_weight) + query_bias).astype(jnp.bfloat16)
    self_pairs = (
        times_transpose(key_inputs, keys_weight) + jnp.concatenate([zero_bias, value_bias])
    ).astype(jnp.bfloat16)
    table = times_transpose(inputs, table_weight) + table_bias
    cross_pairs = (
        times_transpose(enc_all, pair_weight) + jnp.concatenate([zero_bias, pair_bias])
    ).astype(jnp.bfloat16)
    context_low, self_log = self_forward(query_low, self_pairs, table, spread, edge, self_mask)
    norm_one_in = input_values + times_transpose(context_low, out_weight) + out_bias
    stats_one = norm_stats(norm_one_in)
    hidden_one = (norm_one_in - stats_one[0]) * stats_one[1] * small_master[1] + small_master[4]
    one_low = hidden_one.astype(jnp.bfloat16)

    cross_query = (times_transpose(one_low, cross_weight) + cross_bias).astype(jnp.bfloat16)
    cross_low, cross_log = cross_forward(cross_query, cross_pairs, cross_mask)
    norm_two_in = hidden_one + times_transpose(cross_low, back_weight) + back_bias
    stats_two = norm_stats(norm_two_in)
    hidden_two = (norm_two_in - stats_two[0]) * stats_two[1] * small_master[2] + small_master[5]
    two_low = hidden_two.astype(jnp.bfloat16)

    active, slope = gelu_and_slope(times_transpose(two_low, up_weight) + up_bias)
    active_low = active.astype(jnp.bfloat16)
    slope_low = slope.astype(jnp.bfloat16)
    norm_three_in = hidden_two + matmul(active_low, down_weight) + small_master[0]
    stats_three = norm_stats(norm_three_in)
    final_rows = (
        (norm_three_in - stats_three[0]) * stats_three[1] * small_master[3] + small_master[6]
    ).astype(jnp.bfloat16)

    cotangent = jnp.concatenate([main_cotangent, pred_cotangent], axis=0).astype(jnp.float32)
    sum_three, gain_three, shift_three = norm_back(
        norm_three_in, stats_three, small_master[3], cotangent
    )
    ffn_grad = sum_three.astype(jnp.bfloat16)
    slab = proj_rows.shape[0] // 4
    down_part = sum_shares(column_sums(active_low, ffn_grad))
    pre_grad, pre_sum = pre_and_sum(ffn_grad, down_weight, slope_low)
    up_cut = 3 * slab - cross_start - 4 * D
    up_part = sum_shares(column_sums(pre_grad, two_low))
    two_grad = sum_three + matmul(pre_grad, up_weight)

    sum_two, gain_two, shift_two = norm_back(norm_two_in, stats_two, small_master[2], two_grad)
    branch_grad = sum_two.astype(jnp.bfloat16)
    cross_low_grad = matmul(branch_grad, back_weight).astype(jnp.bfloat16)
    cquery_grad, ckey_grad, cvalue_grad = cross_backward(
        cross_query, cross_pairs, cross_mask, cross_log, cross_low_grad
    )
    enc_grad = pair_sum(matmul(ckey_grad, pair_weight[:D]) + matmul(cvalue_grad, pair_weight[D:]))
    one_grad = sum_two + matmul(cquery_grad, cross_weight)

    sum_one, gain_one, shift_one = norm_back(norm_one_in, stats_one, small_master[1], one_grad)
    attn_grad = sum_one.astype(jnp.bfloat16)
    context_grad = matmul(attn_grad, out_weight).astype(jnp.bfloat16)
    query_grad, key_grad, value_grad, table_wide = self_backward(
        query_low, self_pairs, table, spread, edge, turn, self_mask, self_log, context_grad
    )
    table_wide = lax.optimization_barrier((table_wide, down_part))[0]
    table_grad = table_wide.astype(jnp.bfloat16)
    table_rows = (
        column_sums(table_grad, inputs)
        .reshape(HEADS, BUCKETS, D)
        .transpose(1, 0, 2)
        .reshape(rel_width, D)
    )
    late_rows = jnp.concatenate(
        [
            column_sums(query_grad, inputs),
            column_sums(key_grad, key_inputs),
            column_sums(value_grad, key_inputs),
            column_sums(attn_grad, context_low),
            table_rows,
            column_sums(cquery_grad, one_low),
            column_sums(ckey_grad, enc_all),
            column_sums(cvalue_grad, enc_all),
            column_sums(branch_grad, cross_low),
            column_sums(pre_grad[:, :up_cut], two_low),
        ]
    )
    pair_input_grad = matmul(key_grad, keys_weight[:D]) + matmul(value_grad, keys_weight[D:])
    query_input_grad = (
        sum_one + matmul(query_grad, query_weight) + matmul(table_grad, table_weight)
    )
    main_grad = query_input_grad[:half_rows] + pair_sum(pair_input_grad[:group_rows])
    pred_grad = query_input_grad[half_rows:] + pair_input_grad[group_rows:]

    def row_sum(rows):
        return jnp.sum(rows, axis=0, dtype=jnp.float32)

    bias_parts = jnp.concatenate(
        [
            row_sum(query_grad),
            row_sum(value_grad),
            row_sum(attn_grad),
            row_sum(table_grad).reshape(HEADS, BUCKETS).T.reshape(rel_width),
            row_sum(cquery_grad),
            row_sum(cvalue_grad),
            row_sum(branch_grad),
            pre_sum,
        ]
    )
    small_parts = jnp.concatenate(
        [row_sum(ffn_grad), gain_one, gain_two, gain_three, shift_one, shift_two, shift_three]
    )
    vector_parts = jnp.concatenate(
        [bias_parts.reshape(devices, -1), small_parts.reshape(devices, -1)], axis=1
    )
    vector_sum = jnp.sum(
        lax.all_to_all(vector_parts, ("dp", "stream"), 0, 0, tiled=True), axis=0
    )
    bias_len = bias_master.shape[0]
    bias_grad = vector_sum[:bias_len]
    small_sums = to_all(vector_sum[bias_len:], devices)

    slab_three = to_last_quarter(up_part, devices, up_cut)
    late_rows = lax.optimization_barrier((late_rows, vector_sum, slab_three))[0]
    if dp_count == 16:
        late_sum = sum_slabs(late_rows, 3)
    else:
        late_sum = Scatter(late_rows, range(3), dp_count).finish()
    small_grad = lax.optimization_barrier((small_sums, late_sum))[0].reshape(small_master.shape)
    outer = place_on(("dp", dp_count // 4, 4))
    proj_grad = jnp.where(outer == 3, slab_three.astype(jnp.float32), late_sum).T
    down_grad = down_part.astype(jnp.float32)
    return (
        final_rows[:half_rows],
        final_rows[half_rows:],
        main_grad.astype(jnp.bfloat16),
        pred_grad.astype(jnp.bfloat16),
        enc_grad.astype(jnp.bfloat16),
        *adam_step(proj_master, proj_first, proj_second, proj_grad, RATE_MATRIX, WEIGHT_DECAY),
        *adam_step(bias_master, bias_first, bias_second, bias_grad, RATE_VECTOR, 0.0),
        *adam_step(down_master, down_first, down_second, down_grad, RATE_MATRIX, WEIGHT_DECAY),
        *adam_step(small_master, small_first, small_second, small_grad, RATE_SMALL, 0.0),
    )


def solution(mesh):
    rows = P(("dp", "stream"), None)
    columns = P(None, ("dp", "stream"))
    vector = P(("dp", "stream"))
    masters = (columns,) * 3 + (vector,) * 3 + (rows,) * 3 + (P(),) * 3
    return jax.shard_map(
        partial(local, mesh.shape["dp"]),
        mesh=mesh,
        in_specs=(rows, rows, rows, P("dp", None), rows, rows) + masters,
        out_specs=(rows,) * 5 + masters,
        check_vma=False,
    )
```

```python
from functools import partial
import math

import jax
import jax.numpy as jnp
from jax import lax
from jax.experimental import pallas as pl
from jax.experimental.pallas import tpu as pltpu
from jax.sharding import PartitionSpec as P

D = 1024
HEADS = 16
BUCKETS = 32
STEP = 10
HEAD_DIM = 64
LANES = 128
CHUNK = 128
SCORE_SCALE = HEAD_DIM**-0.5

NORM_EPS = 1e-05
BETA_FIRST = 0.9
BETA_SECOND = 0.999
ADAM_EPS = 1e-08
RATE_MATRIX = 0.04
RATE_VECTOR = 0.15
RATE_SMALL = 0.5
WEIGHT_DECAY = 0.01
MASKED = -1e30
SUM_WAVES = 4
SUM_CHUNKS = 2 * SUM_WAVES
FFN_TILE = 1024
FFN_PART = 256
MESH = pl.DeviceIdType.MESH


def bucket_edges():
    return [int(math.ceil(16.0 * 8.0 ** (step_index / 16.0))) for step_index in range(1, 16)]


def bucket_of(distance):
    counted = jnp.zeros_like(distance)
    for threshold in bucket_edges():
        counted = counted + (distance >= threshold).astype(jnp.int32)
    return jnp.where(distance < 16, distance, 16 + counted)


def doc_ids(lengths, length_total):
    doc_ends = jnp.cumsum(lengths)
    places = jnp.arange(length_total, dtype=jnp.int32)
    return jnp.sum((places[:, None] >= doc_ends[None, :]).astype(jnp.int32), axis=1)


def matmul(left_side, right_side):
    return jnp.dot(left_side, right_side, preferred_element_type=jnp.float32)


def outer_sum(left_side, right_side):
    return lax.dot_general(
        left_side, right_side, (((0,), (0,)), ((), ())), preferred_element_type=jnp.float32
    )


def times_transpose(left_side, right_side):
    return lax.dot_general(
        left_side, right_side, (((1,), (1,)), ((), ())), preferred_element_type=jnp.float32
    )


def norm_stats(hidden):
    mean = jnp.mean(hidden, axis=-1, keepdims=True)
    centre = hidden - mean
    spread = jnp.mean(centre * centre, axis=-1, keepdims=True)
    return mean, lax.rsqrt(spread + NORM_EPS)


def norm_back(hidden, stats, gain_row, grad):
    mean, inverse = stats
    normed = (hidden - mean) * inverse
    scaled = grad * gain_row
    first = jnp.mean(scaled, axis=-1, keepdims=True)
    second = jnp.mean(scaled * normed, axis=-1, keepdims=True)
    hidden_grad = (scaled - first - normed * second) * inverse
    return hidden_grad, jnp.sum(grad * normed, axis=0), jnp.sum(grad, axis=0)


def gelu_and_slope(values):
    size = jnp.abs(values) * (0.5**0.5)
    place = 1.0 / (1.0 + 0.3275911 * size)
    fit = 1.061405429
    for coefficient in (-1.453152027, 1.421413741, -0.284496736, 0.254829592):
        fit = fit * place + coefficient
    bell = jnp.exp(-size * size)
    tail = (0.5 * place) * (fit * bell)
    below = jnp.where(values >= 0.0, 1.0 - tail, tail)
    return values * below, below + values * bell * (1.0 / math.sqrt(2.0 * math.pi))


def dot_rows(left_side, right_side):
    return lax.dot_general(
        left_side, right_side, (((1,), (1,)), ((), ())), preferred_element_type=jnp.float32
    )


def lookup(table, index):
    return jnp.take_along_axis(table, index, axis=1, mode="promise_in_bounds")


def wide(column):
    return jnp.broadcast_to(column, (column.shape[0], LANES))


def tiled(block, key_count):
    return jnp.concatenate([block] * (key_count // LANES), axis=1)


def row_blocks(main_count, key_count, size):
    blocks = [(at, min(size, main_count - at), key_count) for at in range(0, main_count, size)]
    step = min(size, LANES)
    for at in range(0, key_count, step):
        seen = min(key_count, (at + step + LANES - 1) // LANES * LANES)
        blocks.append((main_count + at, min(step, key_count - at), seen))
    return blocks


def bias_of(near_bias, far_bias, edge, row_count, key_count):
    lane = lax.broadcasted_iota(jnp.int32, (row_count, LANES), 1)
    return jnp.concatenate(
        [
            jnp.where(lane + at > edge, near_bias, far_bias)
            for at in range(0, key_count, LANES)
        ],
        axis=1,
    )


def both_halves(block, head):
    lane = lax.broadcasted_iota(jnp.int32, block.shape, 1)
    turned = pltpu.roll(block, HEAD_DIM, 1)
    return jnp.where((lane < HEAD_DIM) == (head == 0), block, turned)


def self_forward_kernel(
    query_ref,
    key_ref,
    value_ref,
    own_key_ref,
    own_value_ref,
    table_ref,
    spread_ref,
    edge_ref,
    mask_ref,
    context_ref,
    log_ref,
    score_ref,
    prob_ref,
    near_ref,
    far_ref,
):
    rows, key_count = mask_ref.shape
    main_count = rows - key_count
    parity = lax.rem(pl.program_id(0), 2)
    groups = row_blocks(main_count, key_count, 512)
    chunks = row_blocks(main_count, key_count, CHUNK)
    for head in range(2):
        at = head * HEAD_DIM
        head_lanes = slice(at, at + HEAD_DIM)
        first = (parity * 2 + head) * BUCKETS
        query = query_ref[:, head_lanes] * jnp.bfloat16(SCORE_SCALE)
        keys = key_ref[:, head_lanes]
        values = value_ref[:, head_lanes]
        own_keys = own_key_ref[:, head_lanes].astype(jnp.float32)
        own_values = own_value_ref[:, head_lanes].astype(jnp.float32)
        near_ref[head] = lookup(table_ref[...], spread_ref[...] + first)
        far_ref[head] = lookup(
            table_ref[...], jnp.full((rows, LANES), first + BUCKETS - 1, jnp.int32)
        )
        own_score = wide(
            jnp.sum(query[main_count:].astype(jnp.float32) * own_keys, axis=1, keepdims=True)
        ) + lookup(table_ref[main_count:, :], jnp.full((key_count, LANES), first, jnp.int32))
        for row, count, seen in groups:
            score_ref[head, row : row + count, 0:seen] = dot_rows(
                query[row : row + count], keys[0:seen]
            )
        tops = []
        for row, count, seen in chunks:
            part = slice(row, row + count)
            scores = (
                score_ref[head, part, 0:seen]
                + bias_of(near_ref[head, part], far_ref[head, part], edge_ref[part], count, seen)
                + mask_ref[part, 0:seen]
            )
            score_ref[head, part, 0:seen] = scores
            tops.append(wide(jnp.max(scores, axis=1, keepdims=True)))
        top = jnp.concatenate(tops, axis=0)
        top = jnp.concatenate(
            [top[:main_count], jnp.maximum(top[main_count:], own_score)], axis=0
        )
        own_weight = jnp.exp(own_score - top[main_count:])
        totals = []
        for row, count, seen in chunks:
            part = slice(row, row + count)
            weights = jnp.exp(score_ref[head, part, 0:seen] - tiled(top[part], seen))
            score_ref[head, part, 0:seen] = weights
            totals.append(wide(jnp.sum(weights, axis=1, keepdims=True)))
        total = jnp.concatenate(totals, axis=0)
        total = jnp.concatenate([total[:main_count], total[main_count:] + own_weight], axis=0)
        inverse = 1.0 / total
        log_ref[:, head_lanes] = (top + jnp.log(total))[:, 0:HEAD_DIM]
        own_prob = (own_weight * inverse[main_count:]).astype(jnp.bfloat16).astype(jnp.float32)
        for row, count, seen in chunks:
            part = slice(row, row + count)
            prob_ref[head, part, 0:seen] = (
                score_ref[head, part, 0:seen] * tiled(inverse[part], seen)
            ).astype(jnp.bfloat16)
        for row, count, seen in groups:
            part = slice(row, row + count)
            context = matmul(prob_ref[head, part, 0:seen], values[0:seen])
            if row >= main_count:
                own = slice(row - main_count, row - main_count + count)
                context = context + own_prob[own, 0:HEAD_DIM] * own_values[own]
            context_ref[part, head_lanes] = context.astype(jnp.bfloat16)


def self_backward_kernel(
    query_ref,
    key_ref,
    value_ref,
    own_key_ref,
    own_value_ref,
    table_ref,
    spread_ref,
    edge_ref,
    turn_ref,
    mask_ref,
    log_ref,
    context_ref,
    query_grad_ref,
    key_grad_ref,
    value_grad_ref,
    table_grad_ref,
    score_ref,
    prob_grad_ref,
    prob_ref,
    score_grad_ref,
    near_ref,
    far_ref,
    close_ref,
    rest_ref,
):
    rows, key_count = mask_ref.shape
    main_count = rows - key_count
    parity = lax.rem(pl.program_id(0), 2)
    groups = row_blocks(main_count, key_count, 512)
    chunks = row_blocks(main_count, key_count, CHUNK)
    bucket = bucket_of(lax.broadcasted_iota(jnp.int32, (LANES, LANES), 0))
    bucket_lane = lax.broadcasted_iota(jnp.int32, (LANES, LANES), 1)
    row_lane = lax.broadcasted_iota(jnp.int32, (rows, LANES), 1)
    table_total = jnp.zeros((rows, LANES), jnp.float32)
    own_total = jnp.zeros((key_count, LANES), jnp.float32)
    for head in range(2):
        at = head * HEAD_DIM
        head_lanes = slice(at, at + HEAD_DIM)
        first = (parity * 2 + head) * BUCKETS
        query = query_ref[:, head_lanes] * jnp.bfloat16(SCORE_SCALE)
        keys = key_ref[:, head_lanes]
        values = value_ref[:, head_lanes]
        context = context_ref[:, head_lanes]
        own_keys = own_key_ref[:, head_lanes].astype(jnp.float32)
        own_values = own_value_ref[:, head_lanes].astype(jnp.float32)
        own_query = query[main_count:].astype(jnp.float32)
        own_context = context[main_count:].astype(jnp.float32)
        near_ref[head] = lookup(table_ref[...], spread_ref[...] + first)
        far_ref[head] = lookup(
            table_ref[...], jnp.full((rows, LANES), first + BUCKETS - 1, jnp.int32)
        )
        own_score = wide(jnp.sum(own_query * own_keys, axis=1, keepdims=True)) + lookup(
            table_ref[main_count:, :], jnp.full((key_count, LANES), first, jnp.int32)
        )
        log_total = both_halves(log_ref[...], head)
        own_prob = jnp.exp(own_score - log_total[main_count:])
        own_prob_grad = wide(jnp.sum(own_context * own_values, axis=1, keepdims=True))
        value_grad_ref[key_count:, head_lanes] = (
            own_prob[:, 0:HEAD_DIM].astype(jnp.bfloat16).astype(jnp.float32) * own_context
        ).astype(jnp.bfloat16)
        for row, count, seen in groups:
            part = slice(row, row + count)
            score_ref[head, part, 0:seen] = dot_rows(query[part], keys[0:seen])
            prob_grad_ref[head, part, 0:seen] = dot_rows(context[part], values[0:seen])
        row_dots = []
        for row, count, seen in chunks:
            part = slice(row, row + count)
            edge = edge_ref[part]
            bias = bias_of(near_ref[head, part], far_ref[head, part], edge, count, seen)
            probs = jnp.exp(
                score_ref[head, part, 0:seen]
                + bias
                + (mask_ref[part, 0:seen] - tiled(log_total[part], seen))
            )
            prob_grad = prob_grad_ref[head, part, 0:seen]
            row_dot = wide(jnp.sum(probs * prob_grad, axis=1, keepdims=True))
            if row >= main_count:
                own = slice(row - main_count, row - main_count + count)
                row_dot = row_dot + own_prob[own] * own_prob_grad[own]
                row_dots.append(row_dot)
            score_grad = (probs * (prob_grad - tiled(row_dot, seen))).astype(jnp.bfloat16)
            prob_ref[head, part, 0:seen] = probs.astype(jnp.bfloat16)
            score_grad_ref[head, part, 0:seen] = score_grad
            score_wide = score_grad.astype(jnp.float32)
            lane = lax.broadcasted_iota(jnp.int32, (count, LANES), 1)
            close = jnp.zeros((count, LANES), jnp.float32)
            whole = jnp.zeros((count, LANES), jnp.float32)
            for at_key in range(0, seen, LANES):
                block = score_wide[:, at_key : at_key + LANES]
                whole = whole + block
                close = close + jnp.where(lane + at_key > edge, block, 0.0)
            close_ref[head, part] = close
            rest_ref[head, part] = whole - close
        own_grad = (
            (own_prob * (own_prob_grad - jnp.concatenate(row_dots, axis=0)))
            .astype(jnp.bfloat16)
            .astype(jnp.float32)
        )
        key_grad_ref[key_count:, head_lanes] = (own_grad[:, 0:HEAD_DIM] * own_query).astype(
            jnp.bfloat16
        )
        turned = lookup(close_ref[head], turn_ref[...]).astype(jnp.bfloat16)
        table_total = table_total + matmul(
            turned, (bucket_lane == bucket + first).astype(jnp.bfloat16)
        )
        table_total = table_total + jnp.where(
            row_lane == first + BUCKETS - 1, jnp.sum(rest_ref[head], axis=1, keepdims=True), 0.0
        )
        own_total = own_total + jnp.where(row_lane[main_count:] == first, own_grad, 0.0)
        for row, count, seen in groups:
            part = slice(row, row + count)
            query_grad = matmul(score_grad_ref[head, part, 0:seen], keys[0:seen])
            if row >= main_count:
                own = slice(row - main_count, row - main_count + count)
                query_grad = query_grad + own_grad[own, 0:HEAD_DIM] * own_keys[own]
            query_grad_ref[part, head_lanes] = (query_grad * SCORE_SCALE).astype(jnp.bfloat16)
        for at_key in range(0, key_count, LANES):
            block = slice(at_key, at_key + LANES)
            later = slice(main_count + at_key, rows)
            key_grad_ref[block, head_lanes] = (
                outer_sum(score_grad_ref[head, 0:main_count, block], query[0:main_count])
                + outer_sum(score_grad_ref[head, later, block], query[later])
            ).astype(jnp.bfloat16)
            value_grad_ref[block, head_lanes] = (
                outer_sum(prob_ref[head, 0:main_count, block], context[0:main_count])
                + outer_sum(prob_ref[head, later, block], context[later])
            ).astype(jnp.bfloat16)
    table_total = jnp.concatenate(
        [table_total[:main_count], table_total[main_count:] + own_total], axis=0
    )

    @pl.when(parity == 0)
    def first_pair():
        table_grad_ref[...] = table_total

    @pl.when(parity == 1)
    def second_pair():
        table_grad_ref[...] += table_total


def cross_forward_kernel(
    query_ref, key_ref, value_ref, mask_ref, context_ref, log_ref, score_ref, prob_ref
):
    rows = mask_ref.shape[0]
    for head in range(2):
        at = head * HEAD_DIM
        head_lanes = slice(at, at + HEAD_DIM)
        query = query_ref[:, head_lanes] * jnp.bfloat16(SCORE_SCALE)
        score_ref[head] = dot_rows(query, key_ref[:, head_lanes])
        for row in range(0, rows, CHUNK):
            part = slice(row, min(row + CHUNK, rows))
            scores = score_ref[head, part] + mask_ref[part]
            top = jnp.max(scores, axis=1, keepdims=True)
            weights = jnp.exp(scores - top)
            total = jnp.sum(weights, axis=1, keepdims=True)
            prob_ref[head, part] = (weights * (1.0 / total)).astype(jnp.bfloat16)
            log_ref[part, head_lanes] = jnp.broadcast_to(
                top + jnp.log(total), (scores.shape[0], HEAD_DIM)
            )
        context_ref[:, head_lanes] = matmul(prob_ref[head], value_ref[:, head_lanes]).astype(
            jnp.bfloat16
        )


def cross_backward_kernel(
    query_ref,
    key_ref,
    value_ref,
    mask_ref,
    log_ref,
    context_ref,
    query_grad_ref,
    key_grad_ref,
    value_grad_ref,
    score_ref,
    prob_grad_ref,
    prob_ref,
    score_grad_ref,
):
    rows = mask_ref.shape[0]
    for head in range(2):
        at = head * HEAD_DIM
        head_lanes = slice(at, at + HEAD_DIM)
        query = query_ref[:, head_lanes] * jnp.bfloat16(SCORE_SCALE)
        keys = key_ref[:, head_lanes]
        context = context_ref[:, head_lanes]
        score_ref[head] = dot_rows(query, keys)
        prob_grad_ref[head] = dot_rows(context, value_ref[:, head_lanes])
        for row in range(0, rows, CHUNK):
            part = slice(row, min(row + CHUNK, rows))
            probs = jnp.exp(
                score_ref[head, part] + (mask_ref[part] - log_ref[part, at : at + 1])
            )
            prob_grad = prob_grad_ref[head, part]
            row_dot = jnp.sum(probs * prob_grad, axis=1, keepdims=True)
            prob_ref[head, part] = probs.astype(jnp.bfloat16)
            score_grad_ref[head, part] = (probs * (prob_grad - row_dot)).astype(jnp.bfloat16)
        query_grad_ref[:, head_lanes] = (matmul(score_grad_ref[head], keys) * SCORE_SCALE).astype(
            jnp.bfloat16
        )
        key_grad_ref[:, head_lanes] = outer_sum(score_grad_ref[head], query).astype(jnp.bfloat16)
        value_grad_ref[:, head_lanes] = outer_sum(prob_ref[head], context).astype(jnp.bfloat16)


def pair_block(row_count, row_block=0, first_pair=0):
    return pl.BlockSpec((row_count, LANES), lambda pair: (row_block, first_pair + pair))


def whole_block(shape):
    return pl.BlockSpec(shape, lambda pair: (0, 0))


def attention_call(kernel, name, in_specs, out_specs, out_shape, scratch, arrays, flops, passes):
    moved = sum(array.size * array.dtype.itemsize for array in arrays)
    moved += sum(math.prod(shape.shape) * shape.dtype.itemsize for shape in out_shape)
    return pl.pallas_call(
        kernel,
        grid=(HEADS // 2,),
        in_specs=in_specs,
        out_specs=out_specs,
        out_shape=out_shape,
        scratch_shapes=scratch,
        compiler_params=pltpu.CompilerParams(vmem_limit_bytes=56 * 2**20),
        cost_estimate=pl.CostEstimate(flops=flops, bytes_accessed=moved, transcendentals=passes),
        name=name,
    )(*arrays)


def low_array(row_count):
    return jax.ShapeDtypeStruct((row_count, D), jnp.bfloat16)


def self_forward(query, pairs, table, spread, edge, mask):
    rows, keys = mask.shape
    width = D // LANES
    square = pltpu.VMEM((2, rows, keys), jnp.float32)
    narrow = pltpu.VMEM((2, rows, LANES), jnp.float32)
    return attention_call(
        self_forward_kernel,
        "self_forward",
        [
            pair_block(rows),
            pair_block(keys),
            pair_block(keys, 0, width),
            pair_block(keys, 1),
            pair_block(keys, 1, width),
            pl.BlockSpec((rows, LANES), lambda pair: (0, pair // 2)),
            whole_block((rows, LANES)),
            whole_block((rows, LANES)),
            whole_block((rows, keys)),
        ],
        [pair_block(rows), pair_block(rows)],
        [low_array(rows), jax.ShapeDtypeStruct((rows, D), jnp.float32)],
        [square, pltpu.VMEM((2, rows, keys), jnp.bfloat16), narrow, narrow],
        (query, pairs, pairs, pairs, pairs, table, spread, edge, mask),
        4 * rows * keys * D,
        rows * keys * HEADS,
    )


def self_backward(query, pairs, table, spread, edge, turn, mask, log_total, context_grad):
    rows, keys = mask.shape
    width = D // LANES
    square = pltpu.VMEM((2, rows, keys), jnp.float32)
    square_low = pltpu.VMEM((2, rows, keys), jnp.bfloat16)
    narrow = pltpu.VMEM((2, rows, LANES), jnp.float32)
    table_block = pl.BlockSpec((rows, LANES), lambda pair: (0, pair // 2))
    return attention_call(
        self_backward_kernel,
        "self_backward",
        [
            pair_block(rows),
            pair_block(keys),
            pair_block(keys, 0, width),
            pair_block(keys, 1),
            pair_block(keys, 1, width),
            table_block,
            whole_block((rows, LANES)),
            whole_block((rows, LANES)),
            whole_block((rows, LANES)),
            whole_block((rows, keys)),
            pair_block(rows),
            pair_block(rows),
        ],
        [pair_block(rows), pair_block(2 * keys), pair_block(2 * keys), table_block],
        [
            low_array(rows),
            low_array(2 * keys),
            low_array(2 * keys),
            jax.ShapeDtypeStruct(table.shape, jnp.float32),
        ],
        [square, square, square_low, square_low, narrow, narrow, narrow, narrow],
        (query, pairs, pairs, pairs, pairs, table, spread, edge, turn, mask, log_total, context_grad),
        10 * rows * keys * D,
        rows * keys * HEADS,
    )


def cross_forward(query, pairs, mask):
    rows, keys = mask.shape
    return attention_call(
        cross_forward_kernel,
        "cross_forward",
        [
            pair_block(rows),
            pair_block(keys),
            pair_block(keys, 0, D // LANES),
            whole_block((rows, keys)),
        ],
        [pair_block(rows), pair_block(rows)],
        [low_array(rows), jax.ShapeDtypeStruct((rows, D), jnp.float32)],
        [pltpu.VMEM((2, rows, keys), jnp.float32), pltpu.VMEM((2, rows, keys), jnp.bfloat16)],
        (query, pairs, pairs, mask),
        4 * rows * keys * D,
        rows * keys * HEADS,
    )


def cross_backward(query, pairs, mask, log_total, context_grad):
    rows, keys = mask.shape
    square = pltpu.VMEM((2, rows, keys), jnp.float32)
    square_low = pltpu.VMEM((2, rows, keys), jnp.bfloat16)
    return attention_call(
        cross_backward_kernel,
        "cross_backward",
        [
            pair_block(rows),
            pair_block(keys),
            pair_block(keys, 0, D // LANES),
            whole_block((rows, keys)),
            pair_block(rows),
            pair_block(rows),
        ],
        [pair_block(rows), pair_block(keys), pair_block(keys)],
        [low_array(rows), low_array(keys), low_array(keys)],
        [square, square, square_low, square_low],
        (query, pairs, pairs, mask, log_total, context_grad),
        10 * rows * keys * D,
        rows * keys * HEADS,
    )


def column_sums(left_side, right_side):
    return outer_sum(left_side, right_side).astype(jnp.bfloat16)


def inner_levels(dp_count):
    levels = [("dp", 1, 2), ("stream", 1, 2)]
    if dp_count == 64:
        return levels + [("dp", 2, 2), ("dp", 4, 4)]
    return levels + [("dp", 2, 2)]


def rotation(level, shift, dp_count):
    axis, stride, size = level
    total = 2 if axis == "stream" else dp_count
    pairs = []
    for source in range(total):
        place = (source // stride) % size
        target = source + ((place + shift) % size - place) * stride
        pairs.append((source, target))
    return pairs


def place_on(level):
    axis, stride, size = level
    return (lax.axis_index(axis) // stride) % size


def pick(stacked, index, dim):
    return lax.dynamic_index_in_dim(stacked, index, dim, keepdims=False)


def scatter_level(stacked, dim, level, dp_count, final_type):
    axis, stride, size = level
    mine = place_on(level)
    total = pick(stacked, mine, dim).astype(jnp.float32)
    for shift in range(1, size):
        sent = pick(stacked, (mine + shift) % size, dim)
        came = lax.ppermute(sent, axis, rotation(level, shift, dp_count))
        total = total + came.astype(jnp.float32)
    return total.astype(final_type)


class Scatter:
    def __init__(self, rows, outer_range, dp_count, parts=2):
        self.levels = inner_levels(dp_count)
        self.inner = self.levels[2:]
        self.outer_range = outer_range
        self.dp_count = dp_count
        self.parts = parts
        sizes = [size for axis, stride, size in reversed(self.inner)]
        self.block = rows.shape[0] // (len(outer_range) * math.prod(sizes) * 4)
        self.state = [
            rows.reshape([len(outer_range)] + sizes + [2, 2, self.block, rows.shape[1]])
        ]
        self.done = 0

    def step(self):
        inner_count = len(self.inner)
        if self.done == 0:
            stacked = scatter_level(
                self.state[0], 1 + inner_count, self.levels[0], self.dp_count, jnp.bfloat16
            )
            if self.parts == 1:
                self.state = [stacked]
            else:
                cut = (self.block // 2 + 15) // 16 * 16
                self.state = [stacked[..., :cut, :], stacked[..., cut:, :]]
            order = [self.levels[1]] + self.inner
            other = [self.inner[0], self.levels[1]] + self.inner[1:]
            self.orders = [order, other]
            self.names = [list(reversed(self.inner)) + [self.levels[1]] for part in range(2)]
        elif self.done <= inner_count + 1:
            for part in range(self.parts):
                level = self.orders[part][self.done - 1]
                dim = 1 + self.names[part].index(level)
                self.names[part].remove(level)
                self.state[part] = scatter_level(
                    self.state[part], dim, level, self.dp_count, jnp.bfloat16
                )
        else:
            self.state = [self.outer_step(piece) for piece in self.state]
        self.done += 1

    def outer_step(self, piece):
        level = ("dp", self.dp_count // 4, 4)
        mine = place_on(level)
        first, count = self.outer_range[0], len(self.outer_range)
        total = pick(piece, jnp.clip(mine - first, 0, count - 1), 0).astype(jnp.float32)
        for shift in range(1, 4):
            pairs = [
                pair
                for pair in rotation(level, shift, self.dp_count)
                if pair[1] // level[1] in self.outer_range
            ]
            target = jnp.clip((mine + shift) % 4 - first, 0, count - 1)
            total = total + lax.ppermute(pick(piece, target, 0), "dp", pairs).astype(jnp.float32)
        return total

    def finish(self):
        while self.done < len(self.inner) + 3:
            self.step()
        return jnp.concatenate(self.state)


def after(value, *scatters):
    states = [array for scatter in scatters for array in scatter.state]
    return lax.optimization_barrier((value, *states))[0]


def sum_shares(rows):
    part = lax.psum_scatter(rows, "dp", scatter_dimension=0, tiled=True)
    return lax.psum_scatter(part, "stream", scatter_dimension=0, tiled=True)


def to_last_quarter(share, devices, skipped):
    owners = devices // 4
    size = share.shape[0]
    block = (devices * size - skipped) // owners
    starts = [skipped + owner * block for owner in range(owners)]
    blocks = []
    for part in range((size - 1 + block + size - 1) // size):
        pairs = [
            (start // size + part, 3 * owners + owner)
            for owner, start in enumerate(starts)
            if start // size + part < devices
        ]
        blocks.append(lax.ppermute(share, ("dp", "stream"), pairs))
    mine = lax.axis_index("dp") * 2 + lax.axis_index("stream") - 3 * owners
    offset = jnp.mod(skipped + jnp.maximum(mine, 0) * block, size)
    return lax.dynamic_slice_in_dim(jnp.concatenate(blocks, axis=0), offset, block)


def to_all(part, count):
    shared = jnp.broadcast_to(part[None], (count, *part.shape))
    gathered = lax.all_to_all(shared, ("dp", "stream"), 0, 0, tiled=True)
    return gathered.reshape(-1, *part.shape[1:])


def swap_streams(rows):
    return lax.ppermute(rows, "stream", [(0, 1), (1, 0)])


def both_parts(rows, other):
    leading = lax.axis_index("stream") == 0
    return jnp.concatenate(
        [jnp.where(leading, rows, other), jnp.where(leading, other, rows)], axis=0
    )


def pair_sum(rows):
    half = rows.shape[0] // 2
    stream = lax.axis_index("stream")
    sent = lax.dynamic_slice_in_dim(rows, (1 - stream) * half, half).astype(jnp.bfloat16)
    return lax.dynamic_slice_in_dim(rows, stream * half, half) + swap_streams(sent).astype(
        jnp.float32
    )


def adam_step(master, first_moment, second_moment, gradient, step_rate, step_decay):
    first_new = BETA_FIRST * first_moment + (1.0 - BETA_FIRST) * gradient
    second_new = BETA_SECOND * second_moment + (1.0 - BETA_SECOND) * gradient * gradient
    first_hat = first_new / (1.0 - BETA_FIRST**STEP)
    second_hat = second_new / (1.0 - BETA_SECOND**STEP)
    master_new = master - step_rate * (
        first_hat / (jnp.sqrt(second_hat) + ADAM_EPS) + step_decay * master
    )
    return (master_new, first_new, second_new)


def chunk_rows(block):
    tiles = block // 16
    counts = [(tiles + SUM_CHUNKS - 1 - part) // SUM_CHUNKS * 16 for part in range(SUM_CHUNKS)]
    return [(sum(counts[:part]), counts[part]) for part in range(SUM_CHUNKS)]


def add_rows(target_ref, source_ref, start, count):
    @pl.loop(0, count // 16)
    def tile_step(tile):
        rows = pl.ds(pl.multiple_of(start + tile * 16, 16), 16)
        target_ref[rows, :] = (
            target_ref[rows, :].astype(jnp.float32) + source_ref[rows, :].astype(jnp.float32)
        ).astype(jnp.bfloat16)


def sum_kernel(
    grad_ref,
    out_ref,
    held,
    core_in,
    first_in,
    second_in,
    along_in,
    load_sem,
    core_send,
    core_recv,
    first_send,
    first_recv,
    second_send,
    second_recv,
    along_send,
    along_recv,
):
    slabs, block = grad_ref.shape[0], grad_ref.shape[4]
    place, x = lax.axis_index("dp"), lax.axis_index("stream")
    c, y, z = place % 2, (place // 2) % 2, place // 4
    sibling, across, beside = (place + 1 - 2 * c, x), (place, 1 - x), (place + 2 - 4 * y, x)
    above, below = (place + 4, x), (place - 4, x)
    chunks = chunk_rows(block)

    barrier = pltpu.get_barrier_semaphore()
    for neighbour in (sibling, across, beside):
        pl.semaphore_signal(barrier, inc=1, device_id=neighbour, device_id_type=MESH)

    @pl.when(z < 3)
    def greet_above():
        pl.semaphore_signal(barrier, inc=1, device_id=above, device_id_type=MESH)

    @pl.when(z > 0)
    def greet_below():
        pl.semaphore_signal(barrier, inc=1, device_id=below, device_id_type=MESH)

    pl.semaphore_wait(barrier, 4 + z * (3 - z) // 2)

    def remote(source, target, send_sem, recv_sem, device):
        return pltpu.make_async_remote_copy(
            src_ref=source,
            dst_ref=target,
            send_sem=send_sem,
            recv_sem=recv_sem,
            device_id=device,
            device_id_type=MESH,
        )

    def core_copy(s, yy, xx):
        at = s * 4 + yy * 2 + xx
        return remote(
            grad_ref.at[s, yy, 1 - c, xx],
            core_in.at[s, yy, xx],
            core_send.at[at],
            core_recv.at[at],
            sibling,
        )

    def load(s, yy, xx):
        return pltpu.make_async_copy(
            grad_ref.at[s, yy, c, xx], held.at[s, yy, xx], load_sem.at[s * 4 + yy * 2 + xx]
        )

    def first_copy(s, chunk, other):
        rows = pl.ds(*chunks[chunk])
        at = (s * SUM_CHUNKS + chunk) * 2 + other
        source = held.at[s, other, 1 - x, rows] if chunk < SUM_WAVES else held.at[s, 1 - y, other, rows]
        return remote(
            source,
            first_in.at[s, other, rows],
            first_send.at[at],
            first_recv.at[at],
            across if chunk < SUM_WAVES else beside,
        )

    def second_copy(s, chunk):
        rows = pl.ds(*chunks[chunk])
        source = held.at[s, 1 - y, x, rows] if chunk < SUM_WAVES else held.at[s, y, 1 - x, rows]
        return remote(
            source,
            second_in.at[s, rows],
            second_send.at[s * SUM_CHUNKS + chunk],
            second_recv.at[s * SUM_CHUNKS + chunk],
            beside if chunk < SUM_WAVES else across,
        )

    def along_copy(s, chunk, down):
        rows = pl.ds(*chunks[chunk])
        way = 0 if down else 1
        return remote(
            held.at[s, y, x, rows],
            along_in.at[way, s, rows],
            along_send.at[s * SUM_CHUNKS + chunk],
            along_recv.at[way * slabs * SUM_CHUNKS + s * SUM_CHUNKS + chunk],
            below if down else above,
        )

    def core_stage(s, half):
        if half == 0:
            for yy in range(2):
                for xx in range(2):
                    load(s, yy, xx).wait()
                    core_copy(s, yy, xx).wait_recv()
        for chunk in (half, half + SUM_WAVES):
            for yy in range(2):
                for xx in range(2):
                    add_rows(held.at[s, yy, xx], core_in.at[s, yy, xx], *chunks[chunk])
            for other in range(2):
                first_copy(s, chunk, other).start()

    def first_stage(s, half):
        for chunk in (half, half + SUM_WAVES):
            for other in range(2):
                first_copy(s, chunk, other).wait_recv()
                kept = held.at[s, other, x] if chunk < SUM_WAVES else held.at[s, y, other]
                add_rows(kept, first_in.at[s, other], *chunks[chunk])
            second_copy(s, chunk).start()

    def second_stage(s, half):
        for chunk in (half, half + SUM_WAVES):
            second_copy(s, chunk).wait_recv()
            add_rows(held.at[s, y, x], second_in.at[s], *chunks[chunk])
        along_stage(s, half, 0)

    def along_stage(s, half, hop):
        for down in (True, False):
            source = 3 - hop if down else hop
            if (source > s) if down else (source < s):

                @pl.when(z == source)
                def pass_on():
                    for chunk in (half, half + SUM_WAVES):
                        if hop > 0:
                            along_copy(s, chunk, down).wait_recv()
                            add_rows(
                                held.at[s, y, x], along_in.at[0 if down else 1, s], *chunks[chunk]
                            )
                        along_copy(s, chunk, down).start()

    def last_stage(s, half):
        @pl.when(z == s)
        def finish():
            for chunk in (half, half + SUM_WAVES):
                start, count = chunks[chunk]
                if s < 3:
                    along_copy(s, chunk, True).wait_recv()
                if s > 0:
                    along_copy(s, chunk, False).wait_recv()

                @pl.loop(0, count // 16)
                def tile_step(tile):
                    rows = pl.ds(pl.multiple_of(start + tile * 16, 16), 16)
                    total = held[s, y, x, rows, :].astype(jnp.float32)
                    if s < 3:
                        total = total + along_in[0, s, rows, :].astype(jnp.float32)
                    if s > 0:
                        total = total + along_in[1, s, rows, :].astype(jnp.float32)
                    out_ref[rows, :] = total

    for s in range(slabs):
        for yy in range(2):
            for xx in range(2):
                core_copy(s, yy, xx).start()
                load(s, yy, xx).start()
    out_ref[...] = jnp.zeros_like(out_ref)
    waves = [(s, half) for s in range(slabs) for half in range(SUM_WAVES)]
    stages = [
        core_stage,
        first_stage,
        second_stage,
        partial(along_stage, hop=1),
        partial(along_stage, hop=2),
        last_stage,
    ]
    for step in range(len(waves) + len(stages) - 1):
        for late, stage in enumerate(stages):
            if 0 <= step - late < len(waves):
                stage(*waves[step - late])
    for s in range(slabs):
        for yy in range(2):
            for xx in range(2):
                core_copy(s, yy, xx).wait_send()
        for chunk in range(SUM_CHUNKS):
            for other in range(2):
                first_copy(s, chunk, other).wait_send()
            second_copy(s, chunk).wait_send()

            @pl.when(z != s)
            def sent_along():
                along_copy(s, chunk, True).wait_send()


def sum_slabs(rows, slabs):
    block, width = rows.shape[0] // (slabs * 8), rows.shape[1]
    low = jnp.bfloat16
    dma = pltpu.SemaphoreType.DMA
    return pl.pallas_call(
        sum_kernel,
        out_shape=jax.ShapeDtypeStruct((block, width), jnp.float32),
        in_specs=[pl.BlockSpec(memory_space=pl.ANY)],
        out_specs=pl.BlockSpec(memory_space=pltpu.VMEM),
        scratch_shapes=[
            pltpu.VMEM((slabs, 2, 2, block, width), low),
            pltpu.VMEM((slabs, 2, 2, block, width), low),
            pltpu.VMEM((slabs, 2, block, width), low),
            pltpu.VMEM((slabs, block, width), low),
            pltpu.VMEM((2, slabs, block, width), low),
            dma((slabs * 4,)),
            dma((slabs * 4,)),
            dma((slabs * 4,)),
            dma((slabs * SUM_CHUNKS * 2,)),
            dma((slabs * SUM_CHUNKS * 2,)),
            dma((slabs * SUM_CHUNKS,)),
            dma((slabs * SUM_CHUNKS,)),
            dma((slabs * SUM_CHUNKS,)),
            dma((slabs * SUM_CHUNKS * 2,)),
        ],
        compiler_params=pltpu.CompilerParams(
            collective_id=0, has_side_effects=True, vmem_limit_bytes=56 * 2**20
        ),
        cost_estimate=pl.CostEstimate(
            flops=rows.size, bytes_accessed=4 * rows.size, transcendentals=0
        ),
        name="sum_slabs",
    )(rows.reshape(slabs, 2, 2, 2, block, width))


def part_rows(block):
    tiles = block // 16
    one, two = tiles // 4, tiles // 2
    return [(0, one * 16), (one * 16, two * 16), ((one + two) * 16, (tiles - one - two) * 16)]


def digit(code, place):
    power = 1 + 9 * place + 81 * (place * (place - 1) // 2)
    power = power + 729 * (place * (place - 1) * (place - 2) // 6)
    return code // power % 10


def gather_kernel(
    shard_ref,
    bias_ref,
    main_ref,
    out_ref,
    bias_out_ref,
    main_out_ref,
    own_sem,
    send_sem,
    link_recv,
    core_recv,
    swap_send,
    swap_recv,
):
    block = shard_ref.shape[0]
    place, x = lax.axis_index("dp"), lax.axis_index("stream")
    c, y, z = place % 2, (place // 2) % 2, place // 4
    up, down, across, beside, sibling = range(5)
    devices = [(place + 4, x), (place - 4, x), (place, 1 - x), (place + 2 - 4 * y, x)]
    devices.append((place + 1 - 2 * c, x))
    parts = part_rows(block)
    order = [z] + [digit(code, z) for code in (2101, 1322, 33)]

    barrier = pltpu.get_barrier_semaphore()
    for way in (across, beside, sibling):
        pl.semaphore_signal(barrier, inc=1, device_id=devices[way], device_id_type=MESH)

    @pl.when(z < 3)
    def greet_above():
        pl.semaphore_signal(barrier, inc=1, device_id=devices[up], device_id_type=MESH)

    @pl.when(z > 0)
    def greet_below():
        pl.semaphore_signal(barrier, inc=1, device_id=devices[down], device_id_type=MESH)

    own = pltpu.make_async_copy(shard_ref, out_ref.at[z, y, c, x], own_sem.at[0])
    own.start()
    own_bias = pltpu.make_async_copy(bias_ref, bias_out_ref.at[z, y, c, x], own_sem.at[1])
    own_bias.start()
    pl.semaphore_wait(barrier, 4 + z * (3 - z) // 2)
    own.wait()
    own_bias.wait()

    def copy(way, zz, yy, xx, part, core=None):
        cc = c if core is None else core
        if part == 3:
            region = bias_out_ref.at[zz, yy, cc, xx]
        else:
            region = out_ref.at[zz, yy, cc, xx, pl.ds(*parts[part])]
        at = ((zz * 2 + yy) * 2 + xx) * 4 + part
        return pltpu.make_async_remote_copy(
            src_ref=region,
            dst_ref=region,
            send_sem=send_sem.at[way * 64 + at],
            recv_sem=core_recv.at[at] if way == sibling else link_recv.at[at],
            device_id=devices[way],
            device_id_type=MESH,
        )

    def came(zz, yy, xx, part):
        copy(across, zz, yy, xx, part).wait_recv()

    def along(zz, yy, xx, part):
        @pl.when((z < 3) & (zz <= z))
        def send_up():
            copy(up, zz, yy, xx, part).start()

        @pl.when((z > 0) & (zz >= z))
        def send_down():
            copy(down, zz, yy, xx, part).start()

    def early(k):
        zz = order[k]
        for part in range(2):
            if k > 0:
                came(zz, y, x, part)
            along(zz, y, x, part)
            for way in (beside, across) if part == 0 else (across, beside):
                copy(way, zz, y, x, part).start()
            copy(sibling, zz, y, x, part).start()

    def middle(k):
        zz = order[k]
        came(zz, 1 - y, x, 0)
        copy(across, zz, 1 - y, x, 0).start()
        came(zz, y, 1 - x, 1)
        copy(beside, zz, y, 1 - x, 1).start()
        copy(sibling, zz, 1 - y, x, 0).start()
        copy(sibling, zz, y, 1 - x, 1).start()

    def late(k):
        zz = order[k]
        for yy, xx, part in ((y, 1 - x, 0), (1 - y, x, 1), (1 - y, 1 - x, 0), (1 - y, 1 - x, 1)):
            came(zz, yy, xx, part)
            copy(sibling, zz, yy, xx, part).start()

    def last_own(k):
        for part in (2, 3):
            if k == 0:
                copy(across, z, y, x, part).start()
                copy(beside, z, y, x, part).start()
                regions = [(y, x)]
            elif k == 1:
                came(z, y, 1 - x, part)
                copy(beside, z, y, 1 - x, part).start()
                regions = [(y, 1 - x)]
            else:
                regions = [(1 - y, x), (1 - y, 1 - x)]
            for yy, xx in regions:
                if k == 2:
                    came(z, yy, xx, part)
                along(z, yy, xx, part)
                copy(sibling, z, yy, xx, part).start()

    def last(k):
        zz = order[k]
        for yy, xx in ((y, x), (y, 1 - x), (1 - y, x), (1 - y, 1 - x)):
            for part in (2, 3):
                came(zz, yy, xx, part)
                along(zz, yy, xx, part)
                copy(sibling, zz, yy, xx, part).start()

    swap = pltpu.make_async_remote_copy(
        src_ref=main_ref,
        dst_ref=main_out_ref,
        send_sem=swap_send,
        recv_sem=swap_recv,
        device_id=devices[across],
        device_id_type=MESH,
    )

    def swap_main(k):
        swap.start()

    for stage, k in (
        (early, 0),
        (last_own, 0),
        (last_own, 1),
        (swap_main, 0),
        (early, 1),
        (middle, 0),
        (last_own, 2),
        (early, 2),
        (middle, 1),
        (early, 3),
        (last, 1),
        (late, 0),
        (middle, 2),
        (last, 2),
        (late, 1),
        (middle, 3),
        (last, 3),
        (late, 2),
        (late, 3),
    ):
        stage(k)

    swap.wait()
    for zz in range(4):
        for yy in range(2):
            for xx in range(2):
                for part in range(4):
                    copy(sibling, zz, yy, xx, part, 1 - c).wait_recv()
                    copy(sibling, zz, yy, xx, part).wait_send()

    def sent_along(zz, yy, xx, part):
        @pl.when((z < 3) & (zz <= z))
        def sent_up():
            copy(up, zz, yy, xx, part).wait_send()

        @pl.when((z > 0) & (zz >= z))
        def sent_down():
            copy(down, zz, yy, xx, part).wait_send()

    for zz in range(4):
        for part in range(2):
            sent_along(zz, y, x, part)
            copy(beside, zz, y, x, part).wait_send()
            copy(across, zz, y, x, part).wait_send()
        copy(across, zz, 1 - y, x, 0).wait_send()
        copy(beside, zz, y, 1 - x, 1).wait_send()
        for yy in range(2):
            for xx in range(2):
                sent_along(zz, yy, xx, 2)
                sent_along(zz, yy, xx, 3)
    for part in (2, 3):
        copy(across, z, y, x, part).wait_send()
        copy(beside, z, y, x, part).wait_send()
        copy(beside, z, y, 1 - x, part).wait_send()


def gather_shards(shard, bias, main_rows):
    block, width = shard.shape
    tile = (16, LANES)
    bias_tile = jnp.pad(bias, (0, tile[0] * tile[1] - bias.shape[0])).reshape(tile)
    dma = pltpu.SemaphoreType.DMA
    place = pl.BlockSpec(memory_space=pl.ANY)
    gathered, biases, main_other = pl.pallas_call(
        gather_kernel,
        out_shape=[
            jax.ShapeDtypeStruct((4, 2, 2, 2, block, width), shard.dtype),
            jax.ShapeDtypeStruct((4, 2, 2, 2, *tile), bias.dtype),
            jax.ShapeDtypeStruct(main_rows.shape, main_rows.dtype),
        ],
        in_specs=[place] * 3,
        out_specs=[place] * 3,
        scratch_shapes=[dma((2,)), dma((320,)), dma((64,)), dma((64,)), dma, dma],
        compiler_params=pltpu.CompilerParams(
            collective_id=1, has_side_effects=True, vmem_limit_bytes=56 * 2**20
        ),
        cost_estimate=pl.CostEstimate(
            flops=0, bytes_accessed=64 * shard.size, transcendentals=0
        ),
        name="gather_shards",
    )(shard, bias_tile, main_rows)
    biases = biases.reshape(32, tile[0] * tile[1])[:, : bias.shape[0]].reshape(-1)
    return gathered.reshape(32 * block, width), biases, main_other


def pre_kernel(grad_ref, weight_ref, slope_ref, pre_ref, sum_ref):
    for at in range(0, weight_ref.shape[0], FFN_PART):
        part = slice(at, at + FFN_PART)
        pre = (
            dot_rows(grad_ref[...], weight_ref[part, :]) * slope_ref[:, part].astype(jnp.float32)
        ).astype(jnp.bfloat16)
        pre_ref[:, part] = pre
        sum_ref[:, part] = jnp.sum(pre.astype(jnp.float32), axis=0, keepdims=True)


def pre_and_sum(grad, weight, slope):
    count, depth = grad.shape
    width = weight.shape[0]
    columns = pl.BlockSpec((count, FFN_TILE), lambda tile: (0, tile))
    vector = pl.BlockSpec((1, FFN_TILE), lambda tile: (0, tile))
    pre, total = pl.pallas_call(
        pre_kernel,
        grid=(width // FFN_TILE,),
        in_specs=[
            pl.BlockSpec((count, depth), lambda tile: (0, 0)),
            pl.BlockSpec((FFN_TILE, depth), lambda tile: (tile, 0)),
            columns,
        ],
        out_specs=[columns, vector],
        out_shape=[
            jax.ShapeDtypeStruct((count, width), jnp.bfloat16),
            jax.ShapeDtypeStruct((1, width), jnp.float32),
        ],
        compiler_params=pltpu.CompilerParams(vmem_limit_bytes=56 * 2**20),
        cost_estimate=pl.CostEstimate(
            flops=2 * count * depth * width,
            bytes_accessed=2 * (count * depth + depth * width + 2 * count * width),
            transcendentals=0,
        ),
        name="pre_and_sum",
    )(grad, weight, slope)
    return pre, total[0]


def local(
    dp_count,
    main_rows,
    pred_rows,
    enc_rows,
    doc_lengths,
    main_cotangent,
    pred_cotangent,
    proj_master,
    proj_first,
    proj_second,
    bias_master,
    bias_first,
    bias_second,
    down_master,
    down_first,
    down_second,
    small_master,
    small_first,
    small_second,
):
    devices = 2 * dp_count
    rel_width = BUCKETS * HEADS
    cross_start = 4 * D + rel_width
    half_rows = main_rows.shape[0]
    group_rows = pred_rows.shape[0]

    bias_low = bias_master.astype(jnp.bfloat16)
    proj_low = proj_master.astype(jnp.bfloat16).T
    if dp_count == 16:
        proj_rows, bias_low, main_other = gather_shards(proj_low, bias_low, main_rows)
    else:
        proj_rows = lax.all_gather(proj_low, ("dp", "stream"), axis=0, tiled=True)
        bias_low = to_all(bias_low, devices)
        main_other = swap_streams(main_rows)
    down_low = lax.optimization_barrier((down_master.astype(jnp.bfloat16), proj_rows))[0]
    down_weight = lax.all_gather(down_low, ("dp", "stream"), axis=0, tiled=True)
    bias_wide = bias_low.astype(jnp.float32)
    query_weight = proj_rows[0:D]
    keys_weight = proj_rows[D : 3 * D]
    out_weight = proj_rows[3 * D : 4 * D]
    table_weight = (
        proj_rows[4 * D : cross_start]
        .reshape(BUCKETS, HEADS, D)
        .transpose(1, 0, 2)
        .reshape(rel_width, D)
    )
    cross_weight = proj_rows[cross_start : cross_start + D]
    pair_weight = proj_rows[cross_start + D : cross_start + 3 * D]
    back_weight = proj_rows[cross_start + 3 * D : cross_start + 4 * D]
    up_weight = proj_rows[cross_start + 4 * D :]
    query_bias = bias_wide[0:D]
    value_bias = bias_wide[D : 2 * D]
    out_bias = bias_wide[2 * D : 3 * D]
    table_bias = bias_wide[3 * D : 3 * D + rel_width].reshape(BUCKETS, HEADS).T.reshape(rel_width)
    cross_bias = bias_wide[3 * D + rel_width : 4 * D + rel_width]
    pair_bias = bias_wide[4 * D + rel_width : 5 * D + rel_width]
    back_bias = bias_wide[5 * D + rel_width : 6 * D + rel_width]
    up_bias = bias_wide[6 * D + rel_width :]
    zero_bias = jnp.zeros((D,), jnp.float32)

    main_start = lax.axis_index("stream") * half_rows
    places = jnp.arange(group_rows, dtype=jnp.int32)
    group_docs = doc_ids(doc_lengths[0], group_rows)
    query_docs = jnp.concatenate(
        [lax.dynamic_slice_in_dim(group_docs, main_start, half_rows), group_docs]
    )
    query_places = jnp.concatenate([main_start + jnp.arange(half_rows, dtype=jnp.int32), places])
    main_flag = jnp.arange(half_rows + group_rows, dtype=jnp.int32) < half_rows
    same_doc = query_docs[:, None] == group_docs[None, :]
    distance = query_places[:, None] - places[None, :]
    allowed = same_doc & ((distance > 0) | (distance == 0) & main_flag[:, None])
    self_mask = jnp.where(allowed, 0.0, MASKED)
    cross_mask = jnp.where(same_doc, 0.0, MASKED)
    lane = jnp.arange(LANES, dtype=jnp.int32)
    turn = jnp.mod(query_places[:, None] - lane[None, :], LANES)
    spread = bucket_of(turn)
    edge = jnp.broadcast_to(query_places[:, None] - LANES, turn.shape)

    main_all = both_parts(main_rows, main_other)
    inputs = jnp.concatenate([main_rows, pred_rows], axis=0)
    key_inputs = jnp.concatenate([main_all, pred_rows], axis=0)
    input_values = inputs.astype(jnp.float32)
    query_low = (times_transpose(inputs, query_weight) + query_bias).astype(jnp.bfloat16)
    self_pairs = (
        times_transpose(key_inputs, keys_weight) + jnp.concatenate([zero_bias, value_bias])
    ).astype(jnp.bfloat16)
    table = times_transpose(inputs, table_weight) + table_bias
    context_low, self_log = self_forward(query_low, self_pairs, table, spread, edge, self_mask)
    enc_other = swap_streams(enc_rows) + jnp.bfloat16(0.0) * context_low[0:1, 0:1]
    enc_all = both_parts(enc_rows, enc_other)
    cross_pairs = (
        times_transpose(enc_all, pair_weight) + jnp.concatenate([zero_bias, pair_bias])
    ).astype(jnp.bfloat16)
    norm_one_in = input_values + times_transpose(context_low, out_weight) + out_bias
    stats_one = norm_stats(norm_one_in)
    hidden_one = (norm_one_in - stats_one[0]) * stats_one[1] * small_master[1] + small_master[4]
    one_low = hidden_one.astype(jnp.bfloat16)

    cross_query = (times_transpose(one_low, cross_weight) + cross_bias).astype(jnp.bfloat16)
    cross_low, cross_log = cross_forward(cross_query, cross_pairs, cross_mask)
    norm_two_in = hidden_one + times_transpose(cross_low, back_weight) + back_bias
    stats_two = norm_stats(norm_two_in)
    hidden_two = (norm_two_in - stats_two[0]) * stats_two[1] * small_master[2] + small_master[5]
    two_low = hidden_two.astype(jnp.bfloat16)

    active, slope = gelu_and_slope(times_transpose(two_low, up_weight) + up_bias)
    active_low = active.astype(jnp.bfloat16)
    slope_low = slope.astype(jnp.bfloat16)
    norm_three_in = hidden_two + matmul(active_low, down_weight) + small_master[0]
    stats_three = norm_stats(norm_three_in)
    final_rows = (
        (norm_three_in - stats_three[0]) * stats_three[1] * small_master[3] + small_master[6]
    ).astype(jnp.bfloat16)

    cotangent = jnp.concatenate([main_cotangent, pred_cotangent], axis=0).astype(jnp.float32)
    sum_three, gain_three, shift_three = norm_back(
        norm_three_in, stats_three, small_master[3], cotangent
    )
    ffn_grad = sum_three.astype(jnp.bfloat16)
    slab = proj_rows.shape[0] // 4
    down_part = sum_shares(column_sums(active_low, ffn_grad))
    pre_grad, pre_sum = pre_and_sum(ffn_grad, down_weight, slope_low)
    up_cut = 3 * slab - cross_start - 4 * D
    up_part = sum_shares(column_sums(pre_grad, two_low))
    two_grad = sum_three + matmul(pre_grad, up_weight)

    sum_two, gain_two, shift_two = norm_back(norm_two_in, stats_two, small_master[2], two_grad)
    branch_grad = sum_two.astype(jnp.bfloat16)
    cross_low_grad = matmul(branch_grad, back_weight).astype(jnp.bfloat16)
    cquery_grad, ckey_grad, cvalue_grad = cross_backward(
        cross_query, cross_pairs, cross_mask, cross_log, cross_low_grad
    )
    enc_grad = pair_sum(matmul(ckey_grad, pair_weight[:D]) + matmul(cvalue_grad, pair_weight[D:]))
    one_grad = sum_two + matmul(cquery_grad, cross_weight)

    sum_one, gain_one, shift_one = norm_back(norm_one_in, stats_one, small_master[1], one_grad)
    attn_grad = sum_one.astype(jnp.bfloat16)
    context_grad = matmul(attn_grad, out_weight).astype(jnp.bfloat16)
    query_grad, key_grad, value_grad, table_wide = self_backward(
        query_low, self_pairs, table, spread, edge, turn, self_mask, self_log, context_grad
    )
    table_wide = lax.optimization_barrier((table_wide, down_part))[0]
    table_grad = table_wide.astype(jnp.bfloat16)
    table_rows = (
        column_sums(table_grad, inputs)
        .reshape(HEADS, BUCKETS, D)
        .transpose(1, 0, 2)
        .reshape(rel_width, D)
    )
    late_rows = jnp.concatenate(
        [
            column_sums(query_grad, inputs),
            column_sums(key_grad, key_inputs),
            column_sums(value_grad, key_inputs),
            column_sums(attn_grad, context_low),
            table_rows,
            column_sums(cquery_grad, one_low),
            column_sums(ckey_grad, enc_all),
            column_sums(cvalue_grad, enc_all),
            column_sums(branch_grad, cross_low),
            column_sums(pre_grad[:, :up_cut], two_low),
        ]
    )
    pair_input_grad = matmul(key_grad, keys_weight[:D]) + matmul(value_grad, keys_weight[D:])
    query_input_grad = (
        sum_one + matmul(query_grad, query_weight) + matmul(table_grad, table_weight)
    )
    main_grad = query_input_grad[:half_rows] + pair_sum(pair_input_grad[:group_rows])
    pred_grad = query_input_grad[half_rows:] + pair_input_grad[group_rows:]

    def row_sum(rows):
        return jnp.sum(rows, axis=0, dtype=jnp.float32)

    bias_parts = jnp.concatenate(
        [
            row_sum(query_grad),
            row_sum(value_grad),
            row_sum(attn_grad),
            row_sum(table_grad).reshape(HEADS, BUCKETS).T.reshape(rel_width),
            row_sum(cquery_grad),
            row_sum(cvalue_grad),
            row_sum(branch_grad),
            pre_sum,
        ]
    )
    small_parts = jnp.concatenate(
        [row_sum(ffn_grad), gain_one, gain_two, gain_three, shift_one, shift_two, shift_three]
    )
    vector_sum = lax.psum(jnp.concatenate([bias_parts, small_parts]), ("dp", "stream"))
    slab_three = to_last_quarter(up_part, devices, up_cut)
    late_rows = lax.optimization_barrier((late_rows, slab_three))[0]
    if dp_count == 16:
        late_sum = sum_slabs(late_rows, 3)
    else:
        late_sum = Scatter(late_rows, range(3), dp_count).finish()
    vector_sum = vector_sum + 0.0 * late_sum[0, 0]
    device = lax.axis_index("dp") * 2 + lax.axis_index("stream")
    bias_len = bias_master.shape[0]
    bias_grad = lax.dynamic_slice_in_dim(vector_sum, device * bias_len, bias_len)
    small_grad = vector_sum[devices * bias_len :].reshape(small_master.shape)
    outer = place_on(("dp", dp_count // 4, 4))
    proj_grad = jnp.where(outer == 3, slab_three.astype(jnp.float32), late_sum).T
    down_grad = down_part.astype(jnp.float32)
    return (
        final_rows[:half_rows],
        final_rows[half_rows:],
        main_grad.astype(jnp.bfloat16),
        pred_grad.astype(jnp.bfloat16),
        enc_grad.astype(jnp.bfloat16),
        *adam_step(proj_master, proj_first, proj_second, proj_grad, RATE_MATRIX, WEIGHT_DECAY),
        *adam_step(bias_master, bias_first, bias_second, bias_grad, RATE_VECTOR, 0.0),
        *adam_step(down_master, down_first, down_second, down_grad, RATE_MATRIX, WEIGHT_DECAY),
        *adam_step(small_master, small_first, small_second, small_grad, RATE_SMALL, 0.0),
    )


def solution(mesh):
    rows = P(("dp", "stream"), None)
    columns = P(None, ("dp", "stream"))
    vector = P(("dp", "stream"))
    masters = (columns,) * 3 + (vector,) * 3 + (rows,) * 3 + (P(),) * 3
    return jax.shard_map(
        partial(local, mesh.shape["dp"]),
        mesh=mesh,
        in_specs=(rows, rows, rows, P("dp", None), rows, rows) + masters,
        out_specs=(rows,) * 5 + masters,
        check_vma=False,
    )
```

```python
from functools import partial
import math

import jax
import jax.numpy as jnp
from jax import lax
from jax.experimental import pallas as pl
from jax.experimental.pallas import tpu as pltpu
from jax.sharding import PartitionSpec as P

D = 1024
HEADS = 16
BUCKETS = 32
STEP = 10
HEAD_DIM = 64
LANES = 128
CHUNK = 128
SCORE_SCALE = HEAD_DIM**-0.5

NORM_EPS = 1e-05
BETA_FIRST = 0.9
BETA_SECOND = 0.999
ADAM_EPS = 1e-08
RATE_MATRIX = 0.04
RATE_VECTOR = 0.15
RATE_SMALL = 0.5
WEIGHT_DECAY = 0.01
MASKED = -1e30
SUM_WAVES = 4
SUM_CHUNKS = 2 * SUM_WAVES
FFN_TILE = 1024
FFN_PART = 256
MESH = pl.DeviceIdType.MESH


def bucket_edges():
    return [int(math.ceil(16.0 * 8.0 ** (step_index / 16.0))) for step_index in range(1, 16)]


def bucket_of(distance):
    counted = jnp.zeros_like(distance)
    for threshold in bucket_edges():
        counted = counted + (distance >= threshold).astype(jnp.int32)
    return jnp.where(distance < 16, distance, 16 + counted)


def doc_ids(lengths, length_total):
    doc_ends = jnp.cumsum(lengths)
    places = jnp.arange(length_total, dtype=jnp.int32)
    return jnp.sum((places[:, None] >= doc_ends[None, :]).astype(jnp.int32), axis=1)


def matmul(left_side, right_side):
    return jnp.dot(left_side, right_side, preferred_element_type=jnp.float32)


def outer_sum(left_side, right_side):
    return lax.dot_general(
        left_side, right_side, (((0,), (0,)), ((), ())), preferred_element_type=jnp.float32
    )


def times_transpose(left_side, right_side):
    return lax.dot_general(
        left_side, right_side, (((1,), (1,)), ((), ())), preferred_element_type=jnp.float32
    )


def norm_stats(hidden):
    mean = jnp.mean(hidden, axis=-1, keepdims=True)
    centre = hidden - mean
    spread = jnp.mean(centre * centre, axis=-1, keepdims=True)
    return mean, lax.rsqrt(spread + NORM_EPS)


def norm_back(hidden, stats, gain_row, grad):
    mean, inverse = stats
    normed = (hidden - mean) * inverse
    scaled = grad * gain_row
    first = jnp.mean(scaled, axis=-1, keepdims=True)
    second = jnp.mean(scaled * normed, axis=-1, keepdims=True)
    hidden_grad = (scaled - first - normed * second) * inverse
    return hidden_grad, jnp.sum(grad * normed, axis=0), jnp.sum(grad, axis=0)


def gelu_and_slope(values):
    size = jnp.abs(values) * (0.5**0.5)
    place = 1.0 / (1.0 + 0.3275911 * size)
    fit = 1.061405429
    for coefficient in (-1.453152027, 1.421413741, -0.284496736, 0.254829592):
        fit = fit * place + coefficient
    bell = jnp.exp(-size * size)
    tail = (0.5 * place) * (fit * bell)
    below = jnp.where(values >= 0.0, 1.0 - tail, tail)
    return values * below, below + values * bell * (1.0 / math.sqrt(2.0 * math.pi))


def dot_rows(left_side, right_side):
    return lax.dot_general(
        left_side, right_side, (((1,), (1,)), ((), ())), preferred_element_type=jnp.float32
    )


def lookup(table, index):
    return jnp.take_along_axis(table, index, axis=1, mode="promise_in_bounds")


def wide(column):
    return jnp.broadcast_to(column, (column.shape[0], LANES))


def tiled(block, key_count):
    return jnp.concatenate([block] * (key_count // LANES), axis=1)


def row_blocks(main_count, key_count, size):
    blocks = [(at, min(size, main_count - at), key_count) for at in range(0, main_count, size)]
    step = min(size, LANES)
    for at in range(0, key_count, step):
        seen = min(key_count, (at + step + LANES - 1) // LANES * LANES)
        blocks.append((main_count + at, min(step, key_count - at), seen))
    return blocks


def bias_of(near_bias, far_bias, edge, row_count, key_count):
    lane = lax.broadcasted_iota(jnp.int32, (row_count, LANES), 1)
    return jnp.concatenate(
        [
            jnp.where(lane + at > edge, near_bias, far_bias)
            for at in range(0, key_count, LANES)
        ],
        axis=1,
    )


def both_halves(block, head):
    lane = lax.broadcasted_iota(jnp.int32, block.shape, 1)
    turned = pltpu.roll(block, HEAD_DIM, 1)
    return jnp.where((lane < HEAD_DIM) == (head == 0), block, turned)


def in_turns(works):
    while any([next(work, works) is not works for work in works]):
        pass


def self_forward_kernel(
    query_ref,
    key_ref,
    value_ref,
    own_key_ref,
    own_value_ref,
    table_ref,
    spread_ref,
    edge_ref,
    mask_ref,
    context_ref,
    log_ref,
    score_ref,
    prob_ref,
    near_ref,
    far_ref,
):
    rows, key_count = mask_ref.shape
    main_count = rows - key_count
    parity = lax.rem(pl.program_id(0), 2)
    groups = row_blocks(main_count, key_count, 512)
    chunks = row_blocks(main_count, key_count, CHUNK)
    for head in range(2):
        at = head * HEAD_DIM
        head_lanes = slice(at, at + HEAD_DIM)
        first = (parity * 2 + head) * BUCKETS
        query = query_ref[:, head_lanes] * jnp.bfloat16(SCORE_SCALE)
        keys = key_ref[:, head_lanes]
        values = value_ref[:, head_lanes]
        own_keys = own_key_ref[:, head_lanes].astype(jnp.float32)
        own_values = own_value_ref[:, head_lanes].astype(jnp.float32)
        near_ref[head] = lookup(table_ref[...], spread_ref[...] + first)
        far_ref[head] = lookup(
            table_ref[...], jnp.full((rows, LANES), first + BUCKETS - 1, jnp.int32)
        )
        own_score = wide(
            jnp.sum(query[main_count:].astype(jnp.float32) * own_keys, axis=1, keepdims=True)
        ) + lookup(table_ref[main_count:, :], jnp.full((key_count, LANES), first, jnp.int32))
        for row, count, seen in groups:
            score_ref[head, row : row + count, 0:seen] = dot_rows(
                query[row : row + count], keys[0:seen]
            )
        tops = []
        for row, count, seen in chunks:
            part = slice(row, row + count)
            scores = (
                score_ref[head, part, 0:seen]
                + bias_of(near_ref[head, part], far_ref[head, part], edge_ref[part], count, seen)
                + mask_ref[part, 0:seen]
            )
            score_ref[head, part, 0:seen] = scores
            tops.append(wide(jnp.max(scores, axis=1, keepdims=True)))
        top = jnp.concatenate(tops, axis=0)
        top = jnp.concatenate(
            [top[:main_count], jnp.maximum(top[main_count:], own_score)], axis=0
        )
        own_weight = jnp.exp(own_score - top[main_count:])
        totals = []
        for row, count, seen in chunks:
            part = slice(row, row + count)
            weights = jnp.exp(score_ref[head, part, 0:seen] - tiled(top[part], seen))
            score_ref[head, part, 0:seen] = weights
            totals.append(wide(jnp.sum(weights, axis=1, keepdims=True)))
        total = jnp.concatenate(totals, axis=0)
        total = jnp.concatenate([total[:main_count], total[main_count:] + own_weight], axis=0)
        inverse = 1.0 / total
        log_ref[:, head_lanes] = (top + jnp.log(total))[:, 0:HEAD_DIM]
        own_prob = (own_weight * inverse[main_count:]).astype(jnp.bfloat16).astype(jnp.float32)
        for row, count, seen in chunks:
            part = slice(row, row + count)
            prob_ref[head, part, 0:seen] = (
                score_ref[head, part, 0:seen] * tiled(inverse[part], seen)
            ).astype(jnp.bfloat16)
        for row, count, seen in groups:
            part = slice(row, row + count)
            context = matmul(prob_ref[head, part, 0:seen], values[0:seen])
            if row >= main_count:
                own = slice(row - main_count, row - main_count + count)
                context = context + own_prob[own, 0:HEAD_DIM] * own_values[own]
            context_ref[part, head_lanes] = context.astype(jnp.bfloat16)


def self_backward_kernel(
    query_ref,
    key_ref,
    value_ref,
    own_key_ref,
    own_value_ref,
    table_ref,
    spread_ref,
    edge_ref,
    turn_ref,
    mask_ref,
    log_ref,
    context_ref,
    query_grad_ref,
    key_grad_ref,
    value_grad_ref,
    table_grad_ref,
    score_ref,
    prob_grad_ref,
    prob_ref,
    score_grad_ref,
    near_ref,
    far_ref,
    close_ref,
    rest_ref,
):
    rows, key_count = mask_ref.shape
    main_count = rows - key_count
    parity = lax.rem(pl.program_id(0), 2)
    groups = row_blocks(main_count, key_count, 512)
    chunks = row_blocks(main_count, key_count, CHUNK)
    bucket = bucket_of(lax.broadcasted_iota(jnp.int32, (LANES, LANES), 0))
    bucket_lane = lax.broadcasted_iota(jnp.int32, (LANES, LANES), 1)
    row_lane = lax.broadcasted_iota(jnp.int32, (rows, LANES), 1)
    table_total = jnp.zeros((rows, LANES), jnp.float32)
    own_total = jnp.zeros((key_count, LANES), jnp.float32)
    for head in range(2):
        at = head * HEAD_DIM
        head_lanes = slice(at, at + HEAD_DIM)
        first = (parity * 2 + head) * BUCKETS
        query = query_ref[:, head_lanes] * jnp.bfloat16(SCORE_SCALE)
        keys = key_ref[:, head_lanes]
        values = value_ref[:, head_lanes]
        context = context_ref[:, head_lanes]
        own_keys = own_key_ref[:, head_lanes].astype(jnp.float32)
        own_values = own_value_ref[:, head_lanes].astype(jnp.float32)
        own_query = query[main_count:].astype(jnp.float32)
        own_context = context[main_count:].astype(jnp.float32)
        near_ref[head] = lookup(table_ref[...], spread_ref[...] + first)
        far_ref[head] = lookup(
            table_ref[...], jnp.full((rows, LANES), first + BUCKETS - 1, jnp.int32)
        )
        own_score = wide(jnp.sum(own_query * own_keys, axis=1, keepdims=True)) + lookup(
            table_ref[main_count:, :], jnp.full((key_count, LANES), first, jnp.int32)
        )
        log_total = both_halves(log_ref[...], head)
        own_prob = jnp.exp(own_score - log_total[main_count:])
        own_prob_grad = wide(jnp.sum(own_context * own_values, axis=1, keepdims=True))
        value_grad_ref[key_count:, head_lanes] = (
            own_prob[:, 0:HEAD_DIM].astype(jnp.bfloat16).astype(jnp.float32) * own_context
        ).astype(jnp.bfloat16)
        for row, count, seen in groups:
            part = slice(row, row + count)
            score_ref[head, part, 0:seen] = dot_rows(query[part], keys[0:seen])
            prob_grad_ref[head, part, 0:seen] = dot_rows(context[part], values[0:seen])
        row_dots = []
        for row, count, seen in chunks:
            part = slice(row, row + count)
            edge = edge_ref[part]
            bias = bias_of(near_ref[head, part], far_ref[head, part], edge, count, seen)
            probs = jnp.exp(
                score_ref[head, part, 0:seen]
                + bias
                + (mask_ref[part, 0:seen] - tiled(log_total[part], seen))
            )
            prob_grad = prob_grad_ref[head, part, 0:seen]
            row_dot = wide(jnp.sum(probs * prob_grad, axis=1, keepdims=True))
            if row >= main_count:
                own = slice(row - main_count, row - main_count + count)
                row_dot = row_dot + own_prob[own] * own_prob_grad[own]
                row_dots.append(row_dot)
            score_grad = (probs * (prob_grad - tiled(row_dot, seen))).astype(jnp.bfloat16)
            prob_ref[head, part, 0:seen] = probs.astype(jnp.bfloat16)
            score_grad_ref[head, part, 0:seen] = score_grad
            score_wide = score_grad.astype(jnp.float32)
            lane = lax.broadcasted_iota(jnp.int32, (count, LANES), 1)
            close = jnp.zeros((count, LANES), jnp.float32)
            whole = jnp.zeros((count, LANES), jnp.float32)
            for at_key in range(0, seen, LANES):
                block = score_wide[:, at_key : at_key + LANES]
                whole = whole + block
                close = close + jnp.where(lane + at_key > edge, block, 0.0)
            close_ref[head, part] = close
            rest_ref[head, part] = whole - close
        own_grad = (
            (own_prob * (own_prob_grad - jnp.concatenate(row_dots, axis=0)))
            .astype(jnp.bfloat16)
            .astype(jnp.float32)
        )
        key_grad_ref[key_count:, head_lanes] = (own_grad[:, 0:HEAD_DIM] * own_query).astype(
            jnp.bfloat16
        )
        turned = lookup(close_ref[head], turn_ref[...]).astype(jnp.bfloat16)
        table_total = table_total + matmul(
            turned, (bucket_lane == bucket + first).astype(jnp.bfloat16)
        )
        table_total = table_total + jnp.where(
            row_lane == first + BUCKETS - 1, jnp.sum(rest_ref[head], axis=1, keepdims=True), 0.0
        )
        own_total = own_total + jnp.where(row_lane[main_count:] == first, own_grad, 0.0)
        for row, count, seen in groups:
            part = slice(row, row + count)
            query_grad = matmul(score_grad_ref[head, part, 0:seen], keys[0:seen])
            if row >= main_count:
                own = slice(row - main_count, row - main_count + count)
                query_grad = query_grad + own_grad[own, 0:HEAD_DIM] * own_keys[own]
            query_grad_ref[part, head_lanes] = (query_grad * SCORE_SCALE).astype(jnp.bfloat16)
        for at_key in range(0, key_count, LANES):
            block = slice(at_key, at_key + LANES)
            later = slice(main_count + at_key, rows)
            key_grad_ref[block, head_lanes] = (
                outer_sum(score_grad_ref[head, 0:main_count, block], query[0:main_count])
                + outer_sum(score_grad_ref[head, later, block], query[later])
            ).astype(jnp.bfloat16)
            value_grad_ref[block, head_lanes] = (
                outer_sum(prob_ref[head, 0:main_count, block], context[0:main_count])
                + outer_sum(prob_ref[head, later, block], context[later])
            ).astype(jnp.bfloat16)
    table_total = jnp.concatenate(
        [table_total[:main_count], table_total[main_count:] + own_total], axis=0
    )

    @pl.when(parity == 0)
    def first_pair():
        table_grad_ref[...] = table_total

    @pl.when(parity == 1)
    def second_pair():
        table_grad_ref[...] += table_total


def cross_forward_kernel(
    query_ref, key_ref, value_ref, mask_ref, context_ref, log_ref, score_ref, prob_ref
):
    rows = mask_ref.shape[0]
    def head_steps(head):
        at = head * HEAD_DIM
        head_lanes = slice(at, at + HEAD_DIM)
        query = query_ref[:, head_lanes] * jnp.bfloat16(SCORE_SCALE)
        score_ref[head] = dot_rows(query, key_ref[:, head_lanes])
        yield
        for row in range(0, rows, CHUNK):
            part = slice(row, min(row + CHUNK, rows))
            scores = score_ref[head, part] + mask_ref[part]
            top = jnp.max(scores, axis=1, keepdims=True)
            weights = jnp.exp(scores - top)
            total = jnp.sum(weights, axis=1, keepdims=True)
            prob_ref[head, part] = (weights * (1.0 / total)).astype(jnp.bfloat16)
            log_ref[part, head_lanes] = jnp.broadcast_to(
                top + jnp.log(total), (scores.shape[0], HEAD_DIM)
            )
        context_ref[:, head_lanes] = matmul(prob_ref[head], value_ref[:, head_lanes]).astype(
            jnp.bfloat16
        )
        yield

    in_turns([head_steps(head) for head in range(2)])


def cross_backward_kernel(
    query_ref,
    key_ref,
    value_ref,
    mask_ref,
    log_ref,
    context_ref,
    query_grad_ref,
    key_grad_ref,
    value_grad_ref,
    score_ref,
    prob_grad_ref,
    prob_ref,
    score_grad_ref,
):
    rows = mask_ref.shape[0]
    def head_steps(head):
        at = head * HEAD_DIM
        head_lanes = slice(at, at + HEAD_DIM)
        query = query_ref[:, head_lanes] * jnp.bfloat16(SCORE_SCALE)
        keys = key_ref[:, head_lanes]
        context = context_ref[:, head_lanes]
        score_ref[head] = dot_rows(query, keys)
        prob_grad_ref[head] = dot_rows(context, value_ref[:, head_lanes])
        yield
        for row in range(0, rows, CHUNK):
            part = slice(row, min(row + CHUNK, rows))
            probs = jnp.exp(
                score_ref[head, part] + (mask_ref[part] - log_ref[part, at : at + 1])
            )
            prob_grad = prob_grad_ref[head, part]
            row_dot = jnp.sum(probs * prob_grad, axis=1, keepdims=True)
            prob_ref[head, part] = probs.astype(jnp.bfloat16)
            score_grad_ref[head, part] = (probs * (prob_grad - row_dot)).astype(jnp.bfloat16)
        yield
        query_grad_ref[:, head_lanes] = (matmul(score_grad_ref[head], keys) * SCORE_SCALE).astype(
            jnp.bfloat16
        )
        key_grad_ref[:, head_lanes] = outer_sum(query, score_grad_ref[head]).T.astype(jnp.bfloat16)
        value_grad_ref[:, head_lanes] = outer_sum(context, prob_ref[head]).T.astype(jnp.bfloat16)
        yield

    in_turns([head_steps(head) for head in range(2)])


def pair_block(row_count, row_block=0, first_pair=0):
    return pl.BlockSpec((row_count, LANES), lambda pair: (row_block, first_pair + pair))


def whole_block(shape):
    return pl.BlockSpec(shape, lambda pair: (0, 0))


def attention_call(kernel, name, in_specs, out_specs, out_shape, scratch, arrays, flops, passes):
    moved = sum(array.size * array.dtype.itemsize for array in arrays)
    moved += sum(math.prod(shape.shape) * shape.dtype.itemsize for shape in out_shape)
    return pl.pallas_call(
        kernel,
        grid=(HEADS // 2,),
        in_specs=in_specs,
        out_specs=out_specs,
        out_shape=out_shape,
        scratch_shapes=scratch,
        compiler_params=pltpu.CompilerParams(vmem_limit_bytes=56 * 2**20),
        cost_estimate=pl.CostEstimate(flops=flops, bytes_accessed=moved, transcendentals=passes),
        name=name,
    )(*arrays)


def low_array(row_count):
    return jax.ShapeDtypeStruct((row_count, D), jnp.bfloat16)


def self_forward(query, pairs, table, spread, edge, mask):
    rows, keys = mask.shape
    width = D // LANES
    square = pltpu.VMEM((2, rows, keys), jnp.float32)
    narrow = pltpu.VMEM((2, rows, LANES), jnp.float32)
    return attention_call(
        self_forward_kernel,
        "self_forward",
        [
            pair_block(rows),
            pair_block(keys),
            pair_block(keys, 0, width),
            pair_block(keys, 1),
            pair_block(keys, 1, width),
            pl.BlockSpec((rows, LANES), lambda pair: (0, pair // 2)),
            whole_block((rows, LANES)),
            whole_block((rows, LANES)),
            whole_block((rows, keys)),
        ],
        [pair_block(rows), pair_block(rows)],
        [low_array(rows), jax.ShapeDtypeStruct((rows, D), jnp.float32)],
        [square, pltpu.VMEM((2, rows, keys), jnp.bfloat16), narrow, narrow],
        (query, pairs, pairs, pairs, pairs, table, spread, edge, mask),
        4 * rows * keys * D,
        rows * keys * HEADS,
    )


def self_backward(query, pairs, table, spread, edge, turn, mask, log_total, context_grad):
    rows, keys = mask.shape
    width = D // LANES
    square = pltpu.VMEM((2, rows, keys), jnp.float32)
    square_low = pltpu.VMEM((2, rows, keys), jnp.bfloat16)
    narrow = pltpu.VMEM((2, rows, LANES), jnp.float32)
    table_block = pl.BlockSpec((rows, LANES), lambda pair: (0, pair // 2))
    return attention_call(
        self_backward_kernel,
        "self_backward",
        [
            pair_block(rows),
            pair_block(keys),
            pair_block(keys, 0, width),
            pair_block(keys, 1),
            pair_block(keys, 1, width),
            table_block,
            whole_block((rows, LANES)),
            whole_block((rows, LANES)),
            whole_block((rows, LANES)),
            whole_block((rows, keys)),
            pair_block(rows),
            pair_block(rows),
        ],
        [pair_block(rows), pair_block(2 * keys), pair_block(2 * keys), table_block],
        [
            low_array(rows),
            low_array(2 * keys),
            low_array(2 * keys),
            jax.ShapeDtypeStruct(table.shape, jnp.float32),
        ],
        [square, square, square_low, square_low, narrow, narrow, narrow, narrow],
        (query, pairs, pairs, pairs, pairs, table, spread, edge, turn, mask, log_total, context_grad),
        10 * rows * keys * D,
        rows * keys * HEADS,
    )


def cross_forward(query, pairs, mask):
    rows, keys = mask.shape
    return attention_call(
        cross_forward_kernel,
        "cross_forward",
        [
            pair_block(rows),
            pair_block(keys),
            pair_block(keys, 0, D // LANES),
            whole_block((rows, keys)),
        ],
        [pair_block(rows), pair_block(rows)],
        [low_array(rows), jax.ShapeDtypeStruct((rows, D), jnp.float32)],
        [pltpu.VMEM((2, rows, keys), jnp.float32), pltpu.VMEM((2, rows, keys), jnp.bfloat16)],
        (query, pairs, pairs, mask),
        4 * rows * keys * D,
        rows * keys * HEADS,
    )


def cross_backward(query, pairs, mask, log_total, context_grad):
    rows, keys = mask.shape
    square = pltpu.VMEM((2, rows, keys), jnp.float32)
    square_low = pltpu.VMEM((2, rows, keys), jnp.bfloat16)
    return attention_call(
        cross_backward_kernel,
        "cross_backward",
        [
            pair_block(rows),
            pair_block(keys),
            pair_block(keys, 0, D // LANES),
            whole_block((rows, keys)),
            pair_block(rows),
            pair_block(rows),
        ],
        [pair_block(rows), pair_block(keys), pair_block(keys)],
        [low_array(rows), low_array(keys), low_array(keys)],
        [square, square, square_low, square_low],
        (query, pairs, pairs, mask, log_total, context_grad),
        10 * rows * keys * D,
        rows * keys * HEADS,
    )


def column_sums(left_side, right_side):
    return outer_sum(left_side, right_side).astype(jnp.bfloat16)


def inner_levels(dp_count):
    levels = [("dp", 1, 2), ("stream", 1, 2)]
    if dp_count == 64:
        return levels + [("dp", 2, 2), ("dp", 4, 4)]
    return levels + [("dp", 2, 2)]


def rotation(level, shift, dp_count):
    axis, stride, size = level
    total = 2 if axis == "stream" else dp_count
    pairs = []
    for source in range(total):
        place = (source // stride) % size
        target = source + ((place + shift) % size - place) * stride
        pairs.append((source, target))
    return pairs


def place_on(level):
    axis, stride, size = level
    return (lax.axis_index(axis) // stride) % size


def pick(stacked, index, dim):
    return lax.dynamic_index_in_dim(stacked, index, dim, keepdims=False)


def scatter_level(stacked, dim, level, dp_count, final_type):
    axis, stride, size = level
    mine = place_on(level)
    total = pick(stacked, mine, dim).astype(jnp.float32)
    for shift in range(1, size):
        sent = pick(stacked, (mine + shift) % size, dim)
        came = lax.ppermute(sent, axis, rotation(level, shift, dp_count))
        total = total + came.astype(jnp.float32)
    return total.astype(final_type)


class Scatter:
    def __init__(self, rows, outer_range, dp_count, parts=2):
        self.levels = inner_levels(dp_count)
        self.inner = self.levels[2:]
        self.outer_range = outer_range
        self.dp_count = dp_count
        self.parts = parts
        sizes = [size for axis, stride, size in reversed(self.inner)]
        self.block = rows.shape[0] // (len(outer_range) * math.prod(sizes) * 4)
        self.state = [
            rows.reshape([len(outer_range)] + sizes + [2, 2, self.block, rows.shape[1]])
        ]
        self.done = 0

    def step(self):
        inner_count = len(self.inner)
        if self.done == 0:
            stacked = scatter_level(
                self.state[0], 1 + inner_count, self.levels[0], self.dp_count, jnp.bfloat16
            )
            if self.parts == 1:
                self.state = [stacked]
            else:
                cut = (self.block // 2 + 15) // 16 * 16
                self.state = [stacked[..., :cut, :], stacked[..., cut:, :]]
            order = [self.levels[1]] + self.inner
            other = [self.inner[0], self.levels[1]] + self.inner[1:]
            self.orders = [order, other]
            self.names = [list(reversed(self.inner)) + [self.levels[1]] for part in range(2)]
        elif self.done <= inner_count + 1:
            for part in range(self.parts):
                level = self.orders[part][self.done - 1]
                dim = 1 + self.names[part].index(level)
                self.names[part].remove(level)
                self.state[part] = scatter_level(
                    self.state[part], dim, level, self.dp_count, jnp.bfloat16
                )
        else:
            self.state = [self.outer_step(piece) for piece in self.state]
        self.done += 1

    def outer_step(self, piece):
        level = ("dp", self.dp_count // 4, 4)
        mine = place_on(level)
        first, count = self.outer_range[0], len(self.outer_range)
        total = pick(piece, jnp.clip(mine - first, 0, count - 1), 0).astype(jnp.float32)
        for shift in range(1, 4):
            pairs = [
                pair
                for pair in rotation(level, shift, self.dp_count)
                if pair[1] // level[1] in self.outer_range
            ]
            target = jnp.clip((mine + shift) % 4 - first, 0, count - 1)
            total = total + lax.ppermute(pick(piece, target, 0), "dp", pairs).astype(jnp.float32)
        return total

    def finish(self):
        while self.done < len(self.inner) + 3:
            self.step()
        return jnp.concatenate(self.state)


def after(value, *scatters):
    states = [array for scatter in scatters for array in scatter.state]
    return lax.optimization_barrier((value, *states))[0]


def sum_shares(rows):
    part = lax.psum_scatter(rows, "dp", scatter_dimension=0, tiled=True)
    return lax.psum_scatter(part, "stream", scatter_dimension=0, tiled=True)


def to_last_quarter(share, devices, skipped):
    owners = devices // 4
    size = share.shape[0]
    block = (devices * size - skipped) // owners
    starts = [skipped + owner * block for owner in range(owners)]
    blocks = []
    for part in range((size - 1 + block + size - 1) // size):
        pairs = [
            (start // size + part, 3 * owners + owner)
            for owner, start in enumerate(starts)
            if start // size + part < devices
        ]
        blocks.append(lax.ppermute(share, ("dp", "stream"), pairs))
    mine = lax.axis_index("dp") * 2 + lax.axis_index("stream") - 3 * owners
    offset = jnp.mod(skipped + jnp.maximum(mine, 0) * block, size)
    return lax.dynamic_slice_in_dim(jnp.concatenate(blocks, axis=0), offset, block)


def to_all(part, count):
    shared = jnp.broadcast_to(part[None], (count, *part.shape))
    gathered = lax.all_to_all(shared, ("dp", "stream"), 0, 0, tiled=True)
    return gathered.reshape(-1, *part.shape[1:])


def swap_streams(rows):
    return lax.ppermute(rows, "stream", [(0, 1), (1, 0)])


def both_parts(rows, other):
    leading = lax.axis_index("stream") == 0
    return jnp.concatenate(
        [jnp.where(leading, rows, other), jnp.where(leading, other, rows)], axis=0
    )


def pair_sum(rows):
    half = rows.shape[0] // 2
    stream = lax.axis_index("stream")
    sent = lax.dynamic_slice_in_dim(rows, (1 - stream) * half, half).astype(jnp.bfloat16)
    return lax.dynamic_slice_in_dim(rows, stream * half, half) + swap_streams(sent).astype(
        jnp.float32
    )


def adam_step(master, first_moment, second_moment, gradient, step_rate, step_decay):
    first_new = BETA_FIRST * first_moment + (1.0 - BETA_FIRST) * gradient
    second_new = BETA_SECOND * second_moment + (1.0 - BETA_SECOND) * gradient * gradient
    first_hat = first_new / (1.0 - BETA_FIRST**STEP)
    second_hat = second_new / (1.0 - BETA_SECOND**STEP)
    master_new = master - step_rate * (
        first_hat / (jnp.sqrt(second_hat) + ADAM_EPS) + step_decay * master
    )
    return (master_new, first_new, second_new)


def chunk_rows(block):
    tiles = block // 16
    counts = [(tiles + SUM_CHUNKS - 1 - part) // SUM_CHUNKS * 16 for part in range(SUM_CHUNKS)]
    return [(sum(counts[:part]), counts[part]) for part in range(SUM_CHUNKS)]


def add_rows(target_ref, source_ref, start, count):
    @pl.loop(0, count // 16)
    def tile_step(tile):
        rows = pl.ds(pl.multiple_of(start + tile * 16, 16), 16)
        target_ref[rows, :] = (
            target_ref[rows, :].astype(jnp.float32) + source_ref[rows, :].astype(jnp.float32)
        ).astype(jnp.bfloat16)


def sum_kernel(
    grad_ref,
    out_ref,
    held,
    core_in,
    first_in,
    second_in,
    along_in,
    load_sem,
    core_send,
    core_recv,
    first_send,
    first_recv,
    second_send,
    second_recv,
    along_send,
    along_recv,
):
    slabs, block = grad_ref.shape[0], grad_ref.shape[4]
    place, x = lax.axis_index("dp"), lax.axis_index("stream")
    c, y, z = place % 2, (place // 2) % 2, place // 4
    sibling, across, beside = (place + 1 - 2 * c, x), (place, 1 - x), (place + 2 - 4 * y, x)
    above, below = (place + 4, x), (place - 4, x)
    chunks = chunk_rows(block)

    barrier = pltpu.get_barrier_semaphore()
    for neighbour in (sibling, across, beside):
        pl.semaphore_signal(barrier, inc=1, device_id=neighbour, device_id_type=MESH)

    @pl.when(z < 3)
    def greet_above():
        pl.semaphore_signal(barrier, inc=1, device_id=above, device_id_type=MESH)

    @pl.when(z > 0)
    def greet_below():
        pl.semaphore_signal(barrier, inc=1, device_id=below, device_id_type=MESH)

    pl.semaphore_wait(barrier, 4 + z * (3 - z) // 2)

    def remote(source, target, send_sem, recv_sem, device):
        return pltpu.make_async_remote_copy(
            src_ref=source,
            dst_ref=target,
            send_sem=send_sem,
            recv_sem=recv_sem,
            device_id=device,
            device_id_type=MESH,
        )

    def core_copy(s, yy, xx):
        at = s * 4 + yy * 2 + xx
        return remote(
            grad_ref.at[s, yy, 1 - c, xx],
            core_in.at[s, yy, xx],
            core_send.at[at],
            core_recv.at[at],
            sibling,
        )

    def load(s, yy, xx):
        return pltpu.make_async_copy(
            grad_ref.at[s, yy, c, xx], held.at[s, yy, xx], load_sem.at[s * 4 + yy * 2 + xx]
        )

    def first_copy(s, chunk, other):
        rows = pl.ds(*chunks[chunk])
        at = (s * SUM_CHUNKS + chunk) * 2 + other
        source = held.at[s, other, 1 - x, rows] if chunk < SUM_WAVES else held.at[s, 1 - y, other, rows]
        return remote(
            source,
            first_in.at[s, other, rows],
            first_send.at[at],
            first_recv.at[at],
            across if chunk < SUM_WAVES else beside,
        )

    def second_copy(s, chunk):
        rows = pl.ds(*chunks[chunk])
        source = held.at[s, 1 - y, x, rows] if chunk < SUM_WAVES else held.at[s, y, 1 - x, rows]
        return remote(
            source,
            second_in.at[s, rows],
            second_send.at[s * SUM_CHUNKS + chunk],
            second_recv.at[s * SUM_CHUNKS + chunk],
            beside if chunk < SUM_WAVES else across,
        )

    def along_copy(s, chunk, down):
        rows = pl.ds(*chunks[chunk])
        way = 0 if down else 1
        return remote(
            held.at[s, y, x, rows],
            along_in.at[way, s, rows],
            along_send.at[s * SUM_CHUNKS + chunk],
            along_recv.at[way * slabs * SUM_CHUNKS + s * SUM_CHUNKS + chunk],
            below if down else above,
        )

    def core_stage(s, half):
        if half == 0:
            for yy in range(2):
                for xx in range(2):
                    load(s, yy, xx).wait()
                    core_copy(s, yy, xx).wait_recv()
        for chunk in (half, half + SUM_WAVES):
            for yy in range(2):
                for xx in range(2):
                    add_rows(held.at[s, yy, xx], core_in.at[s, yy, xx], *chunks[chunk])
            for other in range(2):
                first_copy(s, chunk, other).start()

    def first_stage(s, half):
        for chunk in (half, half + SUM_WAVES):
            for other in range(2):
                first_copy(s, chunk, other).wait_recv()
                kept = held.at[s, other, x] if chunk < SUM_WAVES else held.at[s, y, other]
                add_rows(kept, first_in.at[s, other], *chunks[chunk])
            second_copy(s, chunk).start()

    def second_stage(s, half):
        for chunk in (half, half + SUM_WAVES):
            second_copy(s, chunk).wait_recv()
            add_rows(held.at[s, y, x], second_in.at[s], *chunks[chunk])
        along_stage(s, half, 0)

    def along_stage(s, half, hop):
        for down in (True, False):
            source = 3 - hop if down else hop
            if (source > s) if down else (source < s):

                @pl.when(z == source)
                def pass_on():
                    for chunk in (half, half + SUM_WAVES):
                        if hop > 0:
                            along_copy(s, chunk, down).wait_recv()
                            add_rows(
                                held.at[s, y, x], along_in.at[0 if down else 1, s], *chunks[chunk]
                            )
                        along_copy(s, chunk, down).start()

    def last_stage(s, half):
        @pl.when(z == s)
        def finish():
            for chunk in (half, half + SUM_WAVES):
                start, count = chunks[chunk]
                if s < 3:
                    along_copy(s, chunk, True).wait_recv()
                if s > 0:
                    along_copy(s, chunk, False).wait_recv()

                @pl.loop(0, count // 16)
                def tile_step(tile):
                    rows = pl.ds(pl.multiple_of(start + tile * 16, 16), 16)
                    total = held[s, y, x, rows, :].astype(jnp.float32)
                    if s < 3:
                        total = total + along_in[0, s, rows, :].astype(jnp.float32)
                    if s > 0:
                        total = total + along_in[1, s, rows, :].astype(jnp.float32)
                    out_ref[rows, :] = total

    for s in range(slabs):
        for yy in range(2):
            for xx in range(2):
                core_copy(s, yy, xx).start()
                load(s, yy, xx).start()
    out_ref[...] = jnp.zeros_like(out_ref)
    waves = [(s, half) for s in range(slabs) for half in range(SUM_WAVES)]
    stages = [
        core_stage,
        first_stage,
        second_stage,
        partial(along_stage, hop=1),
        partial(along_stage, hop=2),
        last_stage,
    ]
    for step in range(len(waves) + len(stages) - 1):
        for late, stage in enumerate(stages):
            if 0 <= step - late < len(waves):
                stage(*waves[step - late])
    for s in range(slabs):
        for yy in range(2):
            for xx in range(2):
                core_copy(s, yy, xx).wait_send()
        for chunk in range(SUM_CHUNKS):
            for other in range(2):
                first_copy(s, chunk, other).wait_send()
            second_copy(s, chunk).wait_send()

            @pl.when(z != s)
            def sent_along():
                along_copy(s, chunk, True).wait_send()


def sum_slabs(rows, slabs):
    block, width = rows.shape[0] // (slabs * 8), rows.shape[1]
    low = jnp.bfloat16
    dma = pltpu.SemaphoreType.DMA
    return pl.pallas_call(
        sum_kernel,
        out_shape=jax.ShapeDtypeStruct((block, width), jnp.float32),
        in_specs=[pl.BlockSpec(memory_space=pl.ANY)],
        out_specs=pl.BlockSpec(memory_space=pltpu.VMEM),
        scratch_shapes=[
            pltpu.VMEM((slabs, 2, 2, block, width), low),
            pltpu.VMEM((slabs, 2, 2, block, width), low),
            pltpu.VMEM((slabs, 2, block, width), low),
            pltpu.VMEM((slabs, block, width), low),
            pltpu.VMEM((2, slabs, block, width), low),
            dma((slabs * 4,)),
            dma((slabs * 4,)),
            dma((slabs * 4,)),
            dma((slabs * SUM_CHUNKS * 2,)),
            dma((slabs * SUM_CHUNKS * 2,)),
            dma((slabs * SUM_CHUNKS,)),
            dma((slabs * SUM_CHUNKS,)),
            dma((slabs * SUM_CHUNKS,)),
            dma((slabs * SUM_CHUNKS * 2,)),
        ],
        compiler_params=pltpu.CompilerParams(
            collective_id=0, has_side_effects=True, vmem_limit_bytes=56 * 2**20
        ),
        cost_estimate=pl.CostEstimate(
            flops=rows.size, bytes_accessed=4 * rows.size, transcendentals=0
        ),
        name="sum_slabs",
    )(rows.reshape(slabs, 2, 2, 2, block, width))


def part_rows(block):
    tiles = block // 16
    one, two = tiles // 4, tiles // 2
    return [(0, one * 16), (one * 16, two * 16), ((one + two) * 16, (tiles - one - two) * 16)]


def digit(code, place):
    power = 1 + 9 * place + 81 * (place * (place - 1) // 2)
    power = power + 729 * (place * (place - 1) * (place - 2) // 6)
    return code // power % 10


def gather_kernel(
    shard_ref,
    bias_ref,
    main_ref,
    out_ref,
    bias_out_ref,
    main_out_ref,
    own_sem,
    send_sem,
    link_recv,
    core_recv,
    swap_send,
    swap_recv,
):
    block = shard_ref.shape[0]
    place, x = lax.axis_index("dp"), lax.axis_index("stream")
    c, y, z = place % 2, (place // 2) % 2, place // 4
    up, down, across, beside, sibling = range(5)
    devices = [(place + 4, x), (place - 4, x), (place, 1 - x), (place + 2 - 4 * y, x)]
    devices.append((place + 1 - 2 * c, x))
    parts = part_rows(block)
    order = [z] + [digit(code, z) for code in (2101, 1322, 33)]

    barrier = pltpu.get_barrier_semaphore()
    for way in (across, beside, sibling):
        pl.semaphore_signal(barrier, inc=1, device_id=devices[way], device_id_type=MESH)

    @pl.when(z < 3)
    def greet_above():
        pl.semaphore_signal(barrier, inc=1, device_id=devices[up], device_id_type=MESH)

    @pl.when(z > 0)
    def greet_below():
        pl.semaphore_signal(barrier, inc=1, device_id=devices[down], device_id_type=MESH)

    own = pltpu.make_async_copy(shard_ref, out_ref.at[z, y, c, x], own_sem.at[0])
    own.start()
    own_bias = pltpu.make_async_copy(bias_ref, bias_out_ref.at[z, y, c, x], own_sem.at[1])
    own_bias.start()
    pl.semaphore_wait(barrier, 4 + z * (3 - z) // 2)
    own.wait()
    own_bias.wait()

    def copy(way, zz, yy, xx, part, core=None):
        cc = c if core is None else core
        if part == 3:
            region = bias_out_ref.at[zz, yy, cc, xx]
        else:
            region = out_ref.at[zz, yy, cc, xx, pl.ds(*parts[part])]
        at = ((zz * 2 + yy) * 2 + xx) * 4 + part
        return pltpu.make_async_remote_copy(
            src_ref=region,
            dst_ref=region,
            send_sem=send_sem.at[way * 64 + at],
            recv_sem=core_recv.at[at] if way == sibling else link_recv.at[at],
            device_id=devices[way],
            device_id_type=MESH,
        )

    def came(zz, yy, xx, part):
        copy(across, zz, yy, xx, part).wait_recv()

    def along(zz, yy, xx, part):
        @pl.when((z < 3) & (zz <= z))
        def send_up():
            copy(up, zz, yy, xx, part).start()

        @pl.when((z > 0) & (zz >= z))
        def send_down():
            copy(down, zz, yy, xx, part).start()

    def early(k):
        zz = order[k]
        for part in range(2):
            if k > 0:
                came(zz, y, x, part)
            along(zz, y, x, part)
            for way in (beside, across) if part == 0 else (across, beside):
                copy(way, zz, y, x, part).start()
            copy(sibling, zz, y, x, part).start()

    def middle(k):
        zz = order[k]
        came(zz, 1 - y, x, 0)
        copy(across, zz, 1 - y, x, 0).start()
        came(zz, y, 1 - x, 1)
        copy(beside, zz, y, 1 - x, 1).start()
        copy(sibling, zz, 1 - y, x, 0).start()
        copy(sibling, zz, y, 1 - x, 1).start()

    def late(k):
        zz = order[k]
        for yy, xx, part in ((y, 1 - x, 0), (1 - y, x, 1), (1 - y, 1 - x, 0), (1 - y, 1 - x, 1)):
            came(zz, yy, xx, part)
            copy(sibling, zz, yy, xx, part).start()

    def last_own(k):
        for part in (2, 3):
            if k == 0:
                copy(across, z, y, x, part).start()
                copy(beside, z, y, x, part).start()
                regions = [(y, x)]
            elif k == 1:
                came(z, y, 1 - x, part)
                copy(beside, z, y, 1 - x, part).start()
                regions = [(y, 1 - x)]
            else:
                regions = [(1 - y, x), (1 - y, 1 - x)]
            for yy, xx in regions:
                if k == 2:
                    came(z, yy, xx, part)
                along(z, yy, xx, part)
                copy(sibling, z, yy, xx, part).start()

    def last(k):
        zz = order[k]
        for yy, xx in ((y, x), (y, 1 - x), (1 - y, x), (1 - y, 1 - x)):
            for part in (2, 3):
                came(zz, yy, xx, part)
                along(zz, yy, xx, part)
                copy(sibling, zz, yy, xx, part).start()

    swap = pltpu.make_async_remote_copy(
        src_ref=main_ref,
        dst_ref=main_out_ref,
        send_sem=swap_send,
        recv_sem=swap_recv,
        device_id=devices[across],
        device_id_type=MESH,
    )

    def swap_main(k):
        swap.start()

    for stage, k in (
        (early, 0),
        (last_own, 0),
        (last_own, 1),
        (swap_main, 0),
        (early, 1),
        (middle, 0),
        (last_own, 2),
        (early, 2),
        (middle, 1),
        (early, 3),
        (last, 1),
        (late, 0),
        (middle, 2),
        (last, 2),
        (late, 1),
        (middle, 3),
        (last, 3),
        (late, 2),
        (late, 3),
    ):
        stage(k)

    swap.wait()
    for zz in range(4):
        for yy in range(2):
            for xx in range(2):
                for part in range(4):
                    copy(sibling, zz, yy, xx, part, 1 - c).wait_recv()
                    copy(sibling, zz, yy, xx, part).wait_send()

    def sent_along(zz, yy, xx, part):
        @pl.when((z < 3) & (zz <= z))
        def sent_up():
            copy(up, zz, yy, xx, part).wait_send()

        @pl.when((z > 0) & (zz >= z))
        def sent_down():
            copy(down, zz, yy, xx, part).wait_send()

    for zz in range(4):
        for part in range(2):
            sent_along(zz, y, x, part)
            copy(beside, zz, y, x, part).wait_send()
            copy(across, zz, y, x, part).wait_send()
        copy(across, zz, 1 - y, x, 0).wait_send()
        copy(beside, zz, y, 1 - x, 1).wait_send()
        for yy in range(2):
            for xx in range(2):
                sent_along(zz, yy, xx, 2)
                sent_along(zz, yy, xx, 3)
    for part in (2, 3):
        copy(across, z, y, x, part).wait_send()
        copy(beside, z, y, x, part).wait_send()
        copy(beside, z, y, 1 - x, part).wait_send()


def gather_shards(shard, bias, main_rows):
    block, width = shard.shape
    tile = (16, LANES)
    bias_tile = jnp.pad(bias, (0, tile[0] * tile[1] - bias.shape[0])).reshape(tile)
    dma = pltpu.SemaphoreType.DMA
    place = pl.BlockSpec(memory_space=pl.ANY)
    gathered, biases, main_other = pl.pallas_call(
        gather_kernel,
        out_shape=[
            jax.ShapeDtypeStruct((4, 2, 2, 2, block, width), shard.dtype),
            jax.ShapeDtypeStruct((4, 2, 2, 2, *tile), bias.dtype),
            jax.ShapeDtypeStruct(main_rows.shape, main_rows.dtype),
        ],
        in_specs=[place] * 3,
        out_specs=[place] * 3,
        scratch_shapes=[dma((2,)), dma((320,)), dma((64,)), dma((64,)), dma, dma],
        compiler_params=pltpu.CompilerParams(
            collective_id=1, has_side_effects=True, vmem_limit_bytes=56 * 2**20
        ),
        cost_estimate=pl.CostEstimate(
            flops=0, bytes_accessed=64 * shard.size, transcendentals=0
        ),
        name="gather_shards",
    )(shard, bias_tile, main_rows)
    biases = biases.reshape(32, tile[0] * tile[1])[:, : bias.shape[0]].reshape(-1)
    return gathered.reshape(32 * block, width), biases, main_other


def pre_kernel(grad_ref, weight_ref, slope_ref, pre_ref, sum_ref):
    for at in range(0, weight_ref.shape[0], FFN_PART):
        part = slice(at, at + FFN_PART)
        pre = (
            dot_rows(grad_ref[...], weight_ref[part, :]) * slope_ref[:, part].astype(jnp.float32)
        ).astype(jnp.bfloat16)
        pre_ref[:, part] = pre
        sum_ref[:, part] = jnp.sum(pre.astype(jnp.float32), axis=0, keepdims=True)


def pre_and_sum(grad, weight, slope):
    count, depth = grad.shape
    width = weight.shape[0]
    columns = pl.BlockSpec((count, FFN_TILE), lambda tile: (0, tile))
    vector = pl.BlockSpec((1, FFN_TILE), lambda tile: (0, tile))
    pre, total = pl.pallas_call(
        pre_kernel,
        grid=(width // FFN_TILE,),
        in_specs=[
            pl.BlockSpec((count, depth), lambda tile: (0, 0)),
            pl.BlockSpec((FFN_TILE, depth), lambda tile: (tile, 0)),
            columns,
        ],
        out_specs=[columns, vector],
        out_shape=[
            jax.ShapeDtypeStruct((count, width), jnp.bfloat16),
            jax.ShapeDtypeStruct((1, width), jnp.float32),
        ],
        compiler_params=pltpu.CompilerParams(vmem_limit_bytes=56 * 2**20),
        cost_estimate=pl.CostEstimate(
            flops=2 * count * depth * width,
            bytes_accessed=2 * (count * depth + depth * width + 2 * count * width),
            transcendentals=0,
        ),
        name="pre_and_sum",
    )(grad, weight, slope)
    return pre, total[0]


def local(
    dp_count,
    main_rows,
    pred_rows,
    enc_rows,
    doc_lengths,
    main_cotangent,
    pred_cotangent,
    proj_master,
    proj_first,
    proj_second,
    bias_master,
    bias_first,
    bias_second,
    down_master,
    down_first,
    down_second,
    small_master,
    small_first,
    small_second,
):
    devices = 2 * dp_count
    rel_width = BUCKETS * HEADS
    cross_start = 4 * D + rel_width
    half_rows = main_rows.shape[0]
    group_rows = pred_rows.shape[0]

    bias_low = bias_master.astype(jnp.bfloat16)
    proj_low = proj_master.astype(jnp.bfloat16).T
    if dp_count == 16:
        proj_rows, bias_low, main_other = gather_shards(proj_low, bias_low, main_rows)
    else:
        proj_rows = lax.all_gather(proj_low, ("dp", "stream"), axis=0, tiled=True)
        bias_low = to_all(bias_low, devices)
        main_other = swap_streams(main_rows)
    down_low = lax.optimization_barrier((down_master.astype(jnp.bfloat16), proj_rows))[0]
    down_weight = lax.all_gather(down_low, ("dp", "stream"), axis=0, tiled=True)
    bias_wide = bias_low.astype(jnp.float32)
    query_weight = proj_rows[0:D]
    keys_weight = proj_rows[D : 3 * D]
    out_weight = proj_rows[3 * D : 4 * D]
    table_weight = (
        proj_rows[4 * D : cross_start]
        .reshape(BUCKETS, HEADS, D)
        .transpose(1, 0, 2)
        .reshape(rel_width, D)
    )
    cross_weight = proj_rows[cross_start : cross_start + D]
    pair_weight = proj_rows[cross_start + D : cross_start + 3 * D]
    back_weight = proj_rows[cross_start + 3 * D : cross_start + 4 * D]
    up_weight = proj_rows[cross_start + 4 * D :]
    query_bias = bias_wide[0:D]
    value_bias = bias_wide[D : 2 * D]
    out_bias = bias_wide[2 * D : 3 * D]
    table_bias = bias_wide[3 * D : 3 * D + rel_width].reshape(BUCKETS, HEADS).T.reshape(rel_width)
    cross_bias = bias_wide[3 * D + rel_width : 4 * D + rel_width]
    pair_bias = bias_wide[4 * D + rel_width : 5 * D + rel_width]
    back_bias = bias_wide[5 * D + rel_width : 6 * D + rel_width]
    up_bias = bias_wide[6 * D + rel_width :]
    zero_bias = jnp.zeros((D,), jnp.float32)

    main_start = lax.axis_index("stream") * half_rows
    places = jnp.arange(group_rows, dtype=jnp.int32)
    group_docs = doc_ids(doc_lengths[0], group_rows)
    query_docs = jnp.concatenate(
        [lax.dynamic_slice_in_dim(group_docs, main_start, half_rows), group_docs]
    )
    query_places = jnp.concatenate([main_start + jnp.arange(half_rows, dtype=jnp.int32), places])
    main_flag = jnp.arange(half_rows + group_rows, dtype=jnp.int32) < half_rows
    same_doc = query_docs[:, None] == group_docs[None, :]
    distance = query_places[:, None] - places[None, :]
    allowed = same_doc & ((distance > 0) | (distance == 0) & main_flag[:, None])
    self_mask = jnp.where(allowed, 0.0, MASKED)
    cross_mask = jnp.where(same_doc, 0.0, MASKED)
    lane = jnp.arange(LANES, dtype=jnp.int32)
    turn = jnp.mod(query_places[:, None] - lane[None, :], LANES)
    spread = bucket_of(turn)
    edge = jnp.broadcast_to(query_places[:, None] - LANES, turn.shape)

    main_all = both_parts(main_rows, main_other)
    inputs = jnp.concatenate([main_rows, pred_rows], axis=0)
    key_inputs = jnp.concatenate([main_all, pred_rows], axis=0)
    input_values = inputs.astype(jnp.float32)
    query_low = (times_transpose(inputs, query_weight) + query_bias).astype(jnp.bfloat16)
    self_pairs = (
        times_transpose(key_inputs, keys_weight) + jnp.concatenate([zero_bias, value_bias])
    ).astype(jnp.bfloat16)
    table = times_transpose(inputs, table_weight) + table_bias
    context_low, self_log = self_forward(query_low, self_pairs, table, spread, edge, self_mask)
    enc_other = swap_streams(enc_rows) + jnp.bfloat16(0.0) * context_low[0:1, 0:1]
    enc_all = both_parts(enc_rows, enc_other)
    cross_pairs = (
        times_transpose(enc_all, pair_weight) + jnp.concatenate([zero_bias, pair_bias])
    ).astype(jnp.bfloat16)
    norm_one_in = input_values + times_transpose(context_low, out_weight) + out_bias
    stats_one = norm_stats(norm_one_in)
    hidden_one = (norm_one_in - stats_one[0]) * stats_one[1] * small_master[1] + small_master[4]
    one_low = hidden_one.astype(jnp.bfloat16)

    cross_query = (times_transpose(one_low, cross_weight) + cross_bias).astype(jnp.bfloat16)
    cross_low, cross_log = cross_forward(cross_query, cross_pairs, cross_mask)
    norm_two_in = hidden_one + times_transpose(cross_low, back_weight) + back_bias
    stats_two = norm_stats(norm_two_in)
    hidden_two = (norm_two_in - stats_two[0]) * stats_two[1] * small_master[2] + small_master[5]
    two_low = hidden_two.astype(jnp.bfloat16)

    active, slope = gelu_and_slope(times_transpose(two_low, up_weight) + up_bias)
    active_low = active.astype(jnp.bfloat16)
    slope_low = slope.astype(jnp.bfloat16)
    norm_three_in = hidden_two + matmul(active_low, down_weight) + small_master[0]
    stats_three = norm_stats(norm_three_in)
    final_rows = (
        (norm_three_in - stats_three[0]) * stats_three[1] * small_master[3] + small_master[6]
    ).astype(jnp.bfloat16)

    cotangent = jnp.concatenate([main_cotangent, pred_cotangent], axis=0).astype(jnp.float32)
    sum_three, gain_three, shift_three = norm_back(
        norm_three_in, stats_three, small_master[3], cotangent
    )
    ffn_grad = sum_three.astype(jnp.bfloat16)
    slab = proj_rows.shape[0] // 4
    down_part = sum_shares(column_sums(active_low, ffn_grad))
    pre_grad, pre_sum = pre_and_sum(ffn_grad, down_weight, slope_low)
    up_cut = 3 * slab - cross_start - 4 * D
    up_part = sum_shares(column_sums(pre_grad, two_low))
    two_grad = sum_three + matmul(pre_grad, up_weight)

    sum_two, gain_two, shift_two = norm_back(norm_two_in, stats_two, small_master[2], two_grad)
    branch_grad = sum_two.astype(jnp.bfloat16)
    cross_low_grad = matmul(branch_grad, back_weight).astype(jnp.bfloat16)
    cquery_grad, ckey_grad, cvalue_grad = cross_backward(
        cross_query, cross_pairs, cross_mask, cross_log, cross_low_grad
    )
    enc_grad = pair_sum(matmul(ckey_grad, pair_weight[:D]) + matmul(cvalue_grad, pair_weight[D:]))
    one_grad = sum_two + matmul(cquery_grad, cross_weight)

    sum_one, gain_one, shift_one = norm_back(norm_one_in, stats_one, small_master[1], one_grad)
    attn_grad = sum_one.astype(jnp.bfloat16)
    context_grad = matmul(attn_grad, out_weight).astype(jnp.bfloat16)
    query_grad, key_grad, value_grad, table_wide = self_backward(
        query_low, self_pairs, table, spread, edge, turn, self_mask, self_log, context_grad
    )
    table_wide = lax.optimization_barrier((table_wide, down_part))[0]
    table_grad = table_wide.astype(jnp.bfloat16)
    table_rows = (
        column_sums(table_grad, inputs)
        .reshape(HEADS, BUCKETS, D)
        .transpose(1, 0, 2)
        .reshape(rel_width, D)
    )
    late_rows = jnp.concatenate(
        [
            column_sums(query_grad, inputs),
            column_sums(key_grad, key_inputs),
            column_sums(value_grad, key_inputs),
            column_sums(attn_grad, context_low),
            table_rows,
            column_sums(cquery_grad, one_low),
            column_sums(ckey_grad, enc_all),
            column_sums(cvalue_grad, enc_all),
            column_sums(branch_grad, cross_low),
            column_sums(pre_grad[:, :up_cut], two_low),
        ]
    )
    pair_input_grad = matmul(key_grad, keys_weight[:D]) + matmul(value_grad, keys_weight[D:])
    query_input_grad = (
        sum_one + matmul(query_grad, query_weight) + matmul(table_grad, table_weight)
    )
    main_grad = query_input_grad[:half_rows] + pair_sum(pair_input_grad[:group_rows])
    pred_grad = query_input_grad[half_rows:] + pair_input_grad[group_rows:]

    def row_sum(rows):
        return jnp.sum(rows, axis=0, dtype=jnp.float32)

    bias_parts = jnp.concatenate(
        [
            row_sum(query_grad),
            row_sum(value_grad),
            row_sum(attn_grad),
            row_sum(table_grad).reshape(HEADS, BUCKETS).T.reshape(rel_width),
            row_sum(cquery_grad),
            row_sum(cvalue_grad),
            row_sum(branch_grad),
            pre_sum,
        ]
    )
    small_parts = jnp.concatenate(
        [row_sum(ffn_grad), gain_one, gain_two, gain_three, shift_one, shift_two, shift_three]
    )
    vector_sum = lax.psum(jnp.concatenate([bias_parts, small_parts]), ("dp", "stream"))
    slab_three = to_last_quarter(up_part, devices, up_cut)
    late_rows = lax.optimization_barrier((late_rows, slab_three))[0]
    if dp_count == 16:
        late_sum = sum_slabs(late_rows, 3)
    else:
        late_sum = Scatter(late_rows, range(3), dp_count).finish()
    vector_sum = vector_sum + 0.0 * late_sum[0, 0]
    device = lax.axis_index("dp") * 2 + lax.axis_index("stream")
    bias_len = bias_master.shape[0]
    bias_grad = lax.dynamic_slice_in_dim(vector_sum, device * bias_len, bias_len)
    small_grad = vector_sum[devices * bias_len :].reshape(small_master.shape)
    outer = place_on(("dp", dp_count // 4, 4))
    proj_grad = jnp.where(outer == 3, slab_three.astype(jnp.float32), late_sum).T
    down_grad = down_part.astype(jnp.float32)
    return (
        final_rows[:half_rows],
        final_rows[half_rows:],
        main_grad.astype(jnp.bfloat16),
        pred_grad.astype(jnp.bfloat16),
        enc_grad.astype(jnp.bfloat16),
        *adam_step(proj_master, proj_first, proj_second, proj_grad, RATE_MATRIX, WEIGHT_DECAY),
        *adam_step(bias_master, bias_first, bias_second, bias_grad, RATE_VECTOR, 0.0),
        *adam_step(down_master, down_first, down_second, down_grad, RATE_MATRIX, WEIGHT_DECAY),
        *adam_step(small_master, small_first, small_second, small_grad, RATE_SMALL, 0.0),
    )


def solution(mesh):
    rows = P(("dp", "stream"), None)
    columns = P(None, ("dp", "stream"))
    vector = P(("dp", "stream"))
    masters = (columns,) * 3 + (vector,) * 3 + (rows,) * 3 + (P(),) * 3
    return jax.shard_map(
        partial(local, mesh.shape["dp"]),
        mesh=mesh,
        in_specs=(rows, rows, rows, P("dp", None), rows, rows) + masters,
        out_specs=(rows,) * 5 + masters,
        check_vma=False,
    )
```
